32 devices in a mesh: head: 2 (over x), block: 2 (over y), tok: 8 (over z, core).
Axes of the slice: x: 2, y: 2, z: 4, core: 2. Of those that a mesh axis runs over, the one named last changes fastest.
Arguments:
- tokens: bfloat16 [2, 4096, 2048], P('block', 'tok'), may hold values from -6 to 6
- input_weight: bfloat16 [2048, 3, 2048], P(None, None, 'head'), may hold values from -0.125 to 0.125
- rate_weight: bfloat16 [2048, 4], P(None, 'head'), may hold values from -0.375 to 0.375
- fast_init: bfloat16 [4, 3, 512, 512], P('head'), may hold values from -0.25 to 0.25
- output_weight: bfloat16 [2048, 2048], P('head'), may hold values from -0.125 to 0.125
Outputs:
- mixed: bfloat16 [2, 4096, 2048], P('block', 'tok', 'head')
The draws below stay inside these ranges and needn't reach their ends.
All inputs are finite; a program needn't handle non-finite values.
Results may differ from the reference program's by a relative error of at most 0.005.
Values sent between devices are 32-bit elements; how exact they have to be, the bound alone decides.
No kernel may reach another device: no remote copies, remote signals or barrier semaphores. Data moves between devices by JAX's collectives and lax.ppermute only.
A program may use at most 128 MiB of HBM per device.

```python
import jax
import jax.numpy as jnp
from jax import lax

D = 2048
HEADS = 4
DH = 512
FH = 512
BLOCK_LEN = 4096
BLOCKS = 2


def block_scale(key, extent, shards, smallest, largest):
    factor_of, own = 1.0, jax.random.fold_in(key, 6)
    for dim, parts in shards:
        heights = jnp.exp(jax.random.uniform(jax.random.fold_in(own, dim), (parts,), jnp.float32, smallest / len(shards), largest / len(shards)))
        factor_of = factor_of * jnp.repeat(heights, extent[dim] // parts).reshape([-1 if axis == dim else 1 for axis in range(len(extent))])
    return factor_of


def gaussian(key, extent, scale, reach, pieces=(), dtype=jnp.bfloat16):
    gain = block_scale(key, extent, pieces, -0.22, 0.18) if pieces else 1.0
    result = jax.random.normal(key, extent, jnp.float32) * scale * gain
    return jnp.minimum(jnp.maximum(result, -reach), reach).astype(dtype)


def setup_inputs(seed: int = 0) -> dict:
    seeds = jax.random.split(jax.random.key(seed), 6)
    return {
        "tokens": gaussian(seeds[0], (BLOCKS, BLOCK_LEN, D), 1.0, 6.0, ((0, 2), (1, 8))),
        "input_weight": gaussian(seeds[1], (D, 3, HEADS * DH), D ** -0.5, 0.125, ((2, 2),)),
        "rate_weight": gaussian(seeds[2], (D, HEADS), (D // 9) ** -0.5, 0.375, ((1, 2),)),
        "fast_init": gaussian(seeds[3], (HEADS, 3, DH, FH), DH ** -0.5, 0.25, ((0, 2),)),
        "output_weight": gaussian(seeds[4], (HEADS * DH, D), (HEADS * DH) ** -0.5, 0.125, ((0, 2),)),
    }


epsilon = 1e-06
step_size = 0.03
highest = lax.Precision.HIGHEST

def matmul(left, right):
    return jnp.dot(left, right, precision=highest, preferred_element_type=jnp.float32)

def normalize(values):
    return values / jnp.sqrt(lax.optimization_barrier(jnp.mean(values * values, axis=-1, keepdims=True)) + epsilon)

def fast_grad(weights, keys, targets):
    gate = matmul(keys, weights[0])
    upper = matmul(keys, weights[1])
    sigma = jax.nn.sigmoid(gate)
    active = gate * sigma
    hidden = active * upper
    grad_down = matmul(targets.T, hidden)
    back = matmul(targets, weights[2])
    grad_upper = matmul(keys.T, back * active)
    grad_gate = matmul(keys.T, back * upper * sigma * (1.0 + gate * (1.0 - sigma)))
    return jnp.stack([grad_gate, grad_upper, grad_down])

def fast_step(weights, base_rms, grads):
    scale = jnp.sqrt(lax.optimization_barrier(jnp.mean(grads * grads, axis=(1, 2), keepdims=True)) + epsilon)
    moved = weights + step_size * grads / scale
    return moved * base_rms / jnp.sqrt(lax.optimization_barrier(jnp.mean(moved * moved, axis=1, keepdims=True)) + epsilon)

def fast_apply(weights, queries):
    gate = matmul(queries, weights[0])
    upper = matmul(queries, weights[1])
    hidden = gate * jax.nn.sigmoid(gate) * upper
    return normalize(matmul(hidden, weights[2].T))

def reference(tokens, input_weight, rate_weight, fast_init, output_weight):
    flattened = tokens.reshape(BLOCKS * BLOCK_LEN, D)
    projected = jnp.dot(flattened, input_weight.reshape(D, 3 * HEADS * DH), preferred_element_type=jnp.float32)
    projected = projected.reshape(BLOCKS, BLOCK_LEN, 3, HEADS, DH)
    rates = jax.nn.softplus(jnp.dot(flattened, rate_weight, preferred_element_type=jnp.float32))
    rates = rates.reshape(BLOCKS, BLOCK_LEN, HEADS)
    queries = normalize(projected[:, :, 0])
    keys = normalize(projected[:, :, 1])
    targets = projected[:, :, 2] * rates[:, :, :, None]
    results = []
    for head in range(HEADS):
        weights = fast_init[head].astype(jnp.float32)
        base_rms = jnp.sqrt(lax.optimization_barrier(jnp.mean(weights * weights, axis=1, keepdims=True)))
        outputs = []
        for block in range(BLOCKS):
            grads = fast_grad(weights, keys[block, :, head], targets[block, :, head])
            weights = fast_step(weights, base_rms, grads)
            outputs.append(fast_apply(weights, queries[block, :, head]))
        results.append(jnp.stack(outputs))
    joined = jnp.stack(results, axis=2).reshape(BLOCKS * BLOCK_LEN, HEADS * DH).astype(jnp.bfloat16)
    mixed = jnp.dot(joined, output_weight, preferred_element_type=jnp.float32).astype(jnp.bfloat16)
    return mixed.reshape(BLOCKS, BLOCK_LEN, D)
```

```python
import functools

import jax
import jax.numpy as jnp
from jax import lax
from jax.experimental import pallas as pl
from jax.experimental.pallas import tpu as pltpu
from jax.sharding import PartitionSpec as P

epsilon = 1e-06
step_size = 0.03
vmem_bytes = 48 * 2**20
rows_by_rows = (((1,), (1,)), ((), ()))
over_rows = (((0,), (0,)), ((), ()))
plain = (((1,), (0,)), ((), ()))


def params():
    return pltpu.CompilerParams(vmem_limit_bytes=vmem_bytes)


def dot(left, right, dims=plain):
    return lax.dot_general(left, right, dims, preferred_element_type=jnp.float32)


def split(values):
    high = values.astype(jnp.bfloat16)
    return high, (values - high.astype(jnp.float32)).astype(jnp.bfloat16)


def dot3(left, right, dims=plain):
    return dot(left[0], right[0], dims) + (dot(left[0], right[1], dims) + dot(left[1], right[0], dims))


def normalize(values):
    return values / jnp.sqrt(jnp.mean(values * values, axis=-1, keepdims=True) + epsilon)


def project_kernel(first, slot, share, place, tokens, weight, rate, out):
    part = first + pl.program_id(0)
    values = dot(tokens[...], weight[...])

    @pl.when(part < 2)
    def _():
        out[...] = normalize(values)

    @pl.when(part == 2)
    def _():
        head = lax.rem(place[0] + slot, share)
        logits = dot(tokens[...], rate[...], rows_by_rows)
        column = lax.broadcasted_iota(jnp.int32, logits.shape, 1)
        logit = jnp.sum(jnp.where(column == head, logits, 0.0), axis=1, keepdims=True)
        rates = jnp.maximum(logit, 0.0) + jnp.log1p(jnp.exp(-jnp.abs(logit)))
        out[...] = values * rates


def project(place, tokens, weight, rate, first, count, slot, share):
    rows, depth = tokens.shape
    width = weight.shape[2] // share
    return pl.pallas_call(
        functools.partial(project_kernel, first, slot, share),
        grid_spec=pltpu.PrefetchScalarGridSpec(
            num_scalar_prefetch=1,
            grid=(count,),
            in_specs=[
                pl.BlockSpec((rows, depth), lambda i, place: (0, 0)),
                pl.BlockSpec(
                    (None, depth, width),
                    lambda i, place: (first + i, 0, lax.rem(place[0] + slot, share)),
                ),
                pl.BlockSpec(rate.shape, lambda i, place: (0, 0)),
            ],
            out_specs=pl.BlockSpec((None, rows, width), lambda i, place: (i, 0, 0)),
        ),
        out_shape=jax.ShapeDtypeStruct((count, rows, width), jnp.float32),
        compiler_params=params(),
        name="project",
    )(place, tokens, weight, rate)


def down_kernel(count, *refs):
    sides, (weights, upper_half, lower_half, active_out, slope_out, target, hidden) = (
        refs[:count],
        refs[count:],
    )
    gate_weight, up_weight = split(weights[0]), split(weights[1])
    at = 0
    for side in sides:
        rows = side.shape[1]
        chunk = min(rows, 256)
        for start in range(0, rows, chunk):
            keys = split(side[0, start : start + chunk, :])
            gate = dot3(keys, gate_weight)
            upper = dot3(keys, up_weight)
            sigma = jax.nn.sigmoid(gate)
            active = gate * sigma
            here = pl.ds(at, chunk)
            active_out[here, :] = active
            slope_out[here, :] = upper * sigma * (1.0 + gate * (1.0 - sigma))
            hidden[0, here, :], hidden[1, here, :] = split(active * upper)
            target[0, here, :], target[1, here, :] = split(side[1, start : start + chunk, :])
            at += chunk
    grads = dot3((target[0], target[1]), (hidden[0], hidden[1]), over_rows)
    half = upper_half.shape[0]
    upper_half[...] = grads[:half]
    lower_half[...] = grads[half:]


def grad_down(sides, weights):
    rows = sum(side.shape[1] for side in sides)
    width, hidden = weights.shape[1:]
    flat = jax.ShapeDtypeStruct((rows, hidden), jnp.float32)
    half = jax.ShapeDtypeStruct((width // 2, hidden), jnp.float32)
    return pl.pallas_call(
        functools.partial(down_kernel, len(sides)),
        out_shape=(half, half, flat, flat),
        scratch_shapes=[
            pltpu.VMEM((2, rows, width), jnp.bfloat16),
            pltpu.VMEM((2, rows, hidden), jnp.bfloat16),
        ],
        compiler_params=params(),
        name="grad_down",
    )(*sides, weights)


def up_kernel(count, *refs):
    sides, (weights, active, upper_half, lower_half, back_out, key, product) = (
        refs[:count],
        refs[count:],
    )
    down_weight = split(weights[2])
    at = 0
    for side in sides:
        rows = side.shape[1]
        chunk = min(rows, 256)
        for start in range(0, rows, chunk):
            here = pl.ds(at, chunk)
            back = dot3(split(side[1, start : start + chunk, :]), down_weight)
            back_out[here, :] = back
            key[0, here, :], key[1, here, :] = split(side[0, start : start + chunk, :])
            product[0, here, :], product[1, here, :] = split(back * active[here, :])
            at += chunk
    grads = dot3((key[0], key[1]), (product[0], product[1]), over_rows)
    half = upper_half.shape[0]
    upper_half[...] = grads[:half]
    lower_half[...] = grads[half:]


def grad_up(sides, weights, active):
    rows = sum(side.shape[1] for side in sides)
    width, hidden = weights.shape[1:]
    half = jax.ShapeDtypeStruct((width // 2, hidden), jnp.float32)
    return pl.pallas_call(
        functools.partial(up_kernel, len(sides)),
        out_shape=(half, half, jax.ShapeDtypeStruct((rows, hidden), jnp.float32)),
        scratch_shapes=[
            pltpu.VMEM((2, rows, width), jnp.bfloat16),
            pltpu.VMEM((2, rows, hidden), jnp.bfloat16),
        ],
        compiler_params=params(),
        name="grad_up",
    )(*sides, weights, active)


def gate_kernel(count, *refs):
    sides, (back, slope, upper_half, lower_half, key, product) = refs[:count], refs[count:]
    at = 0
    for side in sides:
        rows = side.shape[1]
        chunk = min(rows, 256)
        for start in range(0, rows, chunk):
            here = pl.ds(at, chunk)
            key[0, here, :], key[1, here, :] = split(side[0, start : start + chunk, :])
            product[0, here, :], product[1, here, :] = split(back[here, :] * slope[here, :])
            at += chunk
    grads = dot3((key[0], key[1]), (product[0], product[1]), over_rows)
    half = upper_half.shape[0]
    upper_half[...] = grads[:half]
    lower_half[...] = grads[half:]


def grad_gate(sides, back, slope):
    rows, hidden = back.shape
    width = sides[0].shape[2]
    half = jax.ShapeDtypeStruct((width // 2, hidden), jnp.float32)
    return pl.pallas_call(
        functools.partial(gate_kernel, len(sides)),
        out_shape=(half, half),
        scratch_shapes=[
            pltpu.VMEM((2, rows, width), jnp.bfloat16),
            pltpu.VMEM((2, rows, hidden), jnp.bfloat16),
        ],
        compiler_params=params(),
        name="grad_gate",
    )(*sides, back, slope)


def step_kernel(flag, *refs):
    halves, (weights, start, out) = refs[:6], refs[6:]
    swap = flag[0] == 1
    for m in range(3):
        one, two = halves[2 * m][...], halves[2 * m + 1][...]
        grads = jnp.concatenate([jnp.where(swap, two, one), jnp.where(swap, one, two)], axis=0)
        scale = step_size / jnp.sqrt(jnp.sum(grads * grads) / grads.size + epsilon)
        moved = weights[m] + grads * scale
        first = start[m].astype(jnp.float32)
        base = jnp.sqrt(jnp.mean(first * first, axis=0, keepdims=True))
        column = jnp.mean(moved * moved, axis=0, keepdims=True)
        out[m] = moved * (base / jnp.sqrt(column + epsilon))


def step(flag, halves, weights, start):
    return pl.pallas_call(
        step_kernel,
        in_specs=[pl.BlockSpec(memory_space=pltpu.SMEM)]
        + [pl.BlockSpec(memory_space=pltpu.VMEM)] * 8,
        out_shape=jax.ShapeDtypeStruct(weights.shape, jnp.float32),
        compiler_params=params(),
        name="step",
    )(flag, *halves, weights, start)


def apply_kernel(queries, weights, out):
    gate_weight, up_weight, down_weight = (split(weights[m]) for m in range(3))
    rows = queries.shape[0]
    chunk = min(rows, 256)
    for start in range(0, rows, chunk):
        here = pl.ds(start, chunk)
        query = split(queries[here, :])
        gate = dot3(query, gate_weight)
        hidden = split(gate * jax.nn.sigmoid(gate) * dot3(query, up_weight))
        out[here, :] = normalize(dot3(hidden, down_weight, rows_by_rows))


def fast_apply(queries, weights):
    return pl.pallas_call(
        apply_kernel,
        out_shape=jax.ShapeDtypeStruct(queries.shape, jnp.float32),
        compiler_params=params(),
        name="fast_apply",
    )(queries, weights)


def output_kernel(share, place, *refs):
    blocks, (weight, out) = refs[:share], refs[share:]
    width = blocks[0].shape[1]
    total = None
    for slot, block in enumerate(blocks):
        head = lax.rem(place[0] + slot, share)
        part = dot(
            block[...].astype(jnp.bfloat16),
            weight[pl.ds(pl.multiple_of(head * width, width), width), :],
        )
        total = part if total is None else total + part
    out[...] = total


def output(place, blocks, weight, ahead, members):
    share = len(blocks)
    rows, width = blocks[0].shape
    columns = weight.shape[1] // members
    half = columns // 2
    return pl.pallas_call(
        functools.partial(output_kernel, share),
        grid_spec=pltpu.PrefetchScalarGridSpec(
            num_scalar_prefetch=1,
            grid=(2,),
            in_specs=[pl.BlockSpec((rows, width), lambda i, place: (0, 0))] * share
            + [
                pl.BlockSpec(
                    (weight.shape[0], half),
                    lambda i, place: (0, 2 * lax.rem(place[1] + ahead, members) + i),
                )
            ],
            out_specs=pl.BlockSpec((rows, half), lambda i, place: (0, i)),
        ),
        out_shape=jax.ShapeDtypeStruct((rows, columns), jnp.float32),
        compiler_params=params(),
        name="output",
    )(place, *blocks, weight)


def line_sum(values, share):
    length = lax.axis_size("tok") // share
    if length == 1:
        return values
    if length % 2:
        groups = [[chip * share + core for chip in range(length)] for core in range(share)]
        return lax.psum(values, "tok", axis_index_groups=groups)
    chip = lax.axis_index("tok") // share
    last = length - 1

    def hop(block, pairs):
        route = [(a * share + core, b * share + core) for a, b in pairs for core in range(share)]
        return lax.ppermute(block, "tok", route)

    inner = length // 2 - 1
    for h in range(inner):
        values = values + hop(values, [(h, h + 1), (last - h, last - h - 1)])
    values = values + hop(values, [(inner, inner + 1), (inner + 1, inner)])
    for h in reversed(range(inner)):
        arrived = hop(values, [(h + 1, h), (last - h - 1, last - h)])
        values = jnp.where((chip == h) | (chip == last - h), arrived, values)
    return values


def within_chip(block, share, distance):
    devices = range(lax.axis_size("tok"))
    route = [(t, t // share * share + (t + distance) % share) for t in devices]
    return lax.ppermute(block, "tok", route)


def total_halves(first, second, section, helper, last, share):
    if helper is None:
        return line_sum(first, share), line_sum(second, share)
    lent = lax.ppermute(second, "block", [(section, helper)])
    own = line_sum(jnp.where(lax.axis_index("block") == section, first, lent), share)
    route = [(helper, section)] if last else [(section, helper), (helper, section)]
    return own, lax.ppermute(own, "block", route)


def body(tokens, input_weight, rate_weight, fast_init, output_weight):
    block_count, tok_rows, model_width = tokens.shape
    share = fast_init.shape[0]
    members = lax.axis_size("head")
    groups = lax.axis_size("block")
    position = lax.axis_index("block")
    core = lax.axis_index("tok") % share
    place = jnp.stack([core, lax.axis_index("head")]).astype(jnp.int32)
    flattened = tokens.reshape(tok_rows, model_width)
    weight = jnp.transpose(input_weight, (1, 0, 2))
    rate = jnp.transpose(rate_weight)
    start = lax.dynamic_index_in_dim(fast_init, core, 0, keepdims=False)
    weights = start.astype(jnp.float32)

    far = [project(place, flattened, weight, rate, 1, 2, slot, share) for slot in range(1, share)]
    moved = [within_chip(block, share, slot) for slot, block in enumerate(far, 1)]
    sides = [project(place, flattened, weight, rate, 1, 2, 0, share)] + moved
    far = [project(place, flattened, weight, rate, 0, 1, slot, share)[0] for slot in range(1, share)]
    queries = [project(place, flattened, weight, rate, 0, 1, 0, share)[0]]
    queries += [within_chip(block, share, slot) for slot, block in enumerate(far, 1)]

    chosen = weights
    for section in range(groups):
        last = section + 1 == groups
        helper = section + 1 if not last else section - 1 if section else None
        down = grad_down(sides, weights)
        up = grad_up(sides, weights, down[2])
        gate = grad_gate(sides, up[2], down[3])
        totals = {}
        for m, pair in ((2, down), (1, up), (0, gate)):
            totals[m] = total_halves(pair[0], pair[1], section, helper, last, share)
        halves = [half for m in range(3) for half in totals[m]]
        flag = jnp.where(position == (section if helper is None else helper), 1, 0)
        if helper is None:
            flag = jnp.zeros_like(flag)
        weights = step(flag.astype(jnp.int32).reshape(1), halves, weights, start)
        chosen = jnp.where(position == section, weights, chosen)

    far = [fast_apply(block, chosen) for block in queries[1:]]
    back = [within_chip(block, share, -slot) for slot, block in enumerate(far, 1)]
    blocks = [fast_apply(queries[0], chosen)] + back
    mixed = None
    sent = [output(place, blocks, output_weight, ahead, members) for ahead in range(1, members)]
    arrived = [
        lax.ppermute(block, "head", [(i, (i + ahead) % members) for i in range(members)])
        for ahead, block in enumerate(sent, 1)
    ]
    mixed = output(place, blocks, output_weight, 0, members)
    for block in arrived:
        mixed = mixed + block
    return mixed.astype(jnp.bfloat16).reshape(block_count, tok_rows, -1)


def solution(mesh):
    placed = (
        P("block", "tok", None),
        P(None, None, "head"),
        P(None, "head"),
        P("head", None, None, None),
        P("head", None),
    )
    return jax.shard_map(
        body, mesh=mesh, in_specs=placed, out_specs=P("block", "tok", "head"), check_vma=False
    )
```

```python
import functools

import jax
import jax.numpy as jnp
from jax import lax
from jax.experimental import pallas as pl
from jax.experimental.pallas import tpu as pltpu
from jax.sharding import PartitionSpec as P

epsilon = 1e-06
step_size = 0.03
vmem_bytes = 48 * 2**20
rows_by_rows = (((1,), (1,)), ((), ()))
over_rows = (((0,), (0,)), ((), ()))
plain = (((1,), (0,)), ((), ()))


def params():
    return pltpu.CompilerParams(vmem_limit_bytes=vmem_bytes)


def dot(left, right, dims=plain):
    return lax.dot_general(left, right, dims, preferred_element_type=jnp.float32)


def split(values):
    high = values.astype(jnp.bfloat16)
    return high, (values - high.astype(jnp.float32)).astype(jnp.bfloat16)


def dot3(left, right, dims=plain):
    return dot(left[0], right[0], dims) + (dot(left[0], right[1], dims) + dot(left[1], right[0], dims))


def normalize(values):
    return values / jnp.sqrt(jnp.mean(values * values, axis=-1, keepdims=True) + epsilon)


def project_kernel(first, head, tokens, weight, rate, out):
    part = first + pl.program_id(0)
    values = dot(tokens[...], weight[...])

    @pl.when(part < 2)
    def _():
        out[...] = normalize(values)

    @pl.when(part == 2)
    def _():
        logits = dot(tokens[...], rate[...], rows_by_rows)
        logit = logits[:, head : head + 1]
        rates = jnp.maximum(logit, 0.0) + jnp.log1p(jnp.exp(-jnp.abs(logit)))
        out[...] = values * rates


def project(tokens, weight, rate, first, count, head, heads):
    rows, depth = tokens.shape
    width = weight.shape[2] // heads
    return pl.pallas_call(
        functools.partial(project_kernel, first, head),
        grid=(count,),
        in_specs=[
            pl.BlockSpec((rows, depth), lambda i: (0, 0)),
            pl.BlockSpec((None, depth, width), lambda i: (first + i, 0, head)),
            pl.BlockSpec(rate.shape, lambda i: (0, 0)),
        ],
        out_specs=pl.BlockSpec((None, rows, width), lambda i: (i, 0, 0)),
        out_shape=jax.ShapeDtypeStruct((count, rows, width), jnp.float32),
        compiler_params=params(),
        name="project",
    )(tokens, weight, rate)


def stepped(place, halves, sums, weights, start, share):
    swap = place[1] == 1
    results = []
    for m in range(3):
        one, two = halves[2 * m][...], halves[2 * m + 1][...]
        grads = jnp.concatenate([jnp.where(swap, two, one), jnp.where(swap, one, two)], axis=0)
        square = sums[0][m, 0]
        for other in sums[1:]:
            square = square + other[m, 0]
        scale = jnp.full((1, 1), square / (grads.size * share) + epsilon, jnp.float32)
        moved = weights[m] + grads * (step_size / jnp.sqrt(scale))
        first = start[m].astype(jnp.float32)
        base = jnp.sqrt(jnp.mean(first * first, axis=0, keepdims=True))
        column = jnp.mean(moved * moved, axis=0, keepdims=True)
        results.append(moved * (base / jnp.sqrt(column + epsilon)))
    return results


def sums_kernel(*refs):
    halves, out = refs[:-1], refs[-1]
    row = lax.broadcasted_iota(jnp.int32, out.shape, 0)
    total = jnp.zeros(out.shape, jnp.float32)
    for m in range(3):
        square = sum(jnp.sum(half[...] * half[...]) for half in halves[2 * m : 2 * m + 2])
        total = jnp.where(row == m, square, total)
    out[...] = total


def square_sums(halves):
    return pl.pallas_call(
        sums_kernel,
        out_shape=jax.ShapeDtypeStruct((8, 128), jnp.float32),
        compiler_params=params(),
        name="square_sums",
    )(*halves)


def grad_kernel(share, stepping, place, start, *refs):
    refs = list(refs)
    if stepping:
        halves, refs = refs[:6], refs[6:]
        sums, refs = refs[:share], refs[share:]
        old, refs = refs[0], refs[1:]
    sides, refs = refs[:share], refs[share:]
    outs, refs = refs[:6], refs[6:]
    if stepping:
        new, refs = refs[0], refs[1:]
        weights = stepped(place, halves, sums, old, start, share)
        for m in range(3):
            new[m] = weights[m]
    else:
        weights = [start[m].astype(jnp.float32) for m in range(3)]
    key, target, hidden, upward, gateward = refs
    gate_weight, up_weight, down_weight = (split(block) for block in weights)
    at = 0
    for side in sides:
        rows = side.shape[1]
        chunk = min(rows, 256)
        for begin in range(0, rows, chunk):
            here = pl.ds(at, chunk)
            keys = split(side[0, begin : begin + chunk, :])
            targets = split(side[1, begin : begin + chunk, :])
            key[0, here, :], key[1, here, :] = keys
            target[0, here, :], target[1, here, :] = targets
            gate = dot3(keys, gate_weight)
            upper = dot3(keys, up_weight)
            back = dot3(targets, down_weight)
            sigma = jax.nn.sigmoid(gate)
            active = gate * sigma
            hidden[0, here, :], hidden[1, here, :] = split(active * upper)
            upward[0, here, :], upward[1, here, :] = split(back * active)
            slope = upper * sigma * (1.0 + gate * (1.0 - sigma))
            gateward[0, here, :], gateward[1, here, :] = split(back * slope)
            at += chunk
    for m, left, right in ((2, target, hidden), (1, key, upward), (0, key, gateward)):
        grads = dot3((left[0], left[1]), (right[0], right[1]), over_rows)
        half = outs[2 * m].shape[0]
        outs[2 * m][...] = grads[:half]
        outs[2 * m + 1][...] = grads[half:]


def start_spec(start, head, share):
    _, parts, width, hidden = start.shape
    return pl.BlockSpec(
        (None, parts, width, hidden // share), lambda i, place: (head, 0, 0, place[0])
    )


def whole():
    return pl.BlockSpec(memory_space=pltpu.VMEM)


def fast_grad(place, start, head, sides, share, step=None):
    rows = sum(side.shape[1] for side in sides)
    _, parts, width, hidden = start.shape
    hidden = hidden // share
    half = jax.ShapeDtypeStruct((width // 2, hidden), jnp.float32)
    out_shape = [half] * 6
    operands = list(sides)
    if step is not None:
        halves, sums, weights = step
        operands = list(halves) + list(sums) + [weights] + operands
        out_shape.append(jax.ShapeDtypeStruct((parts, width, hidden), jnp.float32))
    by_width = pltpu.VMEM((2, rows, width), jnp.bfloat16)
    by_hidden = pltpu.VMEM((2, rows, hidden), jnp.bfloat16)
    return pl.pallas_call(
        functools.partial(grad_kernel, share, step is not None),
        grid_spec=pltpu.PrefetchScalarGridSpec(
            num_scalar_prefetch=1,
            grid=(1,),
            in_specs=[start_spec(start, head, share)] + [whole() for _ in operands],
            out_specs=[whole() for _ in out_shape],
            scratch_shapes=[by_width, by_width, by_hidden, by_hidden, by_hidden],
        ),
        out_shape=out_shape,
        compiler_params=params(),
        name="fast_grad",
    )(place, start, *operands)


def apply_kernel(share, place, start, *refs):
    halves, refs = refs[:6], refs[6:]
    sums, refs = refs[:share], refs[share:]
    old, kept, refs = refs[0], refs[1], refs[2:]
    queries, outs = refs[:share], refs[share:]
    keep = place[2] == 1
    weights = stepped(place, halves, sums, old, start, share)
    weights = [jnp.where(keep, kept[m], weights[m]) for m in range(3)]
    gate_weight, up_weight, down_weight = (split(block) for block in weights)
    for query, out in zip(queries, outs):
        rows = query.shape[0]
        chunk = min(rows, 256)
        for begin in range(0, rows, chunk):
            here = pl.ds(begin, chunk)
            values = split(query[here, :])
            gate = dot3(values, gate_weight)
            hidden = split(gate * jax.nn.sigmoid(gate) * dot3(values, up_weight))
            out[here, :] = dot3(hidden, down_weight, rows_by_rows)


def fast_apply(place, start, head, queries, share, halves, sums, weights, kept):
    operands = list(halves) + list(sums) + [weights, kept] + list(queries)
    rows, width = queries[0].shape
    return pl.pallas_call(
        functools.partial(apply_kernel, share),
        grid_spec=pltpu.PrefetchScalarGridSpec(
            num_scalar_prefetch=1,
            grid=(1,),
            in_specs=[start_spec(start, head, share)] + [whole() for _ in operands],
            out_specs=[whole() for _ in queries],
        ),
        out_shape=[jax.ShapeDtypeStruct((rows, width), jnp.float32) for _ in queries],
        compiler_params=params(),
        name="fast_apply",
    )(place, start, *operands)


def finish_kernel(*refs):
    total = refs[0][...]
    for part in refs[1:-1]:
        total = total + part[...]
    refs[-1][...] = normalize(total)


def finish(parts):
    return pl.pallas_call(
        finish_kernel,
        out_shape=jax.ShapeDtypeStruct(parts[0].shape, jnp.float32),
        compiler_params=params(),
        name="finish",
    )(*parts)


def output_kernel(count, sofar, place, *refs):
    blocks, weights, refs = refs[:count], refs[count : 2 * count], refs[2 * count :]
    total = refs[0][...] if sofar else None
    for block, weight in zip(blocks, weights):
        part = dot(block[...].astype(jnp.bfloat16), weight[...].astype(jnp.bfloat16))
        total = part if total is None else total + part
    refs[-1][...] = total.astype(refs[-1].dtype)


def output(place, pairs, columns, dtype, sofar=None):
    count = len(pairs)
    rows, width = pairs[0][0].shape
    half = columns // 2

    def weight_spec(at, every):
        if every:
            return pl.BlockSpec((width, half), lambda i, place: (at, 2 * place[3] + i))
        return pl.BlockSpec((width, half), lambda i, place: (at, i))

    by_half = pl.BlockSpec((rows, half), lambda i, place: (0, i))
    operands = [pair[0] for pair in pairs] + [pair[1] for pair in pairs]
    in_specs = [pl.BlockSpec((rows, width), lambda i, place: (0, 0))] * count
    in_specs += [weight_spec(at, every) for _, _, at, every in pairs]
    if sofar is not None:
        operands.append(sofar)
        in_specs.append(by_half)
    return pl.pallas_call(
        functools.partial(output_kernel, count, sofar is not None),
        grid_spec=pltpu.PrefetchScalarGridSpec(
            num_scalar_prefetch=1, grid=(2,), in_specs=in_specs, out_specs=by_half
        ),
        out_shape=jax.ShapeDtypeStruct((rows, columns), dtype),
        compiler_params=params(),
        name="output",
    )(place, *operands)


def line_sum(values, share):
    length = lax.axis_size("tok") // share
    if length == 1:
        return values
    if length % 2:
        groups = [[chip * share + core for chip in range(length)] for core in range(share)]
        return lax.psum(values, "tok", axis_index_groups=groups)
    chip = lax.axis_index("tok") // share
    last = length - 1

    def hop(block, pairs):
        route = [(a * share + core, b * share + core) for a, b in pairs for core in range(share)]
        return lax.ppermute(block, "tok", route)

    inner = length // 2 - 1
    for h in range(inner):
        values = values + hop(values, [(h, h + 1), (last - h, last - h - 1)])
    middle = [(inner, inner + 1), (inner + 1, inner)]
    stay = [(c, c) for c in range(length) if c not in (inner, inner + 1)]
    arrived = hop(values, middle + stay)
    values = values + jnp.where((chip == inner) | (chip == inner + 1), arrived, 0.0)
    for h in reversed(range(inner)):
        arrived = hop(values, [(h + 1, h), (last - h - 1, last - h)])
        values = jnp.where((chip == h) | (chip == last - h), arrived, values)
    return values


def within_chip(block, share, distance):
    devices = range(lax.axis_size("tok"))
    route = [(t, t // share * share + (t + distance) % share) for t in devices]
    return lax.ppermute(block, "tok", route)


def total_halves(first, second, section, helper, last, share):
    if helper is None:
        return line_sum(first, share), line_sum(second, share)
    route = [(section, helper)] if last else [(section, helper), (helper, section)]
    lent = lax.ppermute(second, "block", route)
    own = line_sum(jnp.where(lax.axis_index("block") == section, first, lent), share)
    route = [(helper, section)] if last else [(section, helper), (helper, section)]
    return own, lax.ppermute(own, "block", route)


def body(tokens, input_weight, rate_weight, fast_init, output_weight):
    block_count, tok_rows, model_width = tokens.shape
    heads, _, head_dim, _ = fast_init.shape
    share = heads
    members = lax.axis_size("head")
    groups = lax.axis_size("block")
    position = lax.axis_index("block")
    member = lax.axis_index("head")
    core = lax.axis_index("tok") % share
    flattened = tokens.reshape(tok_rows, model_width)
    weight = jnp.transpose(input_weight, (1, 0, 2))
    rate = jnp.transpose(rate_weight)
    columns = output_weight.shape[1] // members

    def exchanged(block):
        return [block] + [within_chip(block, share, distance) for distance in range(1, share)]

    def place(section, helper, keep):
        swapped = position == helper if helper is not None else position < 0
        return jnp.stack([core, swapped, keep, member]).astype(jnp.int32)

    sides = [
        exchanged(project(flattened, weight, rate, 1, 2, head, heads)) for head in range(heads)
    ]
    far_weights = [
        lax.ppermute(
            lax.dynamic_slice_in_dim(
                output_weight, (member + ahead) % members * columns, columns, 1
            ).astype(jnp.float32),
            "head",
            [(i, (i + ahead) % members) for i in range(members)],
        )
        for ahead in range(1, members)
    ]
    queries = [
        exchanged(project(flattened, weight, rate, 0, 1, head, heads)[0]) for head in range(heads)
    ]

    weights = [None] * heads
    kept = [None] * heads
    steps = [None] * heads
    here = place(0, None, position < 0)
    for section in range(groups):
        last = section + 1 == groups
        helper = section + 1 if not last else section - 1 if section else None
        for head in range(heads):
            if section == 0:
                grads = fast_grad(here, fast_init, head, sides[head], share)
                hidden = fast_init.shape[3] // share
                begin = lax.dynamic_slice_in_dim(fast_init[head], core * hidden, hidden, 2)
                weights[head] = begin.astype(jnp.float32)
                kept[head] = weights[head]
            else:
                *grads, weights[head] = fast_grad(
                    here, fast_init, head, sides[head], share, steps[head]
                )
                kept[head] = (
                    weights[head]
                    if section == 1
                    else jnp.where(position == section - 1, weights[head], kept[head])
                )
            halves = [None] * 6
            for m in (2, 1, 0):
                halves[2 * m], halves[2 * m + 1] = total_halves(
                    grads[2 * m], grads[2 * m + 1], section, helper, last, share
                )
            steps[head] = halves, exchanged(square_sums(halves)), weights[head]
        here = place(section, helper, position != groups - 1 if last else position < 0)
        if section == 0:
            sides, queries = lax.optimization_barrier((sides, queries))

    near, distant = [], [[] for _ in range(1, members)]
    for head in range(heads):
        parts = fast_apply(here, fast_init, head, queries[head], share, *steps[head], kept[head])
        arrived = [
            within_chip(block, share, -distance) for distance, block in enumerate(parts[1:], 1)
        ]
        near.append(finish([parts[0]] + arrived))
        for ahead in range(1, members):
            distant[ahead - 1].append(
                lax.ppermute(near[head], "head", [(i, (i + ahead) % members) for i in range(members)])
            )
    pairs = [(near[head], output_weight, head, True) for head in range(heads)]
    others = [
        (distant[ahead][head], far_weights[ahead], head, False)
        for head in range(heads)
        for ahead in range(members - 1)
    ]
    if not others:
        mixed = output(here, pairs, columns, jnp.bfloat16)
    else:
        final = others[-1:]
        mixed = output(here, pairs + others[:-1], columns, jnp.float32)
        mixed = output(here, final, columns, jnp.bfloat16, mixed)
    return mixed.reshape(block_count, tok_rows, -1)


def solution(mesh):
    placed = (
        P("block", "tok", None),
        P(None, None, "head"),
        P(None, "head"),
        P("head", None, None, None),
        P("head", None),
    )
    return jax.shard_map(
        body, mesh=mesh, in_specs=placed, out_specs=P("block", "tok", "head"), check_vma=False
    )
```

```python
import functools

import jax
import jax.numpy as jnp
from jax import lax
from jax.experimental import pallas as pl
from jax.experimental.pallas import tpu as pltpu
from jax.sharding import PartitionSpec as P

epsilon = 1e-06
step_size = 0.03
vmem_bytes = 30 * 2**20
rows_by_rows = (((1,), (1,)), ((), ()))
over_rows = (((0,), (0,)), ((), ()))
plain = (((1,), (0,)), ((), ()))


def params():
    return pltpu.CompilerParams(vmem_limit_bytes=vmem_bytes)


def dot(left, right, dims=plain):
    return lax.dot_general(left, right, dims, preferred_element_type=jnp.float32)


def split(values):
    high = values.astype(jnp.bfloat16)
    return high, (values - high.astype(jnp.float32)).astype(jnp.bfloat16)


def dot3(left, right, dims=plain):
    return dot(left[0], right[0], dims) + (dot(left[0], right[1], dims) + dot(left[1], right[0], dims))


def normalize(values):
    return values / jnp.sqrt(jnp.mean(values * values, axis=-1, keepdims=True) + epsilon)


token_shape = jax.ShapeDtypeStruct((8, 128), jnp.float32)
unread = pl.BlockSpec(memory_space=pl.ANY)


def whole():
    return pl.BlockSpec(memory_space=pltpu.VMEM)


def ordered(kernel, grid, in_specs, out_specs, out_shape, scratch, name):
    def traced(place, token, *refs):
        outs = len(out_shape)
        inputs = len(in_specs)
        refs[inputs + outs][...] = jnp.zeros(token_shape.shape, jnp.float32)
        kernel(place, *refs[: inputs + outs], *refs[inputs + outs + 1 :])

    return pl.pallas_call(
        traced,
        grid_spec=pltpu.PrefetchScalarGridSpec(
            num_scalar_prefetch=1,
            grid=grid,
            in_specs=[unread] + in_specs,
            out_specs=list(out_specs)
            + [pl.BlockSpec(token_shape.shape, lambda i, place: (0, 0))],
            scratch_shapes=scratch,
        ),
        out_shape=list(out_shape) + [token_shape],
        compiler_params=params(),
        name=name,
    )


def project_kernel(first, head, place, tokens, weight, rate, out):
    part = first + pl.program_id(0)
    values = dot(tokens[...], weight[...])

    @pl.when(part < 2)
    def _():
        out[...] = normalize(values)

    @pl.when(part == 2)
    def _():
        logits = dot(tokens[...], rate[...], rows_by_rows)
        logit = logits[:, head : head + 1]
        rates = jnp.maximum(logit, 0.0) + jnp.log1p(jnp.exp(-jnp.abs(logit)))
        out[...] = values * rates


def project(place, token, tokens, weight, rate, first, count, head, heads):
    rows, depth = tokens.shape
    width = weight.shape[2] // heads
    return ordered(
        functools.partial(project_kernel, first, head),
        (count,),
        [
            pl.BlockSpec((rows, depth), lambda i, place: (0, 0)),
            pl.BlockSpec((None, depth, width), lambda i, place: (first + i, 0, head)),
            pl.BlockSpec(rate.shape, lambda i, place: (0, 0)),
        ],
        [pl.BlockSpec((None, rows, width), lambda i, place: (i, 0, 0))],
        [jax.ShapeDtypeStruct((count, rows, width), jnp.float32)],
        [],
        "project",
    )(place, token, tokens, weight, rate)


def widen_kernel(place, weight, out):
    out[...] = weight[...].astype(jnp.float32)


def widen(place, token, weight, ahead, members):
    rows, columns = weight.shape
    columns = columns // members
    step = rows // 4
    return ordered(
        widen_kernel,
        (4,),
        [
            pl.BlockSpec(
                (step, columns), lambda i, place: (i, lax.rem(place[3] + ahead, members))
            )
        ],
        [pl.BlockSpec((step, columns), lambda i, place: (i, 0))],
        [jax.ShapeDtypeStruct((rows, columns), jnp.float32)],
        [],
        "widen",
    )(place, token, weight)


def cut(grads, outs, m, place, role):
    size = outs[0].shape[1]
    odd = lax.rem(place[4], 2)
    for out, piece in zip(
        outs,
        (2 * role + odd, 2 * role + 1 - odd, 2 * (1 - role) + odd, 2 * (1 - role) + 1 - odd),
    ):
        out[m] = grads[pl.ds(pl.multiple_of(piece * size, size), size), :]


def joined(pieces, m, place, role, full):
    size = pieces[0].shape[1]
    odd = lax.rem(place[4], 2)
    for block, piece in zip(
        pieces,
        (2 * role + odd, 2 * role + 1 - odd, 2 * (1 - role) + odd, 2 * (1 - role) + 1 - odd),
    ):
        full[pl.ds(pl.multiple_of(piece * size, size), size), :] = block[m]
    return full[...]


def stepped(place, pieces, sums, weights, start, share, full):
    results = []
    for m in range(3):
        grads = joined(pieces, m, place, place[1], full)
        square = sums[0][m, 0]
        for other in sums[1:]:
            square = square + other[m, 0]
        scale = jnp.full((1, 1), square / (grads.size * share) + epsilon, jnp.float32)
        moved = weights[m].astype(jnp.float32) + grads * (step_size / jnp.sqrt(scale))
        first = start[m].astype(jnp.float32)
        base = jnp.sqrt(jnp.mean(first * first, axis=0, keepdims=True))
        column = jnp.mean(moved * moved, axis=0, keepdims=True)
        results.append(moved * (base / jnp.sqrt(column + epsilon)))
    return results


def sums_kernel(place, *refs):
    pieces, out = refs[:-1], refs[-1]
    row = lax.broadcasted_iota(jnp.int32, out.shape, 0)
    total = jnp.zeros(out.shape, jnp.float32)
    for m in range(3):
        square = sum(jnp.sum(piece[m] * piece[m]) for piece in pieces)
        total = jnp.where(row == m, square, total)
    out[...] = total


def square_sums(place, token, pieces):
    return ordered(
        sums_kernel, (1,), [whole()] * len(pieces), [whole()], [token_shape], [], "square_sums"
    )(place, token, *pieces)


def grad_kernel(share, count, first, place, start, *refs):
    refs = list(refs)
    stepping = count > 0
    if stepping:
        pieces, refs = refs[:4], refs[4:]
        sums, refs = refs[:share], refs[share:]
        if not first:
            old, refs = refs[0], refs[1:]
    sides, refs = refs[:share], refs[share:]
    outs, refs = refs[:4], refs[4:]
    if stepping:
        new, refs = refs[0], refs[1:]
    full, key, target, hidden, upward, gateward = refs
    if stepping:
        weights = stepped(place, pieces, sums, start if first else old, start, share, full)
        for m in range(3):
            new[m] = weights[m]
    else:
        weights = [start[m].astype(jnp.float32) for m in range(3)]
    gate_weight, up_weight, down_weight = (split(block) for block in weights)
    at = 0
    for side in sides:
        rows = side.shape[1]
        chunk = min(rows, 256)
        for begin in range(0, rows, chunk):
            here = pl.ds(at, chunk)
            keys = split(side[0, begin : begin + chunk, :])
            targets = split(side[1, begin : begin + chunk, :])
            key[0, here, :], key[1, here, :] = keys
            target[0, here, :], target[1, here, :] = targets
            gate = dot3(keys, gate_weight)
            upper = dot3(keys, up_weight)
            back = dot3(targets, down_weight)
            sigma = jax.nn.sigmoid(gate)
            active = gate * sigma
            hidden[0, here, :], hidden[1, here, :] = split(active * upper)
            upward[0, here, :], upward[1, here, :] = split(back * active)
            slope = upper * sigma * (1.0 + gate * (1.0 - sigma))
            gateward[0, here, :], gateward[1, here, :] = split(back * slope)
            at += chunk
    for m, left, right in ((2, target, hidden), (1, key, upward), (0, key, gateward)):
        full[...] = dot3((left[0], left[1]), (right[0], right[1]), over_rows)
        cut(full, outs, m, place, 0)


def start_spec(start, head, share):
    _, parts, width, hidden = start.shape
    return pl.BlockSpec(
        (None, parts, width, hidden // share), lambda i, place: (head, 0, 0, place[0])
    )


def fast_grad(place, token, start, head, sides, share, count, step=None):
    rows = sum(side.shape[1] for side in sides)
    _, parts, width, hidden = start.shape
    hidden = hidden // share
    piece = jax.ShapeDtypeStruct((parts, width // 4, hidden), jnp.float32)
    out_shape = [piece] * 4
    operands = list(sides)
    if step is not None:
        pieces, sums, weights = step
        old = [] if weights is None else [weights]
        operands = list(pieces) + list(sums) + old + operands
        out_shape.append(jax.ShapeDtypeStruct((parts, width, hidden), jnp.float32))
    by_width = pltpu.VMEM((2, rows, width), jnp.bfloat16)
    by_hidden = pltpu.VMEM((2, rows, hidden), jnp.bfloat16)
    return ordered(
        functools.partial(grad_kernel, share, count, step is not None and step[2] is None),
        (1,),
        [start_spec(start, head, share)] + [whole() for _ in operands],
        [whole() for _ in out_shape],
        out_shape,
        [
            pltpu.VMEM((width, hidden), jnp.float32),
            by_width,
            by_width,
            by_hidden,
            by_hidden,
            by_hidden,
        ],
        "fast_grad",
    )(place, token, start, *operands)


def apply_kernel(share, place, start, *refs):
    pieces, refs = refs[:4], refs[4:]
    sums, refs = refs[:share], refs[share:]
    old, kept, refs = refs[0], refs[1], refs[2:]
    queries, outs, full = refs[:share], refs[share : 2 * share], refs[-1]
    keep = place[2] == 1
    weights = stepped(place, pieces, sums, old, start, share, full)
    weights = [jnp.where(keep, kept[m], weights[m]) for m in range(3)]
    gate_weight, up_weight, down_weight = (split(block) for block in weights)
    for query, out in zip(queries, outs):
        rows = query.shape[0]
        chunk = min(rows, 256)
        for begin in range(0, rows, chunk):
            here = pl.ds(begin, chunk)
            values = split(query[here, :])
            gate = dot3(values, gate_weight)
            hidden = split(gate * jax.nn.sigmoid(gate) * dot3(values, up_weight))
            out[here, :] = dot3(hidden, down_weight, rows_by_rows)


def fast_apply(place, token, start, head, queries, share, pieces, sums, weights, kept):
    operands = list(pieces) + list(sums) + [weights, kept] + list(queries)
    rows, width = queries[0].shape
    return ordered(
        functools.partial(apply_kernel, share),
        (1,),
        [start_spec(start, head, share)] + [whole() for _ in operands],
        [whole() for _ in queries],
        [jax.ShapeDtypeStruct((rows, width), jnp.float32) for _ in queries],
        [pltpu.VMEM(weights.shape[1:], jnp.float32)],
        "fast_apply",
    )(place, token, start, *operands)


def finish_kernel(place, *refs):
    total = refs[0][...]
    for part in refs[1:-1]:
        total = total + part[...]
    refs[-1][...] = normalize(total)


def finish(place, token, parts):
    return ordered(
        finish_kernel,
        (1,),
        [whole() for _ in parts],
        [whole()],
        [jax.ShapeDtypeStruct(parts[0].shape, jnp.float32)],
        [],
        "finish",
    )(place, token, *parts)


def halve(total, bit, place, outs):
    if bit is None:
        outs[0][...] = total
        return
    size = outs[0].shape[1]
    mine = lax.rem(lax.div(place[4], bit), 2) == 1
    low, high = total[:, :size], total[:, size:]
    outs[0][...] = jnp.where(mine, low, high)
    outs[1][...] = jnp.where(mine, high, low)


def gather_kernel(bit, place, own, line, across, corner, *outs):
    helping = place[1] == 1
    total = jnp.where(helping, across[...], own[...]) + jnp.where(helping, corner[...], line[...])
    halve(total, bit, place, outs)


def add_kernel(bit, place, own, other, *outs):
    halve(own[...] + other[...], bit, place, outs)


def pair_kernel(bit, place, own, other, out):
    size = own.shape[1]
    mine = lax.rem(lax.div(place[4], bit), 2) == 1
    out[:, :size] = jnp.where(mine, other[...], own[...])
    out[:, size:] = jnp.where(mine, own[...], other[...])


def combine(place, token, kernel, operands, bit):
    parts, size, width = operands[0].shape
    count = 1
    if kernel is pair_kernel:
        size = 2 * size
    elif bit is not None:
        count, size = 2, size // 2
    return ordered(
        functools.partial(kernel, bit),
        (1,),
        [whole() for _ in operands],
        [whole()] * count,
        [jax.ShapeDtypeStruct((parts, size, width), jnp.float32)] * count,
        [],
        "combine",
    )(place, token, *operands)


def output_kernel(count, sofar, place, *refs):
    blocks, weights, refs = refs[:count], refs[count : 2 * count], refs[2 * count :]
    total = refs[0][...] if sofar else None
    for block, weight in zip(blocks, weights):
        part = dot(block[...].astype(jnp.bfloat16), weight[...].astype(jnp.bfloat16))
        total = part if total is None else total + part
    refs[-1][...] = total.astype(refs[-1].dtype)


def output(place, pairs, columns, dtype, sofar=None):
    count = len(pairs)
    rows, width = pairs[0][0].shape
    half = columns // 2

    def weight_spec(at, every):
        if every:
            return pl.BlockSpec((width, half), lambda i, place: (at, 2 * place[3] + i))
        return pl.BlockSpec((width, half), lambda i, place: (at, i))

    by_half = pl.BlockSpec((rows, half), lambda i, place: (0, i))
    operands = [pair[0] for pair in pairs] + [pair[1] for pair in pairs]
    in_specs = [pl.BlockSpec((rows, width), lambda i, place: (0, 0))] * count
    in_specs += [weight_spec(at, every) for _, _, at, every in pairs]
    if sofar is not None:
        operands.append(sofar)
        in_specs.append(by_half)
    return pl.pallas_call(
        functools.partial(output_kernel, count, sofar is not None),
        grid_spec=pltpu.PrefetchScalarGridSpec(
            num_scalar_prefetch=1, grid=(2,), in_specs=in_specs, out_specs=by_half
        ),
        out_shape=jax.ShapeDtypeStruct((rows, columns), dtype),
        compiler_params=params(),
        name="output",
    )(place, *operands)


def within_chip(block, share, distance):
    devices = range(lax.axis_size("tok"))
    route = [(t, t // share * share + (t + distance) % share) for t in devices]
    return lax.ppermute(block, "tok", route)


def flipped(block, share, bit):
    route = [(t, t ^ (bit * share)) for t in range(lax.axis_size("tok"))]
    return lax.ppermute(block, "tok", route)


def crossed(block, share, bit, rows):
    size = lax.axis_size("tok")
    route = []
    for one, two in rows:
        route += [(one * size + t, two * size + (t ^ (bit * share))) for t in range(size)]
    covered = {source for source, _ in route}
    every = range(size * lax.axis_size("block"))
    route += [(device, device) for device in every if device not in covered]
    return lax.ppermute(block, ("block", "tok"), route)


def body(tokens, input_weight, rate_weight, fast_init, output_weight):
    block_count, tok_rows, model_width = tokens.shape
    heads, _, head_dim, _ = fast_init.shape
    share = heads
    members = lax.axis_size("head")
    groups = lax.axis_size("block")
    position = lax.axis_index("block")
    member = lax.axis_index("head")
    core = lax.axis_index("tok") % share
    chip = lax.axis_index("tok") // share
    length = lax.axis_size("tok") // share
    bits = [1 << b for b in range(1, length.bit_length() - 1)]
    flattened = tokens.reshape(tok_rows, model_width)
    weight = jnp.transpose(input_weight, (1, 0, 2))
    rate = jnp.transpose(rate_weight)
    columns = output_weight.shape[1] // members
    every_head = range(heads)

    def exchanged(block):
        return [block] + [within_chip(block, share, distance) for distance in range(1, share)]

    def around(block, ahead):
        return lax.ppermute(block, "head", [(i, (i + ahead) % members) for i in range(members)])

    def place(helper, keep):
        return jnp.stack([core, position == helper, keep, member, chip]).astype(jnp.int32)

    token = jnp.zeros(token_shape.shape, jnp.float32)
    never = position < 0
    here = place(1, never)
    sides = []
    for head in every_head:
        made, token = project(here, token, flattened, weight, rate, 1, 2, head, heads)
        sides.append(exchanged(made))

    kept = [None] * heads
    steps = [None] * heads
    queries = []
    far_weights = []
    for section in range(groups):
        last = section + 1 == groups
        helper = section - 1 if last else section + 1
        both = [(section, helper), (helper, section)]
        parts = []
        for head in every_head:
            if section:
                sums, token = square_sums(here, token, steps[head][0])
                steps[head] = steps[head][0], exchanged(sums), steps[head][1]
        after = place(helper, never)
        for head in every_head:
            if section == 0:
                *pieces, token = fast_grad(here, token, fast_init, head, sides[head], share, 0)
                weights = None
            else:
                *pieces, weights, token = fast_grad(
                    here, token, fast_init, head, sides[head], share, section, steps[head]
                )
                kept[head] = (
                    weights
                    if section == 1
                    else jnp.where(position == section - 1, weights, kept[head])
                )
            steps[head] = None, weights
            own, line, across, corner = pieces
            parts.append(
                (
                    own,
                    crossed(line, share, 1, [(section, section)]),
                    crossed(across, share, 0, both),
                    crossed(corner, share, 1, both),
                )
            )
        here = after
        if section == 0:
            for ahead in range(1, members):
                wide, token = widen(here, token, output_weight, ahead, members)
                far_weights.append(around(wide, ahead))
            for head in every_head:
                made, token = project(here, token, flattened, weight, rate, 0, 1, head, heads)
                queries.append(exchanged(made[0]))
        kernel = gather_kernel
        for bit in bits + [None]:
            for head in every_head:
                *outs, token = combine(here, token, kernel, parts[head], bit)
                if bit is None:
                    parts[head] = outs[0]
                else:
                    parts[head] = outs[1], flipped(outs[0], share, bit)
            kernel = add_kernel
        for bit in reversed(bits):
            for head in every_head:
                pair = parts[head], flipped(parts[head], share, bit)
                parts[head], token = combine(here, token, pair_kernel, pair, bit)
        for head in every_head:
            total = parts[head]
            pieces = (
                total,
                flipped(total, share, 1),
                crossed(total, share, 0, both),
                crossed(total, share, 1, both),
            )
            steps[head] = pieces, steps[head][1]

    here = place(helper, position != groups - 1)
    near, distant = [], [[] for _ in range(1, members)]
    applied = []
    for head in every_head:
        pieces, weights = steps[head]
        sums, token = square_sums(here, token, pieces)
        *parts, token = fast_apply(
            here, token, fast_init, head, queries[head], share,
            pieces, exchanged(sums), weights, kept[head],
        )
        applied.append(
            [parts[0]]
            + [within_chip(block, share, -distance) for distance, block in enumerate(parts[1:], 1)]
        )
    for head in every_head:
        made, token = finish(here, token, applied[head])
        near.append(made)
        for ahead in range(1, members):
            distant[ahead - 1].append(around(made, ahead))
    pairs = [(near[head], output_weight, head, True) for head in every_head]
    others = [
        (distant[ahead][head], far_weights[ahead], head, False)
        for head in every_head
        for ahead in range(members - 1)
    ]
    if not others:
        mixed = output(here, pairs, columns, jnp.bfloat16)
    else:
        mixed = output(here, pairs + others[:-1], columns, jnp.float32)
        mixed = output(here, others[-1:], columns, jnp.bfloat16, mixed)
    return mixed.reshape(block_count, tok_rows, -1)


def solution(mesh):
    placed = (
        P("block", "tok", None),
        P(None, None, "head"),
        P(None, "head"),
        P("head", None, None, None),
        P("head", None),
    )
    return jax.shard_map(
        body, mesh=mesh, in_specs=placed, out_specs=P("block", "tok", "head"), check_vma=False
    )
```

```python
import functools

import jax
import jax.numpy as jnp
from jax import lax
from jax.experimental import pallas as pl
from jax.experimental.pallas import tpu as pltpu
from jax.sharding import PartitionSpec as P

epsilon = 1e-06
step_size = 0.03
vmem_bytes = 20 * 2**20
rows_by_rows = (((1,), (1,)), ((), ()))
over_rows = (((0,), (0,)), ((), ()))
plain = (((1,), (0,)), ((), ()))


def params(limit=vmem_bytes):
    return pltpu.CompilerParams(vmem_limit_bytes=limit)


def dot(left, right, dims=plain):
    return lax.dot_general(left, right, dims, preferred_element_type=jnp.float32)


def split(values):
    high = values.astype(jnp.bfloat16)
    return high, (values - high.astype(jnp.float32)).astype(jnp.bfloat16)


def dot3(left, right, dims=plain):
    return dot(left[0], right[0], dims) + (dot(left[0], right[1], dims) + dot(left[1], right[0], dims))


def normalize(values):
    return values / jnp.sqrt(jnp.mean(values * values, axis=-1, keepdims=True) + epsilon)


token_shape = jax.ShapeDtypeStruct((8, 128), jnp.float32)
unread = pl.BlockSpec(memory_space=pl.ANY)


def whole():
    return pl.BlockSpec(memory_space=pltpu.VMEM)


expected = {
    "project": 4.0,
    "widen": 1.5,
    "square_sums": 0.6,
    "fast_grad": 6.0,
    "fast_apply": 5.0,
    "finish": 0.6,
    "combine": 0.6,
    "output": 4.0,
}


def ordered(kernel, grid, in_specs, out_specs, out_shape, scratch, name, limit=vmem_bytes, late=0):
    def traced(place, token, *refs):
        outs = len(out_shape)
        inputs = len(in_specs)
        refs = refs[:inputs] + refs[inputs + late :]
        refs[inputs + outs][...] = jnp.zeros(token_shape.shape, jnp.float32)
        kernel(place, *refs[: inputs + outs], *refs[inputs + outs + 1 :])

    return pl.pallas_call(
        traced,
        grid_spec=pltpu.PrefetchScalarGridSpec(
            num_scalar_prefetch=1,
            grid=grid,
            in_specs=[unread] + in_specs + [unread] * late,
            out_specs=list(out_specs)
            + [pl.BlockSpec(token_shape.shape, lambda i, place: (0, 0))],
            scratch_shapes=scratch,
        ),
        out_shape=list(out_shape) + [token_shape],
        compiler_params=params(limit),
        cost_estimate=pl.CostEstimate(
            flops=int(expected[name] * 1.1e9), bytes_accessed=0, transcendentals=0
        ),
        name=name,
    )


def project_kernel(chosen, place, tokens, weight, rate, out, held, arrived):
    depth, width = held.shape[1:]
    pieces = arrived.shape[1]
    size = depth // pieces
    copies = []
    for i, (part, head) in enumerate(chosen):
        for k in range(pieces):
            rows = pl.ds(k * size, size)
            copy = pltpu.make_async_copy(
                weight.at[part, rows, pl.ds(head * width, width)],
                held.at[i, rows, :],
                arrived.at[i, k],
            )
            copy.start()
            copies.append(copy)
    for i, (part, head) in enumerate(chosen):
        values = None
        for k in range(pieces):
            copies[i * pieces + k].wait()
            columns = pl.ds(k * size, size)
            more = dot(tokens[:, columns], held[i, columns, :])
            values = more if values is None else values + more
        if part == 2:
            logits = dot(tokens[...], rate[...], rows_by_rows)
            logit = logits[:, head : head + 1]
            rates = jnp.maximum(logit, 0.0) + jnp.log1p(jnp.exp(-jnp.abs(logit)))
            out[i] = values * rates
        else:
            out[i] = normalize(values)


def project(place, token, tokens, weight, rate, chosen, heads):
    rows, depth = tokens.shape
    count = len(chosen)
    width = weight.shape[2] // heads
    return ordered(
        functools.partial(project_kernel, chosen),
        (1,),
        [whole(), pl.BlockSpec(memory_space=pltpu.HBM), whole()],
        [whole()],
        [jax.ShapeDtypeStruct((count, rows, width), jnp.float32)],
        [pltpu.VMEM((count, depth, width), weight.dtype), pltpu.SemaphoreType.DMA((count, 2))],
        "project",
        56 * 2**20,
    )(place, token, tokens, weight, rate)


def widen_kernel(place, weight, out):
    out[...] = weight[...].astype(jnp.float32)


def widen(place, token, weight, ahead, members, share, late):
    rows, columns = weight.shape[0] // share, weight.shape[1] // members
    step = rows // 2

    def chosen(i, place):
        return place[0] * 2 + i, lax.rem(place[3] + ahead, members)

    return ordered(
        widen_kernel,
        (2,),
        [pl.BlockSpec((step, columns), chosen)],
        [pl.BlockSpec((step, columns), lambda i, place: (i, 0))],
        [jax.ShapeDtypeStruct((rows, columns), jnp.float32)],
        [],
        "widen",
        late=len(late),
    )(place, token, weight, *late)


def cut(grads, outs, m, place, role):
    size = outs[0].shape[1]
    odd = lax.rem(place[4], 2)
    for out, piece in zip(
        outs,
        (2 * role + odd, 2 * role + 1 - odd, 2 * (1 - role) + odd, 2 * (1 - role) + 1 - odd),
    ):
        out[m] = grads[pl.ds(pl.multiple_of(piece * size, size), size), :]


def joined(pieces, m, place, role, full):
    size = pieces[0].shape[1]
    odd = lax.rem(place[4], 2)
    for block, piece in zip(
        pieces,
        (2 * role + odd, 2 * role + 1 - odd, 2 * (1 - role) + odd, 2 * (1 - role) + 1 - odd),
    ):
        full[pl.ds(pl.multiple_of(piece * size, size), size), :] = block[m]
    return full[...]


def stepped(place, pieces, sums, weights, start, share, full):
    results = []
    for m in range(3):
        grads = joined(pieces, m, place, place[1], full)
        square = sums[0][m, 0]
        for other in sums[1:]:
            square = square + other[m, 0]
        scale = jnp.full((1, 1), square / (grads.size * share) + epsilon, jnp.float32)
        moved = weights[m].astype(jnp.float32) + grads * (step_size / jnp.sqrt(scale))
        first = start[m].astype(jnp.float32)
        base = jnp.sqrt(jnp.mean(first * first, axis=0, keepdims=True))
        column = jnp.mean(moved * moved, axis=0, keepdims=True)
        results.append(moved * (base / jnp.sqrt(column + epsilon)))
    return results


def sums_kernel(place, *refs):
    pieces, out = refs[:-1], refs[-1]
    row = lax.broadcasted_iota(jnp.int32, out.shape, 0)
    total = jnp.zeros(out.shape, jnp.float32)
    for m in range(3):
        square = sum(jnp.sum(piece[m] * piece[m]) for piece in pieces)
        total = jnp.where(row == m, square, total)
    out[...] = total


def square_sums(place, token, pieces):
    return ordered(
        sums_kernel, (1,), [whole()] * len(pieces), [whole()], [token_shape], [], "square_sums"
    )(place, token, *pieces)


def grad_kernel(share, count, first, place, start, *refs):
    refs = list(refs)
    stepping = count > 0
    if stepping:
        pieces, refs = refs[:4], refs[4:]
        sums, refs = refs[:share], refs[share:]
        if not first:
            old, refs = refs[0], refs[1:]
    sides, refs = refs[:share], refs[share:]
    outs, refs = refs[:4], refs[4:]
    if stepping:
        new, refs = refs[0], refs[1:]
    full, key, target, hidden, upward, gateward = refs
    if stepping:
        weights = stepped(place, pieces, sums, start if first else old, start, share, full)
        for m in range(3):
            new[m] = weights[m]
    else:
        weights = [start[m].astype(jnp.float32) for m in range(3)]
    gate_weight, up_weight, down_weight = (split(block) for block in weights)
    at = 0
    for side in sides:
        rows = side.shape[1]
        chunk = min(rows, 256)
        for begin in range(0, rows, chunk):
            here = pl.ds(at, chunk)
            keys = split(side[0, begin : begin + chunk, :])
            targets = split(side[1, begin : begin + chunk, :])
            key[0, here, :], key[1, here, :] = keys
            target[0, here, :], target[1, here, :] = targets
            gate = dot3(keys, gate_weight)
            upper = dot3(keys, up_weight)
            back = dot3(targets, down_weight)
            sigma = jax.nn.sigmoid(gate)
            active = gate * sigma
            hidden[0, here, :], hidden[1, here, :] = split(active * upper)
            upward[0, here, :], upward[1, here, :] = split(back * active)
            slope = upper * sigma * (1.0 + gate * (1.0 - sigma))
            gateward[0, here, :], gateward[1, here, :] = split(back * slope)
            at += chunk
    for m, left, right in ((2, target, hidden), (1, key, upward), (0, key, gateward)):
        full[...] = dot3((left[0], left[1]), (right[0], right[1]), over_rows)
        cut(full, outs, m, place, 0)


def start_spec(start, head, share):
    _, parts, width, hidden = start.shape
    return pl.BlockSpec(
        (None, parts, width, hidden // share), lambda i, place: (head, 0, 0, place[0])
    )


def fast_grad(place, token, start, head, sides, share, count, step=None, late=()):
    rows = sum(side.shape[1] for side in sides)
    _, parts, width, hidden = start.shape
    hidden = hidden // share
    piece = jax.ShapeDtypeStruct((parts, width // 4, hidden), jnp.float32)
    out_shape = [piece] * 4
    operands = list(sides)
    if step is not None:
        pieces, sums, weights = step
        old = [] if weights is None else [weights]
        operands = list(pieces) + list(sums) + old + operands
        out_shape.append(jax.ShapeDtypeStruct((parts, width, hidden), jnp.float32))
    by_width = pltpu.VMEM((2, rows, width), jnp.bfloat16)
    by_hidden = pltpu.VMEM((2, rows, hidden), jnp.bfloat16)
    return ordered(
        functools.partial(grad_kernel, share, count, step is not None and step[2] is None),
        (1,),
        [start_spec(start, head, share)] + [whole() for _ in operands],
        [whole() for _ in out_shape],
        out_shape,
        [
            pltpu.VMEM((width, hidden), jnp.float32),
            by_width,
            by_width,
            by_hidden,
            by_hidden,
            by_hidden,
        ],
        "fast_grad",
        late=len(late),
    )(place, token, start, *operands, *late)


def apply_kernel(share, head, place, start, *refs):
    pieces, refs = refs[:4], refs[4:]
    sums, refs = refs[:share], refs[share:]
    old, kept, refs = refs[0], refs[1], refs[2:]
    queries, outs, full = refs[:share], refs[share : 2 * share], refs[-1]
    keep = place[2] == 1
    weights = stepped(place, pieces, sums, old, start, share, full)
    weights = [jnp.where(keep, kept[m], weights[m]) for m in range(3)]
    gate_weight, up_weight, down_weight = (split(block) for block in weights)
    for query, out in zip(queries, outs):
        rows = query.shape[1]
        chunk = min(rows, 256)
        for begin in range(0, rows, chunk):
            here = pl.ds(begin, chunk)
            values = split(query[head, here, :])
            gate = dot3(values, gate_weight)
            hidden = split(gate * jax.nn.sigmoid(gate) * dot3(values, up_weight))
            out[here, :] = dot3(hidden, down_weight, rows_by_rows)


def fast_apply(place, token, start, head, queries, share, pieces, sums, weights, kept):
    operands = list(pieces) + list(sums) + [weights, kept] + list(queries)
    _, rows, width = queries[0].shape
    return ordered(
        functools.partial(apply_kernel, share, head),
        (1,),
        [start_spec(start, head, share)] + [whole() for _ in operands],
        [whole() for _ in queries],
        [jax.ShapeDtypeStruct((rows, width), jnp.float32) for _ in queries],
        [pltpu.VMEM(weights.shape[1:], jnp.float32)],
        "fast_apply",
    )(place, token, start, *operands)


def finish_kernel(place, *refs):
    total = refs[0][...]
    for part in refs[1:-1]:
        total = total + part[...]
    refs[-1][...] = normalize(total)


def finish(place, token, parts):
    return ordered(
        finish_kernel,
        (1,),
        [whole() for _ in parts],
        [whole()],
        [jax.ShapeDtypeStruct(parts[0].shape, jnp.float32)],
        [],
        "finish",
    )(place, token, *parts)


def halve(total, bit, place, outs):
    if bit is None:
        outs[0][...] = total
        return
    size = outs[0].shape[1]
    mine = lax.rem(lax.div(place[4], bit), 2) == 1
    low, high = total[:, :size], total[:, size:]
    outs[0][...] = jnp.where(mine, low, high)
    outs[1][...] = jnp.where(mine, high, low)


def gather_kernel(bit, place, own, line, across, corner, *outs):
    helping = place[1] == 1
    total = jnp.where(helping, across[...], own[...]) + jnp.where(helping, corner[...], line[...])
    halve(total, bit, place, outs)


def add_kernel(bit, place, own, other, *outs):
    halve(own[...] + other[...], bit, place, outs)


def pair_kernel(bit, place, own, other, out):
    size = own.shape[1]
    mine = lax.rem(lax.div(place[4], bit), 2) == 1
    out[:, :size] = jnp.where(mine, other[...], own[...])
    out[:, size:] = jnp.where(mine, own[...], other[...])


def combine(place, token, kernel, operands, bit, late=()):
    parts, size, width = operands[0].shape
    count = 1
    if kernel is pair_kernel:
        size = 2 * size
    elif bit is not None:
        count, size = 2, size // 2
    return ordered(
        functools.partial(kernel, bit),
        (1,),
        [whole() for _ in operands],
        [whole()] * count,
        [jax.ShapeDtypeStruct((parts, size, width), jnp.float32)] * count,
        [],
        "combine",
        late=len(late),
    )(place, token, *operands, *late)


def output_kernel(heads, share, sofar, place, *refs):
    refs, out = list(refs[:-1]), refs[-1]
    total = None
    for head, far in heads:
        block = refs.pop(0)[...].astype(jnp.bfloat16)
        weight = refs.pop(0)[...]
        if far:
            for distance in range(1, share):
                other = refs.pop(0)[...]
                weight = jnp.where(lax.rem(place[0] + share - distance, share) == head, other, weight)
        part = dot(block, weight.astype(jnp.bfloat16))
        total = part if total is None else total + part
    if sofar:
        total = total + refs.pop(0)[...]
    out[...] = total.astype(out.dtype)


def output(place, token, near, distant, columns, share, dtype, sofar=None):
    rows, width = (near + distant)[0][1].shape
    half = columns // 2
    by_half = pl.BlockSpec((rows, half), lambda i, place: (0, i))
    by_rows = pl.BlockSpec((rows, width), lambda i, place: (0, 0))
    operands, in_specs = [], []
    for head, block, weight in near:
        operands += [block, weight]
        spec = pl.BlockSpec((width, half), lambda i, place, head=head: (head, 2 * place[3] + i))
        in_specs += [by_rows, spec]
    for head, block, weights in distant:
        operands += [block] + list(weights)
        in_specs += [by_rows] + [
            pl.BlockSpec((width, half), lambda i, place: (0, i)) for _ in weights
        ]
    if sofar is not None:
        operands.append(sofar)
        in_specs.append(by_half)
    heads = [(head, False) for head, _, _ in near] + [(head, True) for head, _, _ in distant]
    return ordered(
        functools.partial(output_kernel, heads, share, sofar is not None),
        (2,),
        in_specs,
        [by_half],
        [jax.ShapeDtypeStruct((rows, columns), dtype)],
        [],
        "output",
    )(place, token, *operands)


def within_chip(block, share, distance):
    devices = range(lax.axis_size("tok"))
    route = [(t, t // share * share + (t + distance) % share) for t in devices]
    return lax.ppermute(block, "tok", route)


def flipped(block, share, bit):
    route = [(t, t ^ (bit * share)) for t in range(lax.axis_size("tok"))]
    return lax.ppermute(block, "tok", route)


def crossed(block, share, bit, rows):
    size = lax.axis_size("tok")
    route = []
    for one, two in rows:
        route += [(one * size + t, two * size + (t ^ (bit * share))) for t in range(size)]
    covered = {source for source, _ in route}
    every = range(size * lax.axis_size("block"))
    route += [(device, device) for device in every if device not in covered]
    return lax.ppermute(block, ("block", "tok"), route)


def body(tokens, input_weight, rate_weight, fast_init, output_weight):
    block_count, tok_rows, model_width = tokens.shape
    heads, _, head_dim, _ = fast_init.shape
    share = heads
    members = lax.axis_size("head")
    groups = lax.axis_size("block")
    position = lax.axis_index("block")
    member = lax.axis_index("head")
    core = lax.axis_index("tok") % share
    chip = lax.axis_index("tok") // share
    length = lax.axis_size("tok") // share
    bits = [1 << b for b in range(1, length.bit_length() - 1)]
    flattened = tokens.reshape(tok_rows, model_width)
    weight = jnp.transpose(input_weight, (1, 0, 2))
    rate = jnp.transpose(rate_weight)
    columns = output_weight.shape[1] // members
    every_head = range(heads)

    def exchanged(block):
        return [block] + [within_chip(block, share, distance) for distance in range(1, share)]

    def around(block, ahead):
        return lax.ppermute(block, "head", [(i, (i + ahead) % members) for i in range(members)])

    def place(helper, keep):
        return jnp.stack([core, position == helper, keep, member, chip]).astype(jnp.int32)

    token = jnp.zeros(token_shape.shape, jnp.float32)
    never = position < 0
    here = place(1, never)
    sides = []
    for head in every_head:
        made, token = project(
            here, token, flattened, weight, rate, [(1, head), (2, head)], heads
        )
        sides.append(exchanged(made))

    kept = [None] * heads
    steps = [None] * heads
    queries = []
    far_weights = []
    parts = [None] * heads

    def start_section(section, head, here, helper, token):
        both = [(section, helper), (helper, section)]
        if section == 0:
            late = queries[head][0] if head else ()
            *pieces, token = fast_grad(
                here, token, fast_init, head, sides[head], share, 0, None, late
            )
            weights = None
        else:
            pieces, weights = steps[head]
            sums, token = square_sums(here, token, pieces)
            *pieces, weights, token = fast_grad(
                here, token, fast_init, head, sides[head], share, section,
                (pieces, exchanged(sums), weights),
            )
            kept[head] = (
                weights
                if section == 1
                else jnp.where(position == section - 1, weights, kept[head])
            )
        own, line, across, corner = pieces
        steps[head] = None, weights
        parts[head] = (
            own,
            crossed(line, share, 1, [(section, section)]),
            crossed(across, share, 0, both),
            crossed(corner, share, 1, both),
        )
        return token

    def advance(stage, head, here, both, token, late):
        count = len(bits)
        if stage <= count:
            bit = bits[stage] if stage < count else None
            kernel = add_kernel if stage else gather_kernel
            *outs, token = combine(here, token, kernel, parts[head], bit, late)
            total = outs[-1]
            if bit is not None:
                parts[head] = total, flipped(outs[0], share, bit)
                return token
        else:
            bit = bits[2 * count - stage]
            total, token = combine(here, token, pair_kernel, parts[head], bit, late)
        if stage < 2 * count:
            parts[head] = total, flipped(total, share, bits[2 * count - stage - 1])
        else:
            pieces = (
                total,
                flipped(total, share, 1),
                crossed(total, share, 0, both),
                crossed(total, share, 1, both),
            )
            steps[head] = pieces, steps[head][1]
        return token

    near, distant = [], [[] for _ in range(1, members)]
    for section in range(groups):
        last = section + 1 == groups
        helper = section - 1 if last else section + 1
        both = [(section, helper), (helper, section)]
        previous, here = here, place(helper, never)
        for head in every_head:
            token = start_section(section, head, previous, helper, token)
            if section == 0 and head == 0:
                for ahead in range(1, members):
                    late = [block for blocks in sides[1:] for block in blocks]
                    wide, token = widen(here, token, output_weight, ahead, members, share, late)
                    far_weights.append(exchanged(around(wide, ahead)))
                chosen_parts = [(0, other) for other in every_head]
                made, token = project(here, token, flattened, weight, rate, chosen_parts, heads)
                moved = exchanged(made)
                queries += [(block, other) for other in every_head for block in [moved]]
        stages = 2 * len(bits) + 1
        for turn in range(stages + heads - 1):
            for head in every_head:
                stage = turn - head
                if 0 <= stage < stages:
                    late = []
                    if section == 1 and head == 0 and stage == 1:
                        late = [block for blocks in far_weights for block in blocks]
                    token = advance(stage, head, here, both, token, late)

    here = place(helper, position != groups - 1)
    for head in every_head:
        pieces, weights = steps[head]
        sums, token = square_sums(here, token, pieces)
        *made, token = fast_apply(
            here, token, fast_init, head, queries[head][0], share,
            pieces, exchanged(sums), weights, kept[head],
        )
        back = [within_chip(block, share, -distance) for distance, block in enumerate(made[1:], 1)]
        whole_block, token = finish(here, token, [made[0]] + back)
        near.append(whole_block)
        for ahead in range(1, members):
            distant[ahead - 1].append(around(whole_block, ahead))
    pairs = [(head, near[head], output_weight) for head in every_head]
    others = [
        (head, distant[ahead][head], far_weights[ahead])
        for head in every_head
        for ahead in range(members - 1)
    ]
    first, final = others[: 1 - members], others[1 - members :]
    if members == 1:
        mixed, token = output(here, token, pairs, [], columns, share, jnp.bfloat16)
    else:
        mixed, token = output(here, token, pairs, first, columns, share, jnp.float32)
        mixed, token = output(here, token, [], final, columns, share, jnp.bfloat16, mixed)
    return mixed.reshape(block_count, tok_rows, -1)


def solution(mesh):
    placed = (
        P("block", "tok", None),
        P(None, None, "head"),
        P(None, "head"),
        P("head", None, None, None),
        P("head", None),
    )
    return jax.shard_map(
        body, mesh=mesh, in_specs=placed, out_specs=P("block", "tok", "head"), check_vma=False
    )
```

```python
import functools

import jax
import jax.numpy as jnp
from jax import lax
from jax.experimental import pallas as pl
from jax.experimental.pallas import tpu as pltpu
from jax.sharding import PartitionSpec as P

epsilon = 1e-06
step_size = 0.03
vmem_bytes = 20 * 2**20
rows_by_rows = (((1,), (1,)), ((), ()))
over_rows = (((0,), (0,)), ((), ()))
plain = (((1,), (0,)), ((), ()))


def params(limit=vmem_bytes):
    return pltpu.CompilerParams(vmem_limit_bytes=limit)


def dot(left, right, dims=plain):
    return lax.dot_general(left, right, dims, preferred_element_type=jnp.float32)


def split(values):
    high = values.astype(jnp.bfloat16)
    return high, (values - high.astype(jnp.float32)).astype(jnp.bfloat16)


def dot3(left, right, dims=plain):
    return dot(left[0], right[0], dims) + (dot(left[0], right[1], dims) + dot(left[1], right[0], dims))


def normalize(values):
    return values / jnp.sqrt(jnp.mean(values * values, axis=-1, keepdims=True) + epsilon)


token_shape = jax.ShapeDtypeStruct((8, 128), jnp.float32)
unread = pl.BlockSpec(memory_space=pl.ANY)


def whole():
    return pl.BlockSpec(memory_space=pltpu.VMEM)


hiding = {"project": 40 * 10**9, "widen": 40 * 10**9}


def ordered(kernel, grid, in_specs, out_specs, out_shape, scratch, name, limit=vmem_bytes, late=0):
    def traced(place, token, *refs):
        outs = len(out_shape)
        inputs = len(in_specs)
        refs = refs[:inputs] + refs[inputs + late :]
        refs[inputs + outs][...] = jnp.zeros(token_shape.shape, jnp.float32)
        kernel(place, *refs[: inputs + outs], *refs[inputs + outs + 1 :])

    return pl.pallas_call(
        traced,
        grid_spec=pltpu.PrefetchScalarGridSpec(
            num_scalar_prefetch=1,
            grid=grid,
            in_specs=[unread] + in_specs + [unread] * late,
            out_specs=list(out_specs)
            + [pl.BlockSpec(token_shape.shape, lambda i, place: (0, 0))],
            scratch_shapes=scratch,
        ),
        out_shape=list(out_shape) + [token_shape],
        compiler_params=params(limit),
        cost_estimate=pl.CostEstimate(
            flops=hiding.get(name, 0), bytes_accessed=0, transcendentals=0
        ),
        name=name,
    )


def project_kernel(chosen, place, tokens, weight, rate, out):
    values = dot(tokens[...], weight[...])
    for i, (part, head) in enumerate(chosen):

        @pl.when(pl.program_id(0) == i)
        def _():
            if part == 2:
                logits = dot(tokens[...], rate[...], rows_by_rows)
                logit = logits[:, head : head + 1]
                rates = jnp.maximum(logit, 0.0) + jnp.log1p(jnp.exp(-jnp.abs(logit)))
                out[...] = values * rates
            else:
                out[...] = normalize(values)


def project(place, token, tokens, weight, rate, chosen, heads):
    rows, depth = tokens.shape
    count = len(chosen)
    width = weight.shape[2] // heads
    by_part = [part for part, _ in chosen]
    by_head = [head for _, head in chosen]

    def table(values, i):
        picked = values[0]
        for at, value in enumerate(values[1:], 1):
            picked = jnp.where(i >= at, value, picked)
        return picked

    return ordered(
        functools.partial(project_kernel, chosen),
        (count,),
        [
            pl.BlockSpec((rows, depth), lambda i, place: (0, 0)),
            pl.BlockSpec(
                (None, depth, width),
                lambda i, place: (table(by_part, i), 0, table(by_head, i)),
            ),
            pl.BlockSpec(rate.shape, lambda i, place: (0, 0)),
        ],
        [pl.BlockSpec((None, rows, width), lambda i, place: (i, 0, 0))],
        [jax.ShapeDtypeStruct((count, rows, width), jnp.float32)],
        [],
        "project",
        50 * 2**20,
    )(place, token, tokens, weight, rate)


def widen_kernel(place, weight, out):
    out[...] = weight[...].astype(jnp.float32)


def widen(place, token, weight, ahead, members, share, late):
    rows, columns = weight.shape[0] // share, weight.shape[1] // members
    step = rows // 2

    def chosen(i, place):
        return place[0] * 2 + i, lax.rem(place[3] + ahead, members)

    return ordered(
        widen_kernel,
        (2,),
        [pl.BlockSpec((step, columns), chosen)],
        [pl.BlockSpec((step, columns), lambda i, place: (i, 0))],
        [jax.ShapeDtypeStruct((rows, columns), jnp.float32)],
        [],
        "widen",
        late=len(late),
    )(place, token, weight, *late)


def cut(grads, outs, m, place, role):
    size = outs[0].shape[1]
    odd = lax.rem(place[4], 2)
    for out, piece in zip(
        outs,
        (2 * role + odd, 2 * role + 1 - odd, 2 * (1 - role) + odd, 2 * (1 - role) + 1 - odd),
    ):
        out[m] = grads[pl.ds(pl.multiple_of(piece * size, size), size), :]


def joined(pieces, m, place, role, full):
    size = pieces[0].shape[1]
    odd = lax.rem(place[4], 2)
    for block, piece in zip(
        pieces,
        (2 * role + odd, 2 * role + 1 - odd, 2 * (1 - role) + odd, 2 * (1 - role) + 1 - odd),
    ):
        full[pl.ds(pl.multiple_of(piece * size, size), size), :] = block[m]
    return full[...]


def stepped(place, pieces, sums, weights, start, share, full):
    results = []
    for m in range(3):
        grads = joined(pieces, m, place, place[1], full)
        square = sums[0][m, 0]
        for other in sums[1:]:
            square = square + other[m, 0]
        scale = jnp.full((1, 1), square / (grads.size * share) + epsilon, jnp.float32)
        moved = weights[m].astype(jnp.float32) + grads * (step_size / jnp.sqrt(scale))
        first = start[m].astype(jnp.float32)
        base = jnp.sqrt(jnp.mean(first * first, axis=0, keepdims=True))
        column = jnp.mean(moved * moved, axis=0, keepdims=True)
        results.append(moved * (base / jnp.sqrt(column + epsilon)))
    return results


def sums_kernel(place, *refs):
    pieces, out = refs[:-1], refs[-1]
    row = lax.broadcasted_iota(jnp.int32, out.shape, 0)
    total = jnp.zeros(out.shape, jnp.float32)
    for m in range(3):
        square = sum(jnp.sum(piece[m] * piece[m]) for piece in pieces)
        total = jnp.where(row == m, square, total)
    out[...] = total


def square_sums(place, token, pieces):
    return ordered(
        sums_kernel, (1,), [whole()] * len(pieces), [whole()], [token_shape], [], "square_sums"
    )(place, token, *pieces)


def grad_kernel(share, count, first, place, start, *refs):
    refs = list(refs)
    stepping = count > 0
    if stepping:
        pieces, refs = refs[:4], refs[4:]
        sums, refs = refs[:share], refs[share:]
        if not first:
            old, refs = refs[0], refs[1:]
    sides, refs = refs[:share], refs[share:]
    outs, refs = refs[:4], refs[4:]
    if stepping:
        new, refs = refs[0], refs[1:]
    full, key, target, hidden, upward, gateward = refs
    if stepping:
        weights = stepped(place, pieces, sums, start if first else old, start, share, full)
        for m in range(3):
            new[m] = weights[m]
    else:
        weights = [start[m].astype(jnp.float32) for m in range(3)]
    gate_weight, up_weight, down_weight = (split(block) for block in weights)
    at = 0
    for side in sides:
        rows = side.shape[1]
        chunk = min(rows, 256)
        for begin in range(0, rows, chunk):
            here = pl.ds(at, chunk)
            keys = split(side[0, begin : begin + chunk, :])
            targets = split(side[1, begin : begin + chunk, :])
            key[0, here, :], key[1, here, :] = keys
            target[0, here, :], target[1, here, :] = targets
            gate = dot3(keys, gate_weight)
            upper = dot3(keys, up_weight)
            back = dot3(targets, down_weight)
            sigma = jax.nn.sigmoid(gate)
            active = gate * sigma
            hidden[0, here, :], hidden[1, here, :] = split(active * upper)
            upward[0, here, :], upward[1, here, :] = split(back * active)
            slope = upper * sigma * (1.0 + gate * (1.0 - sigma))
            gateward[0, here, :], gateward[1, here, :] = split(back * slope)
            at += chunk
    for m, left, right in ((2, target, hidden), (1, key, upward), (0, key, gateward)):
        full[...] = dot3((left[0], left[1]), (right[0], right[1]), over_rows)
        cut(full, outs, m, place, 0)


def start_spec(start, head, share):
    _, parts, width, hidden = start.shape
    return pl.BlockSpec(
        (None, parts, width, hidden // share), lambda i, place: (head, 0, 0, place[0])
    )


def fast_grad(place, token, start, head, sides, share, count, step=None, late=()):
    rows = sum(side.shape[1] for side in sides)
    _, parts, width, hidden = start.shape
    hidden = hidden // share
    piece = jax.ShapeDtypeStruct((parts, width // 4, hidden), jnp.float32)
    out_shape = [piece] * 4
    operands = list(sides)
    if step is not None:
        pieces, sums, weights = step
        old = [] if weights is None else [weights]
        operands = list(pieces) + list(sums) + old + operands
        out_shape.append(jax.ShapeDtypeStruct((parts, width, hidden), jnp.float32))
    by_width = pltpu.VMEM((2, rows, width), jnp.bfloat16)
    by_hidden = pltpu.VMEM((2, rows, hidden), jnp.bfloat16)
    return ordered(
        functools.partial(grad_kernel, share, count, step is not None and step[2] is None),
        (1,),
        [start_spec(start, head, share)] + [whole() for _ in operands],
        [whole() for _ in out_shape],
        out_shape,
        [
            pltpu.VMEM((width, hidden), jnp.float32),
            by_width,
            by_width,
            by_hidden,
            by_hidden,
            by_hidden,
        ],
        "fast_grad",
        late=len(late),
    )(place, token, start, *operands, *late)


def apply_kernel(share, head, place, start, *refs):
    pieces, refs = refs[:4], refs[4:]
    sums, refs = refs[:share], refs[share:]
    old, kept, refs = refs[0], refs[1], refs[2:]
    queries, outs, full = refs[:share], refs[share : 2 * share], refs[-1]
    keep = place[2] == 1
    weights = stepped(place, pieces, sums, old, start, share, full)
    weights = [jnp.where(keep, kept[m], weights[m]) for m in range(3)]
    gate_weight, up_weight, down_weight = (split(block) for block in weights)
    for query, out in zip(queries, outs):
        rows = query.shape[1]
        chunk = min(rows, 256)
        for begin in range(0, rows, chunk):
            here = pl.ds(begin, chunk)
            values = split(query[2 + head, here, :])
            gate = dot3(values, gate_weight)
            hidden = split(gate * jax.nn.sigmoid(gate) * dot3(values, up_weight))
            out[here, :] = dot3(hidden, down_weight, rows_by_rows)


def fast_apply(place, token, start, head, queries, share, pieces, sums, weights, kept, late):
    operands = list(pieces) + list(sums) + [weights, kept] + list(queries)
    _, rows, width = queries[0].shape
    return ordered(
        functools.partial(apply_kernel, share, head),
        (1,),
        [start_spec(start, head, share)] + [whole() for _ in operands],
        [whole() for _ in queries],
        [jax.ShapeDtypeStruct((rows, width), jnp.float32) for _ in queries],
        [pltpu.VMEM(weights.shape[1:], jnp.float32)],
        "fast_apply",
        late=len(late),
    )(place, token, start, *operands, *late)


def finish_kernel(place, *refs):
    total = refs[0][...]
    for part in refs[1:-1]:
        total = total + part[...]
    refs[-1][...] = normalize(total)


def finish(place, token, parts):
    return ordered(
        finish_kernel,
        (1,),
        [whole() for _ in parts],
        [whole()],
        [jax.ShapeDtypeStruct(parts[0].shape, jnp.float32)],
        [],
        "finish",
    )(place, token, *parts)


def halve(total, bit, place, outs):
    if bit is None:
        outs[0][...] = total
        return
    size = outs[0].shape[1]
    mine = lax.rem(lax.div(place[4], bit), 2) == 1
    low, high = total[:, :size], total[:, size:]
    outs[0][...] = jnp.where(mine, low, high)
    outs[1][...] = jnp.where(mine, high, low)


def gather_kernel(bit, place, own, line, across, corner, *outs):
    helping = place[1] == 1
    total = jnp.where(helping, across[...], own[...]) + jnp.where(helping, corner[...], line[...])
    halve(total, bit, place, outs)


def add_kernel(bit, place, own, other, *outs):
    halve(own[...] + other[...], bit, place, outs)


def pair_kernel(bit, place, own, other, out):
    size = own.shape[1]
    mine = lax.rem(lax.div(place[4], bit), 2) == 1
    out[:, :size] = jnp.where(mine, other[...], own[...])
    out[:, size:] = jnp.where(mine, own[...], other[...])


def combine(place, token, kernel, operands, bit, late=()):
    parts, size, width = operands[0].shape
    count = 1
    if kernel is pair_kernel:
        size = 2 * size
    elif bit is not None:
        count, size = 2, size // 2
    return ordered(
        functools.partial(kernel, bit),
        (1,),
        [whole() for _ in operands],
        [whole()] * count,
        [jax.ShapeDtypeStruct((parts, size, width), jnp.float32)] * count,
        [],
        "combine",
        late=len(late),
    )(place, token, *operands, *late)


def output_kernel(heads, share, sofar, place, *refs):
    refs, out = list(refs[:-1]), refs[-1]
    total = None
    for head, far in heads:
        block = refs.pop(0)[...].astype(jnp.bfloat16)
        weight = refs.pop(0)[...]
        if far:
            for distance in range(1, share):
                other = refs.pop(0)[...]
                weight = jnp.where(lax.rem(place[0] + share - distance, share) == head, other, weight)
        part = dot(block, weight.astype(jnp.bfloat16))
        total = part if total is None else total + part
    if sofar:
        total = total + refs.pop(0)[...]
    out[...] = total.astype(out.dtype)


def output(place, token, near, distant, columns, share, dtype, sofar=None):
    rows, width = (near + distant)[0][1].shape
    half = columns // 2
    by_half = pl.BlockSpec((rows, half), lambda i, place: (0, i))
    by_rows = pl.BlockSpec((rows, width), lambda i, place: (0, 0))
    operands, in_specs = [], []
    for head, block, weight in near:
        operands += [block, weight]
        spec = pl.BlockSpec((width, half), lambda i, place, head=head: (head, 2 * place[3] + i))
        in_specs += [by_rows, spec]
    for head, block, weights in distant:
        operands += [block] + list(weights)
        in_specs += [by_rows] + [
            pl.BlockSpec((width, half), lambda i, place: (0, i)) for _ in weights
        ]
    if sofar is not None:
        operands.append(sofar)
        in_specs.append(by_half)
    heads = [(head, False) for head, _, _ in near] + [(head, True) for head, _, _ in distant]
    return ordered(
        functools.partial(output_kernel, heads, share, sofar is not None),
        (2,),
        in_specs,
        [by_half],
        [jax.ShapeDtypeStruct((rows, columns), dtype)],
        [],
        "output",
    )(place, token, *operands)


def within_chip(block, share, distance):
    devices = range(lax.axis_size("tok"))
    route = [(t, t // share * share + (t + distance) % share) for t in devices]
    return lax.ppermute(block, "tok", route)


def flipped(block, share, bit):
    route = [(t, t ^ (bit * share)) for t in range(lax.axis_size("tok"))]
    return lax.ppermute(block, "tok", route)


def crossed(block, share, bit, rows):
    size = lax.axis_size("tok")
    route = []
    for one, two in rows:
        route += [(one * size + t, two * size + (t ^ (bit * share))) for t in range(size)]
    covered = {source for source, _ in route}
    every = range(size * lax.axis_size("block"))
    route += [(device, device) for device in every if device not in covered]
    return lax.ppermute(block, ("block", "tok"), route)


def body(tokens, input_weight, rate_weight, fast_init, output_weight):
    block_count, tok_rows, model_width = tokens.shape
    heads, _, head_dim, _ = fast_init.shape
    share = heads
    members = lax.axis_size("head")
    groups = lax.axis_size("block")
    position = lax.axis_index("block")
    member = lax.axis_index("head")
    core = lax.axis_index("tok") % share
    chip = lax.axis_index("tok") // share
    length = lax.axis_size("tok") // share
    bits = [1 << b for b in range(1, length.bit_length() - 1)]
    flattened = tokens.reshape(tok_rows, model_width)
    weight = jnp.transpose(input_weight, (1, 0, 2))
    rate = jnp.transpose(rate_weight)
    columns = output_weight.shape[1] // members
    every_head = range(heads)

    def exchanged(block):
        return [block] + [within_chip(block, share, distance) for distance in range(1, share)]

    def around(block, ahead):
        return lax.ppermute(block, "head", [(i, (i + ahead) % members) for i in range(members)])

    def place(helper, keep):
        return jnp.stack([core, position == helper, keep, member, chip]).astype(jnp.int32)

    token = jnp.zeros(token_shape.shape, jnp.float32)
    never = position < 0
    here = place(1, never)
    sides = [None] * heads

    for head in every_head:
        chosen_parts = [(1, head), (2, head)]
        if head + 1 == heads:
            chosen_parts += [(0, other) for other in every_head]
        made, token = project(here, token, flattened, weight, rate, chosen_parts, heads)
        sides[head] = exchanged(made)
    queries = sides[-1]

    kept = [None] * heads
    steps = [None] * heads
    far_weights = []
    parts = [None] * heads

    def start_section(section, head, here, helper, token):
        both = [(section, helper), (helper, section)]
        if section == 0:
            *pieces, token = fast_grad(here, token, fast_init, head, sides[head], share, 0)
            weights = None
        else:
            pieces, weights = steps[head]
            sums, token = square_sums(here, token, pieces)
            *pieces, weights, token = fast_grad(
                here, token, fast_init, head, sides[head], share, section,
                (pieces, exchanged(sums), weights),
            )
            kept[head] = (
                weights
                if section == 1
                else jnp.where(position == section - 1, weights, kept[head])
            )
        own, line, across, corner = pieces
        steps[head] = None, weights
        parts[head] = (
            own,
            crossed(line, share, 1, [(section, section)]),
            crossed(across, share, 0, both),
            crossed(corner, share, 1, both),
        )
        return token

    def advance(stage, head, here, both, token, late):
        count = len(bits)
        if stage <= count:
            bit = bits[stage] if stage < count else None
            kernel = add_kernel if stage else gather_kernel
            *outs, token = combine(here, token, kernel, parts[head], bit, late)
            total = outs[-1]
            if bit is not None:
                parts[head] = total, flipped(outs[0], share, bit)
                return token
        else:
            bit = bits[2 * count - stage]
            total, token = combine(here, token, pair_kernel, parts[head], bit, late)
        if stage < 2 * count:
            parts[head] = total, flipped(total, share, bits[2 * count - stage - 1])
        else:
            pieces = (
                total,
                flipped(total, share, 1),
                crossed(total, share, 0, both),
                crossed(total, share, 1, both),
            )
            steps[head] = pieces, steps[head][1]
        return token

    near, distant = [], [[] for _ in range(1, members)]
    for section in range(groups):
        last = section + 1 == groups
        helper = section - 1 if last else section + 1
        both = [(section, helper), (helper, section)]
        previous, here = here, place(helper, never)
        for head in every_head:
            token = start_section(section, head, previous, helper, token)
            if section == 0 and head == 0:
                for ahead in range(1, members):
                    wide, token = widen(here, token, output_weight, ahead, members, share, ())
                    far_weights.append(exchanged(around(wide, ahead)))
        stages = 2 * len(bits) + 1
        for turn in range(stages + heads - 1):
            for head in every_head:
                stage = turn - head
                if 0 <= stage < stages:
                    late = []
                    if section == 0 and head == heads - 1 and stage == stages - 1:
                        late = [blocks[0] for blocks in far_weights]
                    if section == 1 and head == heads - 1 and stage == 0:
                        late = [block for blocks in far_weights for block in blocks]
                    token = advance(stage, head, here, both, token, late)

    here = place(helper, position != groups - 1)
    for head in every_head:
        pieces, weights = steps[head]
        sums, token = square_sums(here, token, pieces)
        *made, token = fast_apply(
            here, token, fast_init, head, queries, share,
            pieces, exchanged(sums), weights, kept[head],
            [block for blocks in distant for block in blocks],
        )
        back = [within_chip(block, share, -distance) for distance, block in enumerate(made[1:], 1)]
        whole_block, token = finish(here, token, [made[0]] + back)
        near.append(whole_block)
        for ahead in range(1, members):
            distant[ahead - 1].append(around(whole_block, ahead))
    pairs = [(head, near[head], output_weight) for head in every_head]
    others = [
        (head, distant[ahead][head], far_weights[ahead])
        for head in every_head
        for ahead in range(members - 1)
    ]
    first, final = others[: 1 - members], others[1 - members :]
    if members == 1:
        mixed, token = output(here, token, pairs, [], columns, share, jnp.bfloat16)
    else:
        mixed, token = output(here, token, pairs, first, columns, share, jnp.float32)
        mixed, token = output(here, token, [], final, columns, share, jnp.bfloat16, mixed)
    return mixed.reshape(block_count, tok_rows, -1)


def solution(mesh):
    placed = (
        P("block", "tok", None),
        P(None, None, "head"),
        P(None, "head"),
        P("head", None, None, None),
        P("head", None),
    )
    return jax.shard_map(
        body, mesh=mesh, in_specs=placed, out_specs=P("block", "tok", "head"), check_vma=False
    )
```

```python
import functools

import jax
import jax.numpy as jnp
from jax import lax
from jax.experimental import pallas as pl
from jax.experimental.pallas import tpu as pltpu
from jax.sharding import PartitionSpec as P

epsilon = 1e-06
step_size = 0.03
vmem_bytes = 20 * 2**20
rows_by_rows = (((1,), (1,)), ((), ()))
over_rows = (((0,), (0,)), ((), ()))
plain = (((1,), (0,)), ((), ()))


def params(limit=vmem_bytes):
    return pltpu.CompilerParams(vmem_limit_bytes=limit)


def dot(left, right, dims=plain):
    return lax.dot_general(left, right, dims, preferred_element_type=jnp.float32)


def split(values):
    high = values.astype(jnp.bfloat16)
    return high, (values - high.astype(jnp.float32)).astype(jnp.bfloat16)


def dot3(left, right, dims=plain):
    return dot(left[0], right[0], dims) + (dot(left[0], right[1], dims) + dot(left[1], right[0], dims))


def normalize(values):
    return values / jnp.sqrt(jnp.mean(values * values, axis=-1, keepdims=True) + epsilon)


token_shape = jax.ShapeDtypeStruct((8, 128), jnp.float32)
unread = pl.BlockSpec(memory_space=pl.ANY)


def whole():
    return pl.BlockSpec(memory_space=pltpu.VMEM)


hiding = {"project": 40 * 10**9, "output": 2 * 10**9}


def ordered(kernel, grid, in_specs, out_specs, out_shape, scratch, name, limit=vmem_bytes, late=0):
    def traced(place, token, *refs):
        outs = len(out_shape)
        inputs = len(in_specs)
        refs = refs[:inputs] + refs[inputs + late :]
        refs[inputs + outs][...] = jnp.zeros(token_shape.shape, jnp.float32)
        kernel(place, *refs[: inputs + outs], *refs[inputs + outs + 1 :])

    return pl.pallas_call(
        traced,
        grid_spec=pltpu.PrefetchScalarGridSpec(
            num_scalar_prefetch=1,
            grid=grid,
            in_specs=[unread] + in_specs + [unread] * late,
            out_specs=list(out_specs)
            + [pl.BlockSpec(token_shape.shape, lambda i, place: (0, 0))],
            scratch_shapes=scratch,
        ),
        out_shape=list(out_shape) + [token_shape],
        compiler_params=params(limit),
        cost_estimate=pl.CostEstimate(
            flops=hiding.get(name, 0), bytes_accessed=0, transcendentals=0
        ),
        name=name,
    )


def project_kernel(chosen, place, tokens, weight, rate, out):
    values = dot(tokens[...], weight[...])
    for i, (part, head) in enumerate(chosen):

        @pl.when(pl.program_id(0) == i)
        def _():
            if part == 2:
                logits = dot(tokens[...], rate[...], rows_by_rows)
                logit = logits[:, head : head + 1]
                rates = jnp.maximum(logit, 0.0) + jnp.log1p(jnp.exp(-jnp.abs(logit)))
                result = values * rates
            else:
                result = normalize(values)
            for core in range(out.shape[0]):
                out[core] = result


def project(place, token, tokens, weight, rate, chosen, heads):
    share = heads
    rows, depth = tokens.shape
    count = len(chosen)
    width = weight.shape[2] // heads
    by_part = [part for part, _ in chosen]
    by_head = [head for _, head in chosen]

    def table(values, i):
        picked = values[0]
        for at, value in enumerate(values[1:], 1):
            picked = jnp.where(i >= at, value, picked)
        return picked

    return ordered(
        functools.partial(project_kernel, chosen),
        (count,),
        [
            pl.BlockSpec((rows, depth), lambda i, place: (0, 0)),
            pl.BlockSpec(
                (None, depth, width),
                lambda i, place: (table(by_part, i), 0, table(by_head, i)),
            ),
            pl.BlockSpec(rate.shape, lambda i, place: (0, 0)),
        ],
        [pl.BlockSpec((share, None, rows, width), lambda i, place: (0, i, 0, 0))],
        [jax.ShapeDtypeStruct((share, count, rows, width), jnp.float32)],
        [],
        "project",
        50 * 2**20,
    )(place, token, tokens, weight, rate)


def widen_kernel(place, weight, out):
    out[...] = weight[...].astype(jnp.float32)


def widen(place, token, weight, ahead, members, share, late):
    rows, columns = weight.shape[0] // share, weight.shape[1] // members
    step = rows // 2

    def chosen(i, place):
        return place[0] * 2 + i, lax.rem(place[3] + ahead, members)

    return ordered(
        widen_kernel,
        (2,),
        [pl.BlockSpec((step, columns), chosen)],
        [pl.BlockSpec((step, columns), lambda i, place: (i, 0))],
        [jax.ShapeDtypeStruct((rows, columns), jnp.float32)],
        [],
        "widen",
        late=len(late),
    )(place, token, weight, *late)


def cut(grads, outs, m, place, role):
    size = outs[0].shape[1]
    odd = lax.rem(place[4], 2)
    for out, piece in zip(
        outs,
        (2 * role + odd, 2 * role + 1 - odd, 2 * (1 - role) + odd, 2 * (1 - role) + 1 - odd),
    ):
        out[m] = grads[pl.ds(pl.multiple_of(piece * size, size), size), :]


def joined(pieces, m, place, role, full):
    size = pieces[0].shape[1]
    odd = lax.rem(place[4], 2)
    for block, piece in zip(
        pieces,
        (2 * role + odd, 2 * role + 1 - odd, 2 * (1 - role) + odd, 2 * (1 - role) + 1 - odd),
    ):
        full[pl.ds(pl.multiple_of(piece * size, size), size), :] = block[m]
    return full[...]


def stepped(place, pieces, sums, weights, start, share, full):
    results = []
    for m in range(3):
        grads = joined(pieces, m, place, place[1], full)
        square = sums[0][m, 0]
        for other in sums[1:]:
            square = square + other[m, 0]
        scale = jnp.full((1, 1), square / (grads.size * share) + epsilon, jnp.float32)
        moved = weights[m].astype(jnp.float32) + grads * (step_size / jnp.sqrt(scale))
        first = start[m].astype(jnp.float32)
        base = jnp.sqrt(jnp.mean(first * first, axis=0, keepdims=True))
        column = jnp.mean(moved * moved, axis=0, keepdims=True)
        results.append(moved * (base / jnp.sqrt(column + epsilon)))
    return results


def sums_kernel(place, *refs):
    pieces, out = refs[:-1], refs[-1]
    row = lax.broadcasted_iota(jnp.int32, out.shape, 0)
    total = jnp.zeros(out.shape, jnp.float32)
    for m in range(3):
        square = sum(jnp.sum(piece[m] * piece[m]) for piece in pieces)
        total = jnp.where(row == m, square, total)
    out[...] = total


def square_sums(place, token, pieces):
    return ordered(
        sums_kernel, (1,), [whole()] * len(pieces), [whole()], [token_shape], [], "square_sums"
    )(place, token, *pieces)


def grad_kernel(share, count, first, place, start, *refs):
    refs = list(refs)
    stepping = count > 0
    if stepping:
        pieces, refs = refs[:4], refs[4:]
        sums, refs = refs[:share], refs[share:]
        if not first:
            old, refs = refs[0], refs[1:]
    sides, refs = refs[0], refs[1:]
    outs, refs = refs[:4], refs[4:]
    if stepping:
        new, refs = refs[0], refs[1:]
    full, key, target, hidden, upward, gateward = refs
    if stepping:
        weights = stepped(place, pieces, sums, start if first else old, start, share, full)
        for m in range(3):
            new[m] = weights[m]
    else:
        weights = [start[m].astype(jnp.float32) for m in range(3)]
    gate_weight, up_weight = (block.astype(jnp.bfloat16) for block in weights[:2])
    down_weight = split(weights[2])
    rows = sides.shape[2]
    chunk = min(rows, 256)
    for core in range(share):
        for begin in range(0, rows, chunk):
            here = pl.ds(core * rows + begin, chunk)
            keys = split(sides[core, 0, begin : begin + chunk, :])
            targets = split(sides[core, 1, begin : begin + chunk, :])
            key[here, :], target[here, :] = keys[0], targets[0]
            gate = dot(keys[0], gate_weight) + dot(keys[1], gate_weight)
            upper = dot(keys[0], up_weight) + dot(keys[1], up_weight)
            back = dot3(targets, down_weight)
            sigma = jax.nn.sigmoid(gate)
            active = gate * sigma
            hidden[0, here, :], hidden[1, here, :] = split(active * upper)
            upward[0, here, :], upward[1, here, :] = split(back * active)
            slope = upper * sigma * (1.0 + gate * (1.0 - sigma))
            gateward[0, here, :], gateward[1, here, :] = split(back * slope)
    for m, left, right in ((2, target, hidden), (1, key, upward), (0, key, gateward)):
        rows_first = left[...]
        full[...] = dot(rows_first, right[0], over_rows) + dot(rows_first, right[1], over_rows)
        cut(full, outs, m, place, 0)


def start_spec(start, head, share):
    _, parts, width, hidden = start.shape
    return pl.BlockSpec(
        (None, parts, width, hidden // share), lambda i, place: (head, 0, 0, place[0])
    )


def fast_grad(place, token, start, head, sides, share, count, step=None, late=()):
    rows = sides.shape[0] * sides.shape[2]
    _, parts, width, hidden = start.shape
    hidden = hidden // share
    piece = jax.ShapeDtypeStruct((parts, width // 4, hidden), jnp.float32)
    out_shape = [piece] * 4
    operands = [sides]
    if step is not None:
        pieces, sums, weights = step
        old = [] if weights is None else [weights]
        operands = list(pieces) + list(sums) + old + operands
        out_shape.append(jax.ShapeDtypeStruct((parts, width, hidden), jnp.float32))
    by_width = pltpu.VMEM((rows, width), jnp.bfloat16)
    by_hidden = pltpu.VMEM((2, rows, hidden), jnp.bfloat16)
    return ordered(
        functools.partial(grad_kernel, share, count, step is not None and step[2] is None),
        (1,),
        [start_spec(start, head, share)] + [whole() for _ in operands],
        [whole() for _ in out_shape],
        out_shape,
        [
            pltpu.VMEM((width, hidden), jnp.float32),
            by_width,
            by_width,
            by_hidden,
            by_hidden,
            by_hidden,
        ],
        "fast_grad",
        late=len(late),
    )(place, token, start, *operands, *late)


def apply_kernel(share, head, place, start, *refs):
    pieces, refs = refs[:4], refs[4:]
    sums, refs = refs[:share], refs[share:]
    old, kept, refs = refs[0], refs[1], refs[2:]
    queries, out, full = refs
    keep = place[2] == 1
    weights = stepped(place, pieces, sums, old, start, share, full)
    weights = [jnp.where(keep, kept[m], weights[m]) for m in range(3)]
    gate_weight, up_weight, down_weight = (split(block) for block in weights)
    rows = queries.shape[2]
    chunk = min(rows, 256)
    for core in range(share):
        for begin in range(0, rows, chunk):
            here = pl.ds(begin, chunk)
            values = split(queries[core, head, here, :])
            gate = dot3(values, gate_weight)
            hidden = split(gate * jax.nn.sigmoid(gate) * dot3(values, up_weight))
            out[core, here, :] = dot3(hidden, down_weight, rows_by_rows)


def fast_apply(place, token, start, head, queries, share, pieces, sums, weights, kept, late):
    operands = list(pieces) + list(sums) + [weights, kept, queries]
    _, _, rows, width = queries.shape
    return ordered(
        functools.partial(apply_kernel, share, head),
        (1,),
        [start_spec(start, head, share)] + [whole() for _ in operands],
        [whole()],
        [jax.ShapeDtypeStruct((share, rows, width), jnp.float32)],
        [pltpu.VMEM(weights.shape[1:], jnp.float32)],
        "fast_apply",
        late=len(late),
    )(place, token, start, *operands, *late)


def finish_kernel(place, *refs):
    parts, out = refs
    total = parts[0]
    for i in range(1, parts.shape[0]):
        total = total + parts[i]
    out[...] = normalize(total)


def finish(place, token, parts):
    return ordered(
        finish_kernel,
        (1,),
        [whole()],
        [whole()],
        [jax.ShapeDtypeStruct(parts.shape[1:], jnp.float32)],
        [],
        "finish",
    )(place, token, parts)


def halve(total, bit, place, outs):
    if bit is None:
        outs[0][...] = total
        return
    size = outs[0].shape[1]
    mine = lax.rem(lax.div(place[4], bit), 2) == 1
    low, high = total[:, :size], total[:, size:]
    outs[0][...] = jnp.where(mine, low, high)
    outs[1][...] = jnp.where(mine, high, low)


def gather_kernel(bit, place, own, line, across, corner, *outs):
    helping = place[1] == 1
    total = jnp.where(helping, across[...], own[...]) + jnp.where(helping, corner[...], line[...])
    halve(total, bit, place, outs)


def add_kernel(bit, place, own, other, *outs):
    halve(own[...] + other[...], bit, place, outs)


def pair_kernel(bit, place, own, other, out):
    size = own.shape[1]
    mine = lax.rem(lax.div(place[4], bit), 2) == 1
    out[:, :size] = jnp.where(mine, other[...], own[...])
    out[:, size:] = jnp.where(mine, own[...], other[...])


def combine(place, token, kernel, operands, bit, late=()):
    parts, size, width = operands[0].shape
    count = 1
    if kernel is pair_kernel:
        size = 2 * size
    elif bit is not None:
        count, size = 2, size // 2
    return ordered(
        functools.partial(kernel, bit),
        (1,),
        [whole() for _ in operands],
        [whole()] * count,
        [jax.ShapeDtypeStruct((parts, size, width), jnp.float32)] * count,
        [],
        "combine",
        late=len(late),
    )(place, token, *operands, *late)


def output_kernel(heads, share, sofar, place, *refs):
    refs, out = list(refs[:-1]), refs[-1]
    total = None
    for head, far in heads:
        block = refs.pop(0)[...].astype(jnp.bfloat16)
        weight = refs.pop(0)[...]
        if far:
            for distance in range(1, share):
                other = refs.pop(0)[...]
                weight = jnp.where(lax.rem(place[0] + share - distance, share) == head, other, weight)
        part = dot(block, weight.astype(jnp.bfloat16))
        total = part if total is None else total + part
    if sofar:
        total = total + refs.pop(0)[...]
    out[...] = total.astype(out.dtype)


def output(place, token, near, distant, columns, share, dtype, sofar=None):
    rows, width = (near + distant)[0][1].shape
    half = columns // 2
    by_half = pl.BlockSpec((rows, half), lambda i, place: (0, i))
    by_rows = pl.BlockSpec((rows, width), lambda i, place: (0, 0))
    operands, in_specs = [], []
    for head, block, weight in near:
        operands += [block, weight]
        spec = pl.BlockSpec((width, half), lambda i, place, head=head: (head, 2 * place[3] + i))
        in_specs += [by_rows, spec]
    for head, block, weights in distant:
        operands += [block] + list(weights)
        in_specs += [by_rows] + [
            pl.BlockSpec((width, half), lambda i, place: (0, i)) for _ in weights
        ]
    if sofar is not None:
        operands.append(sofar)
        in_specs.append(by_half)
    heads = [(head, False) for head, _, _ in near] + [(head, True) for head, _, _ in distant]
    return ordered(
        functools.partial(output_kernel, heads, share, sofar is not None),
        (2,),
        in_specs,
        [by_half],
        [jax.ShapeDtypeStruct((rows, columns), dtype)],
        [],
        "output",
    )(place, token, *operands)


def within_chip(block, share, distance):
    devices = range(lax.axis_size("tok"))
    route = [(t, t // share * share + (t + distance) % share) for t in devices]
    return lax.ppermute(block, "tok", route)


def swapped(blocks, share):
    size = lax.axis_size("tok")
    chips = [[first + core for core in range(share)] for first in range(0, size, share)]
    return lax.all_to_all(blocks, "tok", 0, 0, axis_index_groups=chips, tiled=True)


def flipped(block, share, bit):
    route = [(t, t ^ (bit * share)) for t in range(lax.axis_size("tok"))]
    return lax.ppermute(block, "tok", route)


def crossed(block, share, bit, rows):
    size = lax.axis_size("tok")
    route = []
    for one, two in rows:
        route += [(one * size + t, two * size + (t ^ (bit * share))) for t in range(size)]
    covered = {source for source, _ in route}
    every = range(size * lax.axis_size("block"))
    route += [(device, device) for device in every if device not in covered]
    return lax.ppermute(block, ("block", "tok"), route)


def body(tokens, input_weight, rate_weight, fast_init, output_weight):
    block_count, tok_rows, model_width = tokens.shape
    heads, _, head_dim, _ = fast_init.shape
    share = heads
    members = lax.axis_size("head")
    groups = lax.axis_size("block")
    position = lax.axis_index("block")
    member = lax.axis_index("head")
    core = lax.axis_index("tok") % share
    chip = lax.axis_index("tok") // share
    length = lax.axis_size("tok") // share
    bits = [1 << b for b in range(1, length.bit_length() - 1)]
    flattened = tokens.reshape(tok_rows, model_width)
    weight = jnp.transpose(input_weight, (1, 0, 2))
    rate = jnp.transpose(rate_weight)
    columns = output_weight.shape[1] // members
    every_head = range(heads)

    def exchanged(block):
        return [block] + [within_chip(block, share, distance) for distance in range(1, share)]

    def around(block, ahead):
        return lax.ppermute(block, "head", [(i, (i + ahead) % members) for i in range(members)])

    def place(helper, keep):
        return jnp.stack([core, position == helper, keep, member, chip]).astype(jnp.int32)

    token = jnp.zeros(token_shape.shape, jnp.float32)
    never = position < 0
    here = place(1, never)
    sides = [None] * heads

    kept = [None] * heads
    steps = [None] * heads
    far_weights = []
    parts = [None] * heads

    def start_section(section, head, here, helper, token):
        both = [(section, helper), (helper, section)]
        if section == 0:
            made, token = project(
                here, token, flattened, weight, rate, [(1, head), (2, head)], heads
            )
            sides[head] = swapped(made, share)
            *pieces, token = fast_grad(here, token, fast_init, head, sides[head], share, 0)
            weights = None
        else:
            pieces, weights = steps[head]
            sums, token = square_sums(here, token, pieces)
            *pieces, weights, token = fast_grad(
                here, token, fast_init, head, sides[head], share, section,
                (pieces, exchanged(sums), weights),
            )
            kept[head] = (
                weights
                if section == 1
                else jnp.where(position == section - 1, weights, kept[head])
            )
        own, line, across, corner = pieces
        steps[head] = None, weights
        parts[head] = (
            own,
            crossed(line, share, 1, [(section, section)]),
            crossed(across, share, 0, both),
            crossed(corner, share, 1, both),
        )
        return token

    def advance(stage, head, here, both, token, late):
        count = len(bits)
        if stage <= count:
            bit = bits[stage] if stage < count else None
            kernel = add_kernel if stage else gather_kernel
            *outs, token = combine(here, token, kernel, parts[head], bit, late)
            total = outs[-1]
            if bit is not None:
                parts[head] = total, flipped(outs[0], share, bit)
                return token
        else:
            bit = bits[2 * count - stage]
            total, token = combine(here, token, pair_kernel, parts[head], bit, late)
        if stage < 2 * count:
            parts[head] = total, flipped(total, share, bits[2 * count - stage - 1])
        else:
            pieces = (
                total,
                flipped(total, share, 1),
                crossed(total, share, 0, both),
                crossed(total, share, 1, both),
            )
            steps[head] = pieces, steps[head][1]
        return token

    near, distant = [], [[] for _ in range(1, members)]
    for section in range(groups):
        last = section + 1 == groups
        helper = section - 1 if last else section + 1
        both = [(section, helper), (helper, section)]
        previous, here = here, place(helper, never)
        for head in every_head:
            token = start_section(section, head, previous, helper, token)
            if section == 0 and head == 0:
                for ahead in range(1, members):
                    wide, token = widen(here, token, output_weight, ahead, members, share, ())
                    far_weights.append(exchanged(around(wide, ahead)))
        stages = 2 * len(bits) + 1
        for turn in range(stages + heads - 1):
            for head in every_head:
                stage = turn - head
                if 0 <= stage < stages:
                    late = []
                    if section == 1 and head == heads - 1 and stage == 0:
                        late = [blocks[0] for blocks in far_weights]
                    if section == 0 and head == 0 and stage == 1:
                        late = [queries]
                    token = advance(stage, head, here, both, token, late)
                    if section == 0 and head == 0 and stage == 0:
                        chosen_parts = [(0, other) for other in every_head]
                        made, token = project(
                            here, token, flattened, weight, rate, chosen_parts, heads
                        )
                        queries = swapped(made, share)

    here = place(helper, position != groups - 1)
    for head in every_head:
        pieces, weights = steps[head]
        sums, token = square_sums(here, token, pieces)
        *made, token = fast_apply(
            here, token, fast_init, head, queries, share,
            pieces, exchanged(sums), weights, kept[head],
            (),
        )
        whole_block, token = finish(here, token, swapped(made[0], share))
        near.append(whole_block)
        for ahead in range(1, members):
            distant[ahead - 1].append(around(whole_block, ahead))
    pairs = [(head, near[head], output_weight) for head in every_head]
    others = [
        (head, distant[ahead][head], far_weights[ahead])
        for head in every_head
        for ahead in range(members - 1)
    ]
    first, final = others[: 1 - members], others[1 - members :]
    if members == 1:
        mixed, token = output(here, token, pairs, [], columns, share, jnp.bfloat16)
    else:
        mixed, token = output(here, token, pairs, first, columns, share, jnp.float32)
        mixed, token = output(here, token, [], final, columns, share, jnp.bfloat16, mixed)
    return mixed.reshape(block_count, tok_rows, -1)


def solution(mesh):
    placed = (
        P("block", "tok", None),
        P(None, None, "head"),
        P(None, "head"),
        P("head", None, None, None),
        P("head", None),
    )
    return jax.shard_map(
        body, mesh=mesh, in_specs=placed, out_specs=P("block", "tok", "head"), check_vma=False
    )
```

```python
import functools

import jax
import jax.numpy as jnp
from jax import lax
from jax.experimental import pallas as pl
from jax.experimental.pallas import tpu as pltpu
from jax.sharding import PartitionSpec as P

epsilon = 1e-06
step_size = 0.03
vmem_bytes = 14 * 2**20
rows_by_rows = (((1,), (1,)), ((), ()))
over_rows = (((0,), (0,)), ((), ()))
plain = (((1,), (0,)), ((), ()))


def params(limit=vmem_bytes):
    return pltpu.CompilerParams(vmem_limit_bytes=limit)


def dot(left, right, dims=plain):
    return lax.dot_general(left, right, dims, preferred_element_type=jnp.float32)


def split(values):
    high = values.astype(jnp.bfloat16)
    return high, (values - high.astype(jnp.float32)).astype(jnp.bfloat16)


def dot3(left, right, dims=plain):
    return dot(left[0], right[0], dims) + (dot(left[0], right[1], dims) + dot(left[1], right[0], dims))


def normalize(values):
    return values / jnp.sqrt(jnp.mean(values * values, axis=-1, keepdims=True) + epsilon)


token_shape = jax.ShapeDtypeStruct((8, 128), jnp.float32)
unread = pl.BlockSpec(memory_space=pl.ANY)


def whole():
    return pl.BlockSpec(memory_space=pltpu.VMEM)


hiding = {"project": 40 * 10**9, "output": 2 * 10**9}


def ordered(kernel, grid, in_specs, out_specs, out_shape, scratch, name, limit=vmem_bytes, late=0):
    def traced(place, token, *refs):
        outs = len(out_shape)
        inputs = len(in_specs)
        refs = refs[:inputs] + refs[inputs + late :]
        refs[inputs + outs][...] = jnp.zeros(token_shape.shape, jnp.float32)
        kernel(place, *refs[: inputs + outs], *refs[inputs + outs + 1 :])

    return pl.pallas_call(
        traced,
        grid_spec=pltpu.PrefetchScalarGridSpec(
            num_scalar_prefetch=1,
            grid=grid,
            in_specs=[unread] + in_specs + [unread] * late,
            out_specs=list(out_specs)
            + [pl.BlockSpec(token_shape.shape, lambda i, place: (0, 0))],
            scratch_shapes=scratch,
        ),
        out_shape=list(out_shape) + [token_shape],
        compiler_params=params(limit),
        cost_estimate=pl.CostEstimate(
            flops=hiding.get(name, 0), bytes_accessed=0, transcendentals=0
        ),
        name=name,
    )


def project_kernel(chosen, pairs, place, tokens, weight, rate, *outs):
    values = dot(tokens[...], weight[...])
    for i, (part, head) in enumerate(chosen):

        @pl.when(pl.program_id(0) == i)
        def _():
            if part == 2:
                logits = dot(tokens[...], rate[...], rows_by_rows)
                logit = logits[:, head : head + 1]
                rates = jnp.maximum(logit, 0.0) + jnp.log1p(jnp.exp(-jnp.abs(logit)))
                outs[0][...] = values * rates
            else:
                outs[0 if i < pairs else 1][...] = normalize(values)


def project(place, token, tokens, weight, rate, chosen, heads, pairs):
    rows, depth = tokens.shape
    count = len(chosen)
    width = weight.shape[2] // heads
    by_part = [part for part, _ in chosen]
    by_head = [head for _, head in chosen]

    def table(values, i):
        picked = values[0]
        for at, value in enumerate(values[1:], 1):
            picked = jnp.where(i >= at, value, picked)
        return picked

    sizes = [pairs] + ([count - pairs] if count > pairs else [])
    places = [lambda i: jnp.minimum(i, pairs - 1), lambda i: jnp.maximum(i - pairs, 0)]
    return ordered(
        functools.partial(project_kernel, chosen, pairs),
        (count,),
        [
            pl.BlockSpec((rows, depth), lambda i, place: (0, 0)),
            pl.BlockSpec(
                (None, depth, width),
                lambda i, place: (table(by_part, i), 0, table(by_head, i)),
            ),
            pl.BlockSpec(rate.shape, lambda i, place: (0, 0)),
        ],
        [
            pl.BlockSpec((None, rows, width), lambda i, place, at=at: (at(i), 0, 0))
            for at in places[: len(sizes)]
        ],
        [jax.ShapeDtypeStruct((size, rows, width), jnp.float32) for size in sizes],
        [],
        "project",
        50 * 2**20,
    )(place, token, tokens, weight, rate)


def widen_kernel(place, weight, out):
    out[...] = weight[...].astype(jnp.float32)


def widen(place, token, weight, ahead, members, share):
    rows, columns = weight.shape[0] // share, weight.shape[1] // members
    step = rows // 2

    def chosen(i, place):
        return place[0] * 2 + i, lax.rem(place[3] + ahead, members)

    return ordered(
        widen_kernel,
        (2,),
        [pl.BlockSpec((step, columns), chosen)],
        [pl.BlockSpec((step, columns), lambda i, place: (i, 0))],
        [jax.ShapeDtypeStruct((rows, columns), jnp.float32)],
        [],
        "widen",
    )(place, token, weight)


def cut(grads, outs, m, place, role):
    size = outs[0].shape[1]
    odd = lax.rem(place[4], 2)
    for out, piece in zip(
        outs,
        (2 * role + odd, 2 * role + 1 - odd, 2 * (1 - role) + odd, 2 * (1 - role) + 1 - odd),
    ):
        out[m] = grads[pl.ds(pl.multiple_of(piece * size, size), size), :]


def joined(pieces, m, place, role, full):
    size = pieces[0].shape[1]
    odd = lax.rem(place[4], 2)
    for block, piece in zip(
        pieces,
        (2 * role + odd, 2 * role + 1 - odd, 2 * (1 - role) + odd, 2 * (1 - role) + 1 - odd),
    ):
        full[pl.ds(pl.multiple_of(piece * size, size), size), :] = block[m]
    return full[...]


def stepped(place, pieces, sums, weights, start, share, full):
    results = []
    for m in range(3):
        grads = joined(pieces, m, place, place[1], full)
        square = sums[0][m, 0]
        for other in sums[1:]:
            square = square + other[m, 0]
        scale = jnp.full((1, 1), square / (grads.size * share) + epsilon, jnp.float32)
        moved = weights[m].astype(jnp.float32) + grads * (step_size / jnp.sqrt(scale))
        first = start[m].astype(jnp.float32)
        base = jnp.sqrt(jnp.mean(first * first, axis=0, keepdims=True))
        column = jnp.mean(moved * moved, axis=0, keepdims=True)
        results.append(moved * (base / jnp.sqrt(column + epsilon)))
    return results


def sums_kernel(place, *refs):
    pieces, out = refs[:-1], refs[-1]
    row = lax.broadcasted_iota(jnp.int32, out.shape, 0)
    total = jnp.zeros(out.shape, jnp.float32)
    for m in range(3):
        square = sum(jnp.sum(piece[m] * piece[m]) for piece in pieces)
        total = jnp.where(row == m, square, total)
    out[...] = total


def square_sums(place, token, pieces):
    return ordered(
        sums_kernel, (1,), [whole()] * len(pieces), [whole()], [token_shape], [], "square_sums"
    )(place, token, *pieces)


def grad_kernel(share, count, first, place, start, *refs):
    refs = list(refs)
    stepping = count > 0
    if stepping:
        pieces, refs = refs[:4], refs[4:]
        sums, refs = refs[:share], refs[share:]
        if not first:
            old, refs = refs[0], refs[1:]
    sides, refs = refs[:share], refs[share:]
    outs, refs = refs[:4], refs[4:]
    if stepping:
        new, refs = refs[0], refs[1:]
    full, key, target, hidden, upward, gateward = refs
    if stepping:
        weights = stepped(place, pieces, sums, start if first else old, start, share, full)
        for m in range(3):
            new[m] = weights[m]
    else:
        weights = [start[m].astype(jnp.float32) for m in range(3)]
    gate_weight, up_weight, down_weight = (split(block) for block in weights)
    rows = sides[0].shape[1]
    chunk = min(rows, 256)
    for at, side in enumerate(sides):
        for begin in range(0, rows, chunk):
            here = pl.ds(at * rows + begin, chunk)
            keys = split(side[0, begin : begin + chunk, :])
            targets = split(side[1, begin : begin + chunk, :])
            key[here, :], target[here, :] = keys[0], targets[0]
            gate = dot3(keys, gate_weight)
            upper = dot3(keys, up_weight)
            back = dot3(targets, down_weight)
            sigma = jax.nn.sigmoid(gate)
            active = gate * sigma
            hidden[0, here, :], hidden[1, here, :] = split(active * upper)
            upward[0, here, :], upward[1, here, :] = split(back * active)
            slope = upper * sigma * (1.0 + gate * (1.0 - sigma))
            gateward[0, here, :], gateward[1, here, :] = split(back * slope)
    for m, left, right in ((2, target, hidden), (1, key, upward), (0, key, gateward)):
        rows_first = left[...]
        full[...] = dot(rows_first, right[0], over_rows) + dot(rows_first, right[1], over_rows)
        cut(full, outs, m, place, 0)


def start_spec(start, head, share):
    _, parts, width, hidden = start.shape
    return pl.BlockSpec(
        (None, parts, width, hidden // share), lambda i, place: (head, 0, 0, place[0])
    )


def fast_grad(place, token, start, head, sides, share, count, step=None, late=()):
    rows = sum(side.shape[1] for side in sides)
    _, parts, width, hidden = start.shape
    hidden = hidden // share
    piece = jax.ShapeDtypeStruct((parts, width // 4, hidden), jnp.float32)
    out_shape = [piece] * 4
    operands = list(sides)
    if step is not None:
        pieces, sums, weights = step
        old = [] if weights is None else [weights]
        operands = list(pieces) + list(sums) + old + operands
        out_shape.append(jax.ShapeDtypeStruct((parts, width, hidden), jnp.float32))
    by_width = pltpu.VMEM((rows, width), jnp.bfloat16)
    by_hidden = pltpu.VMEM((2, rows, hidden), jnp.bfloat16)
    return ordered(
        functools.partial(grad_kernel, share, count, step is not None and step[2] is None),
        (1,),
        [start_spec(start, head, share)] + [whole() for _ in operands],
        [whole() for _ in out_shape],
        out_shape,
        [
            pltpu.VMEM((width, hidden), jnp.float32),
            by_width,
            by_width,
            by_hidden,
            by_hidden,
            by_hidden,
        ],
        "fast_grad",
        late=len(late),
    )(place, token, start, *operands, *late)


def apply_kernel(share, head, place, start, *refs):
    pieces, refs = refs[:4], refs[4:]
    sums, refs = refs[:share], refs[share:]
    old, kept, refs = refs[0], refs[1], refs[2:]
    queries, out, full = refs[:share], refs[share], refs[-1]
    keep = place[2] == 1
    weights = stepped(place, pieces, sums, old, start, share, full)
    weights = [jnp.where(keep, kept[m], weights[m]) for m in range(3)]
    gate_weight, up_weight, down_weight = (split(block) for block in weights)
    rows = queries[0].shape[1]
    chunk = min(rows, 256)
    for distance, query in enumerate(queries):
        slot = lax.rem(place[0] + share - distance, share)
        for begin in range(0, rows, chunk):
            here = pl.ds(begin, chunk)
            values = split(query[head, here, :])
            gate = dot3(values, gate_weight)
            hidden = split(gate * jax.nn.sigmoid(gate) * dot3(values, up_weight))
            out[slot, here, :] = dot3(hidden, down_weight, rows_by_rows)


def fast_apply(place, token, start, head, queries, share, pieces, sums, weights, kept, late):
    operands = list(pieces) + list(sums) + [weights, kept] + list(queries)
    _, rows, width = queries[0].shape
    return ordered(
        functools.partial(apply_kernel, share, head),
        (1,),
        [start_spec(start, head, share)] + [whole() for _ in operands],
        [whole()],
        [jax.ShapeDtypeStruct((share, rows, width), jnp.float32)],
        [pltpu.VMEM(weights.shape[1:], jnp.float32)],
        "fast_apply",
        late=len(late),
    )(place, token, start, *operands, *late)


def finish_kernel(place, *refs):
    parts, out = refs
    total = parts[0]
    for i in range(1, parts.shape[0]):
        total = total + parts[i]
    out[...] = normalize(total)


def finish(place, token, parts):
    return ordered(
        finish_kernel,
        (1,),
        [whole()],
        [whole()],
        [jax.ShapeDtypeStruct(parts.shape[1:], jnp.float32)],
        [],
        "finish",
    )(place, token, parts)


def halve(total, bit, place, outs):
    if bit is None:
        outs[0][...] = total
        return
    size = outs[0].shape[1]
    mine = lax.rem(lax.div(place[4], bit), 2) == 1
    low, high = total[:, :size], total[:, size:]
    outs[0][...] = jnp.where(mine, low, high)
    outs[1][...] = jnp.where(mine, high, low)


def gather_kernel(bit, place, own, line, across, corner, *outs):
    helping = place[1] == 1
    total = jnp.where(helping, across[...], own[...]) + jnp.where(helping, corner[...], line[...])
    halve(total, bit, place, outs)


def add_kernel(bit, place, own, other, *outs):
    halve(own[...] + other[...], bit, place, outs)


def pair_kernel(bit, place, own, other, out):
    size = own.shape[1]
    mine = lax.rem(lax.div(place[4], bit), 2) == 1
    out[:, :size] = jnp.where(mine, other[...], own[...])
    out[:, size:] = jnp.where(mine, own[...], other[...])


def combine(place, token, kernel, operands, bit, late=()):
    parts, size, width = operands[0].shape
    count = 1
    if kernel is pair_kernel:
        size = 2 * size
    elif bit is not None:
        count, size = 2, size // 2
    return ordered(
        functools.partial(kernel, bit),
        (1,),
        [whole() for _ in operands],
        [whole()] * count,
        [jax.ShapeDtypeStruct((parts, size, width), jnp.float32)] * count,
        [],
        "combine",
        late=len(late),
    )(place, token, *operands, *late)


def output_kernel(heads, prepared, share, place, *refs):
    refs = list(refs)
    out = refs.pop(-2 if prepared is not None else -1)
    total = None

    def chosen(head):
        weight = refs.pop(0)[...]
        for distance in range(1, share):
            other = refs.pop(0)[...]
            weight = jnp.where(lax.rem(place[0] + share - distance, share) == head, other, weight)
        return weight.astype(jnp.bfloat16)

    for head, far in heads:
        block = refs.pop(0)[...].astype(jnp.bfloat16)
        part = dot(block, chosen(head) if far else refs.pop(0)[...])
        total = part if total is None else total + part
    out[...] = total
    if prepared is not None:
        refs[-1][...] = chosen(prepared)


def output(place, token, near, distant, prepared, columns, share):
    rows, width = near[0][1].shape
    half = columns // 2
    by_half = pl.BlockSpec((rows, half), lambda i, place: (0, i))
    by_rows = pl.BlockSpec((rows, width), lambda i, place: (0, 0))
    weight_half = pl.BlockSpec((width, half), lambda i, place: (0, i))
    operands, in_specs = [], []
    for head, block, weight in near:
        operands += [block, weight]
        spec = pl.BlockSpec((width, half), lambda i, place, head=head: (head, 2 * place[3] + i))
        in_specs += [by_rows, spec]
    for head, block, weights in distant:
        operands += [block] + list(weights)
        in_specs += [by_rows] + [weight_half for _ in weights]
    out_specs, out_shape = [by_half], [jax.ShapeDtypeStruct((rows, columns), jnp.float32)]
    ready = None
    if prepared is not None:
        ready, weights = prepared
        operands += list(weights)
        in_specs += [weight_half for _ in weights]
        out_specs.append(weight_half)
        out_shape.append(jax.ShapeDtypeStruct((width, columns), jnp.bfloat16))
    heads = [(head, False) for head, _, _ in near] + [(head, True) for head, _, _ in distant]
    return ordered(
        functools.partial(output_kernel, heads, ready, share),
        (2,),
        in_specs,
        out_specs,
        out_shape,
        [],
        "output",
    )(place, token, *operands)


def last_kernel(place, sofar, block, weight, out):
    total = sofar[...] + dot(block[...].astype(jnp.bfloat16), weight[...])
    out[...] = total.astype(out.dtype)


def add_last(place, token, sofar, block, weight):
    return ordered(
        last_kernel,
        (1,),
        [whole()] * 3,
        [whole()],
        [jax.ShapeDtypeStruct(sofar.shape, jnp.bfloat16)],
        [],
        "add_last",
    )(place, token, sofar, block, weight)


def within_chip(block, share, distance):
    devices = range(lax.axis_size("tok"))
    route = [(t, t // share * share + (t + distance) % share) for t in devices]
    return lax.ppermute(block, "tok", route)


def swapped(blocks, share):
    size = lax.axis_size("tok")
    chips = [[first + core for core in range(share)] for first in range(0, size, share)]
    return lax.all_to_all(blocks, "tok", 0, 0, axis_index_groups=chips, tiled=True)


def flipped(block, share, bit):
    route = [(t, t ^ (bit * share)) for t in range(lax.axis_size("tok"))]
    return lax.ppermute(block, "tok", route)


def crossed(block, share, bit, one, two, both):
    size = lax.axis_size("tok")
    route = [(one * size + t, two * size + (t ^ (bit * share))) for t in range(size)]
    if one != two:
        back = bit * share if both else 0
        route += [(two * size + t, one * size + (t ^ back)) for t in range(size)]
    covered = {source for source, _ in route}
    every = range(size * lax.axis_size("block"))
    route += [(device, device) for device in every if device not in covered]
    return lax.ppermute(block, ("block", "tok"), route)


def body(tokens, input_weight, rate_weight, fast_init, output_weight):
    block_count, tok_rows, model_width = tokens.shape
    heads, _, head_dim, _ = fast_init.shape
    share = heads
    members = lax.axis_size("head")
    groups = lax.axis_size("block")
    position = lax.axis_index("block")
    member = lax.axis_index("head")
    core = lax.axis_index("tok") % share
    chip = lax.axis_index("tok") // share
    length = lax.axis_size("tok") // share
    bits = [1 << b for b in range(1, length.bit_length() - 1)]
    flattened = tokens.reshape(tok_rows, model_width)
    weight = jnp.transpose(input_weight, (1, 0, 2))
    rate = jnp.transpose(rate_weight)
    columns = output_weight.shape[1] // members
    every_head = range(heads)

    def exchanged(block):
        return [block] + [within_chip(block, share, distance) for distance in range(1, share)]

    def around(block, ahead):
        return lax.ppermute(block, "head", [(i, (i + ahead) % members) for i in range(members)])

    def place(helper, keep):
        return jnp.stack([core, position == helper, keep, member, chip]).astype(jnp.int32)

    token = jnp.zeros(token_shape.shape, jnp.float32)
    never = position < 0
    here = place(1, never)
    sides = []
    for head in every_head:
        chosen_parts = [(1, head), (2, head)]
        if head + 1 == heads:
            chosen_parts += [(0, other) for other in every_head]
        *made, token = project(here, token, flattened, weight, rate, chosen_parts, heads, 2)
        sides.append(exchanged(made[0]))
    queries = exchanged(made[1])

    kept = [None] * heads
    steps = [None] * heads
    far_weights = []
    parts = [None] * heads

    def start_section(section, head, here, helper, token):
        if section == 0:
            late = queries if head + 1 == heads else ()
            *pieces, token = fast_grad(
                here, token, fast_init, head, sides[head], share, 0, None, late
            )
            weights = None
        else:
            pieces, weights = steps[head]
            sums, token = square_sums(here, token, pieces)
            *pieces, weights, token = fast_grad(
                here, token, fast_init, head, sides[head], share, section,
                (pieces, exchanged(sums), weights),
            )
            kept[head] = (
                weights
                if section == 1
                else jnp.where(position == section - 1, weights, kept[head])
            )
        own, line, across, corner = pieces
        steps[head] = None, weights
        parts[head] = (
            own,
            crossed(line, share, 1, section, section, False),
            crossed(across, share, 0, section, helper, False),
            crossed(corner, share, 1, section, helper, False),
        )
        return token

    def advance(stage, head, here, section, helper, last, token, late):
        count = len(bits)
        if stage <= count:
            bit = bits[stage] if stage < count else None
            kernel = add_kernel if stage else gather_kernel
            *outs, token = combine(here, token, kernel, parts[head], bit, late)
            total = outs[-1]
            if bit is not None:
                parts[head] = total, flipped(outs[0], share, bit)
                return token
        else:
            bit = bits[2 * count - stage]
            total, token = combine(here, token, pair_kernel, parts[head], bit, late)
        if stage < 2 * count:
            parts[head] = total, flipped(total, share, bits[2 * count - stage - 1])
        else:
            pieces = (
                total,
                crossed(total, share, 1, section, section, False)
                if last
                else flipped(total, share, 1),
                crossed(total, share, 0, helper, section, not last),
                crossed(total, share, 1, helper, section, not last),
            )
            steps[head] = pieces, steps[head][1]
        return token

    near, distant = [], [[] for _ in range(1, members)]
    for section in range(groups):
        last = section + 1 == groups
        helper = section - 1 if last else section + 1
        previous, here = here, place(helper, never)
        for head in every_head:
            token = start_section(section, head, previous, helper, token)
        stages = 2 * len(bits) + 1
        for turn in range(stages + heads - 1):
            for head in every_head:
                stage = turn - head
                if 0 <= stage < stages:
                    late = []
                    if section == 1 and head == heads - 1 and stage == 0:
                        late = [blocks[0] for blocks in far_weights]
                    token = advance(stage, head, here, section, helper, last, token, late)
                    if section == 0 and head == 0 and stage == 0:
                        for ahead in range(1, members):
                            wide, token = widen(here, token, output_weight, ahead, members, share)
                            far_weights.append(exchanged(around(wide, ahead)))

    here = place(helper, position != groups - 1)
    for head in every_head:
        pieces, weights = steps[head]
        sums, token = square_sums(here, token, pieces)
        *made, token = fast_apply(
            here, token, fast_init, head, queries, share,
            pieces, exchanged(sums), weights, kept[head],
            (),
        )
        whole_block, token = finish(here, token, swapped(made[0], share))
        near.append(whole_block)
        for ahead in range(1, members):
            distant[ahead - 1].append(around(whole_block, ahead))
    pairs = [(head, near[head], output_weight) for head in every_head]
    others = [
        (head, distant[ahead][head], far_weights[ahead])
        for head in every_head
        for ahead in range(members - 1)
    ]
    if not others:
        mixed, token = output(here, token, pairs, [], None, columns, share)
        mixed = mixed.astype(jnp.bfloat16)
    else:
        head, block, candidates = others[-1]
        mixed, ready, token = output(
            here, token, pairs, others[:-1], (head, candidates), columns, share
        )
        mixed, token = add_last(here, token, mixed, block, ready)
    return mixed.reshape(block_count, tok_rows, -1)


def solution(mesh):
    placed = (
        P("block", "tok", None),
        P(None, None, "head"),
        P(None, "head"),
        P("head", None, None, None),
        P("head", None),
    )
    return jax.shard_map(
        body, mesh=mesh, in_specs=placed, out_specs=P("block", "tok", "head"), check_vma=False
    )
```

```python
import functools

import jax
import jax.numpy as jnp
from jax import lax
from jax.experimental import pallas as pl
from jax.experimental.pallas import tpu as pltpu
from jax.sharding import PartitionSpec as P

epsilon = 1e-06
step_size = 0.03
vmem_bytes = 14 * 2**20
rows_by_rows = (((1,), (1,)), ((), ()))
over_rows = (((0,), (0,)), ((), ()))
plain = (((1,), (0,)), ((), ()))


def params(limit=vmem_bytes):
    return pltpu.CompilerParams(vmem_limit_bytes=limit)


def dot(left, right, dims=plain):
    return lax.dot_general(left, right, dims, preferred_element_type=jnp.float32)


def split(values):
    high = values.astype(jnp.bfloat16)
    return high, (values - high.astype(jnp.float32)).astype(jnp.bfloat16)


def dot3(left, right, dims=plain):
    return dot(left[0], right[0], dims) + (dot(left[0], right[1], dims) + dot(left[1], right[0], dims))


def normalize(values):
    return values / jnp.sqrt(jnp.mean(values * values, axis=-1, keepdims=True) + epsilon)


token_shape = jax.ShapeDtypeStruct((8, 128), jnp.float32)
unread = pl.BlockSpec(memory_space=pl.ANY)


def whole():
    return pl.BlockSpec(memory_space=pltpu.VMEM)


hiding = {
    "project": 40 * 10**9,
    "output": 8 * 10**9,
    "combine": 4 * 10**9,
    "combine_last": 0,
    "fast_apply": 6 * 10**9,
}


def ordered(kernel, grid, in_specs, out_specs, out_shape, scratch, name, limit=vmem_bytes, late=0):
    def traced(place, token, *refs):
        outs = len(out_shape)
        inputs = len(in_specs)
        refs = refs[:inputs] + refs[inputs + late :]
        refs[inputs + outs][...] = jnp.zeros(token_shape.shape, jnp.float32)
        kernel(place, *refs[: inputs + outs], *refs[inputs + outs + 1 :])

    return pl.pallas_call(
        traced,
        grid_spec=pltpu.PrefetchScalarGridSpec(
            num_scalar_prefetch=1,
            grid=grid,
            in_specs=[unread] + in_specs + [unread] * late,
            out_specs=list(out_specs)
            + [pl.BlockSpec(token_shape.shape, lambda i, place: (0, 0))],
            scratch_shapes=scratch,
        ),
        out_shape=list(out_shape) + [token_shape],
        compiler_params=params(limit),
        cost_estimate=pl.CostEstimate(
            flops=hiding.get(name, 0), bytes_accessed=0, transcendentals=0
        ),
        name=name,
    )


def project_kernel(chosen, pairs, place, tokens, weight, rate, *outs):
    values = dot(tokens[...], weight[...])
    for i, (part, head) in enumerate(chosen):

        @pl.when(pl.program_id(0) == i)
        def _():
            if part == 2:
                logits = dot(tokens[...], rate[...], rows_by_rows)
                logit = logits[:, head : head + 1]
                rates = jnp.maximum(logit, 0.0) + jnp.log1p(jnp.exp(-jnp.abs(logit)))
                outs[0][...] = values * rates
            else:
                outs[0 if i < pairs else 1][...] = normalize(values)


def project(place, token, tokens, weight, rate, chosen, heads, pairs):
    rows, depth = tokens.shape
    count = len(chosen)
    width = weight.shape[2] // heads
    by_part = [part for part, _ in chosen]
    by_head = [head for _, head in chosen]

    def table(values, i):
        picked = values[0]
        for at, value in enumerate(values[1:], 1):
            picked = jnp.where(i >= at, value, picked)
        return picked

    sizes = [pairs] + ([count - pairs] if count > pairs else [])
    places = [lambda i: jnp.minimum(i, pairs - 1), lambda i: jnp.maximum(i - pairs, 0)]
    return ordered(
        functools.partial(project_kernel, chosen, pairs),
        (count,),
        [
            pl.BlockSpec((rows, depth), lambda i, place: (0, 0)),
            pl.BlockSpec(
                (None, depth, width),
                lambda i, place: (table(by_part, i), 0, table(by_head, i)),
            ),
            pl.BlockSpec(rate.shape, lambda i, place: (0, 0)),
        ],
        [
            pl.BlockSpec((None, rows, width), lambda i, place, at=at: (at(i), 0, 0))
            for at in places[: len(sizes)]
        ],
        [jax.ShapeDtypeStruct((size, rows, width), jnp.float32) for size in sizes],
        [],
        "project",
        50 * 2**20,
    )(place, token, tokens, weight, rate)


def widen_kernel(place, weight, out):
    out[...] = weight[...].astype(jnp.float32)


def widen(place, token, weight, ahead, members, share):
    rows, columns = weight.shape[0] // share, weight.shape[1] // members
    step = rows // 2

    def chosen(i, place):
        return place[0] * 2 + i, lax.rem(place[3] + ahead, members)

    return ordered(
        widen_kernel,
        (2,),
        [pl.BlockSpec((step, columns), chosen)],
        [pl.BlockSpec((step, columns), lambda i, place: (i, 0))],
        [jax.ShapeDtypeStruct((rows, columns), jnp.float32)],
        [],
        "widen",
    )(place, token, weight)


def piece_rows(place, role, size):
    odd = lax.rem(place[4], 2)
    for piece in (2 * role + odd, 2 * role + 1 - odd, 2 * (1 - role) + odd, 2 * (1 - role) + 1 - odd):
        yield pl.ds(pl.multiple_of(piece * size, size), size)


def cut(grads, outs, m, place):
    own, line, other = outs
    size = own.shape[1]
    first, second, third, fourth = piece_rows(place, 0, size)
    own[m] = grads[first, :]
    line[m] = grads[second, :]
    other[m, :size, :] = grads[third, :]
    other[m, size:, :] = grads[fourth, :]


def joined(pairs, m, place, full):
    size = pairs[0].shape[1] // 2
    rows = piece_rows(place, place[1], size)
    for pair in pairs:
        full[next(rows), :] = pair[m, :size, :]
        full[next(rows), :] = pair[m, size:, :]
    return full[...]


def stepped(place, pieces, sums, weights, start, share, full):
    results = []
    for m in range(3):
        grads = joined(pieces, m, place, full)
        square = sums[0][m, 0]
        for other in sums[1:]:
            square = square + other[m, 0]
        scale = jnp.full((1, 1), square / (grads.size * share) + epsilon, jnp.float32)
        moved = weights[m].astype(jnp.float32) + grads * (step_size / jnp.sqrt(scale))
        first = start[m].astype(jnp.float32)
        base = jnp.sqrt(jnp.mean(first * first, axis=0, keepdims=True))
        column = jnp.mean(moved * moved, axis=0, keepdims=True)
        results.append(moved * (base / jnp.sqrt(column + epsilon)))
    return results


def sums_kernel(place, *refs):
    pieces, out = refs[:-1], refs[-1]
    row = lax.broadcasted_iota(jnp.int32, out.shape, 0)
    total = jnp.zeros(out.shape, jnp.float32)
    for m in range(3):
        square = sum(jnp.sum(piece[m] * piece[m]) for piece in pieces)
        total = jnp.where(row == m, square, total)
    out[...] = total


def square_sums(place, token, pieces):
    return ordered(
        sums_kernel, (1,), [whole()] * len(pieces), [whole()], [token_shape], [], "square_sums"
    )(place, token, *pieces)


def grad_kernel(share, count, first, place, start, *refs):
    refs = list(refs)
    stepping = count > 0
    if stepping:
        pieces, refs = refs[:2], refs[2:]
        sums, refs = refs[:share], refs[share:]
        if not first:
            old, refs = refs[0], refs[1:]
    sides, refs = refs[:share], refs[share:]
    outs, refs = refs[:3], refs[3:]
    if stepping:
        new, refs = refs[0], refs[1:]
    full, key, target, hidden, upward, gateward = refs
    if stepping:
        weights = stepped(place, pieces, sums, start if first else old, start, share, full)
        for m in range(3):
            new[m] = weights[m]
    else:
        weights = [start[m].astype(jnp.float32) for m in range(3)]
    gate_weight, up_weight, down_weight = (split(block) for block in weights)
    rows = sides[0].shape[1]
    chunk = min(rows, 256)
    for at, side in enumerate(sides):
        for begin in range(0, rows, chunk):
            here = pl.ds(at * rows + begin, chunk)
            keys = split(side[0, begin : begin + chunk, :])
            targets = split(side[1, begin : begin + chunk, :])
            key[here, :], target[here, :] = keys[0], targets[0]
            gate = dot3(keys, gate_weight)
            upper = dot3(keys, up_weight)
            back = dot3(targets, down_weight)
            sigma = jax.nn.sigmoid(gate)
            active = gate * sigma
            hidden[0, here, :], hidden[1, here, :] = split(active * upper)
            upward[0, here, :], upward[1, here, :] = split(back * active)
            slope = upper * sigma * (1.0 + gate * (1.0 - sigma))
            gateward[0, here, :], gateward[1, here, :] = split(back * slope)
    for m, left, right in ((2, target, hidden), (1, key, upward), (0, key, gateward)):
        rows_first = left[...]
        full[...] = dot(rows_first, right[0], over_rows) + dot(rows_first, right[1], over_rows)
        cut(full, outs, m, place)


def start_spec(start, head, share):
    _, parts, width, hidden = start.shape
    return pl.BlockSpec(
        (None, parts, width, hidden // share), lambda i, place: (head, 0, 0, place[0])
    )


def fast_grad(place, token, start, head, sides, share, count, step=None, late=()):
    rows = sum(side.shape[1] for side in sides)
    _, parts, width, hidden = start.shape
    hidden = hidden // share
    piece = jax.ShapeDtypeStruct((parts, width // 4, hidden), jnp.float32)
    pair = jax.ShapeDtypeStruct((parts, width // 2, hidden), jnp.float32)
    out_shape = [piece, piece, pair]
    operands = list(sides)
    if step is not None:
        pieces, sums, weights = step
        old = [] if weights is None else [weights]
        operands = list(pieces) + list(sums) + old + operands
        out_shape.append(jax.ShapeDtypeStruct((parts, width, hidden), jnp.float32))
    by_width = pltpu.VMEM((rows, width), jnp.bfloat16)
    by_hidden = pltpu.VMEM((2, rows, hidden), jnp.bfloat16)
    return ordered(
        functools.partial(grad_kernel, share, count, step is not None and step[2] is None),
        (1,),
        [start_spec(start, head, share)] + [whole() for _ in operands],
        [whole() for _ in out_shape],
        out_shape,
        [
            pltpu.VMEM((width, hidden), jnp.float32),
            by_width,
            by_width,
            by_hidden,
            by_hidden,
            by_hidden,
        ],
        "fast_grad",
        late=len(late),
    )(place, token, start, *operands, *late)


def apply_kernel(share, head, place, start, *refs):
    pieces, refs = refs[:2], refs[2:]
    sums, refs = refs[:share], refs[share:]
    old, kept, refs = refs[0], refs[1], refs[2:]
    queries, out, full = refs[:share], refs[share], refs[-1]
    keep = place[2] == 1
    weights = stepped(place, pieces, sums, old, start, share, full)
    weights = [jnp.where(keep, kept[m], weights[m]) for m in range(3)]
    gate_weight, up_weight, down_weight = (split(block) for block in weights)
    rows = queries[0].shape[1]
    chunk = min(rows, 256)
    for distance, query in enumerate(queries):
        slot = lax.rem(place[0] + share - distance, share)
        for begin in range(0, rows, chunk):
            here = pl.ds(begin, chunk)
            values = split(query[head, here, :])
            gate = dot3(values, gate_weight)
            hidden = split(gate * jax.nn.sigmoid(gate) * dot3(values, up_weight))
            out[slot, here, :] = dot3(hidden, down_weight, rows_by_rows)


def fast_apply(place, token, start, head, queries, share, pieces, sums, weights, kept, late):
    operands = list(pieces) + list(sums) + [weights, kept] + list(queries)
    _, rows, width = queries[0].shape
    return ordered(
        functools.partial(apply_kernel, share, head),
        (1,),
        [start_spec(start, head, share)] + [whole() for _ in operands],
        [whole()],
        [jax.ShapeDtypeStruct((share, rows, width), jnp.float32)],
        [pltpu.VMEM(weights.shape[1:], jnp.float32)],
        "fast_apply",
        late=len(late),
    )(place, token, start, *operands, *late)


def finish_kernel(place, *refs):
    parts, out = refs
    total = parts[0]
    for i in range(1, parts.shape[0]):
        total = total + parts[i]
    out[...] = normalize(total)


def finish(place, token, parts):
    return ordered(
        finish_kernel,
        (1,),
        [whole()],
        [whole()],
        [jax.ShapeDtypeStruct(parts.shape[1:], jnp.float32)],
        [],
        "finish",
    )(place, token, parts)


def halve(total, bit, place, outs):
    if bit is None:
        outs[0][...] = total
        return
    size = outs[0].shape[1]
    mine = lax.rem(lax.div(place[4], bit), 2) == 1
    low, high = total[:, :size], total[:, size:]
    outs[0][...] = jnp.where(mine, low, high)
    outs[1][...] = jnp.where(mine, high, low)


def gather_kernel(bit, place, own, line, other, send, keep):
    helping = place[1] == 1
    size = own.shape[1]
    send[...] = jnp.where(helping, other[:, size:], line[...])
    keep[...] = jnp.where(helping, other[:, :size], own[...])


def add_kernel(bit, place, own, other, *outs):
    halve(own[...] + other[...], bit, place, outs)


def pair_kernel(bit, place, own, other, out):
    size = own.shape[1]
    if bit is None:
        out[:, :size] = own[...]
        out[:, size:] = other[...]
        return
    mine = lax.rem(lax.div(place[4], bit), 2) == 1
    out[:, :size] = jnp.where(mine, other[...], own[...])
    out[:, size:] = jnp.where(mine, own[...], other[...])


def combine(place, token, kernel, operands, bit, late=(), name="combine"):
    parts, size, width = operands[0].shape
    count = 1
    if kernel is pair_kernel:
        size = 2 * size
    elif kernel is gather_kernel:
        count = 2
    elif bit is not None:
        count, size = 2, size // 2
    return ordered(
        functools.partial(kernel, bit),
        (1,),
        [whole() for _ in operands],
        [whole()] * count,
        [jax.ShapeDtypeStruct((parts, size, width), jnp.float32)] * count,
        [],
        name,
        late=len(late),
    )(place, token, *operands, *late)


def output_kernel(heads, prepared, share, place, *refs):
    refs = list(refs)
    out = refs.pop(-2 if prepared is not None else -1)
    total = None

    def chosen(head):
        weight = refs.pop(0)[...]
        for distance in range(1, share):
            other = refs.pop(0)[...]
            weight = jnp.where(lax.rem(place[0] + share - distance, share) == head, other, weight)
        return weight.astype(jnp.bfloat16)

    for head, far in heads:
        block = refs.pop(0)[...].astype(jnp.bfloat16)
        part = dot(block, chosen(head) if far else refs.pop(0)[...])
        total = part if total is None else total + part
    out[...] = total
    if prepared is not None:
        refs[-1][...] = chosen(prepared)


def output(place, token, near, distant, prepared, columns, share):
    rows, width = near[0][1].shape
    half = columns // 2
    by_half = pl.BlockSpec((rows, half), lambda i, place: (0, i))
    by_rows = pl.BlockSpec((rows, width), lambda i, place: (0, 0))
    weight_half = pl.BlockSpec((width, half), lambda i, place: (0, i))
    operands, in_specs = [], []
    for head, block, weight in near:
        operands += [block, weight]
        spec = pl.BlockSpec((width, half), lambda i, place, head=head: (head, 2 * place[3] + i))
        in_specs += [by_rows, spec]
    for head, block, weights in distant:
        operands += [block] + list(weights)
        in_specs += [by_rows] + [weight_half for _ in weights]
    out_specs, out_shape = [by_half], [jax.ShapeDtypeStruct((rows, columns), jnp.float32)]
    ready = None
    if prepared is not None:
        ready, weights = prepared
        operands += list(weights)
        in_specs += [weight_half for _ in weights]
        out_specs.append(weight_half)
        out_shape.append(jax.ShapeDtypeStruct((width, columns), jnp.bfloat16))
    heads = [(head, False) for head, _, _ in near] + [(head, True) for head, _, _ in distant]
    return ordered(
        functools.partial(output_kernel, heads, ready, share),
        (2,),
        in_specs,
        out_specs,
        out_shape,
        [],
        "output",
    )(place, token, *operands)


def last_kernel(place, sofar, block, weight, out):
    total = sofar[...] + dot(block[...].astype(jnp.bfloat16), weight[...])
    out[...] = total.astype(out.dtype)


def add_last(place, token, sofar, block, weight):
    return ordered(
        last_kernel,
        (1,),
        [whole()] * 3,
        [whole()],
        [jax.ShapeDtypeStruct(sofar.shape, jnp.bfloat16)],
        [],
        "add_last",
    )(place, token, sofar, block, weight)


def within_chip(block, share, distance):
    devices = range(lax.axis_size("tok"))
    route = [(t, t // share * share + (t + distance) % share) for t in devices]
    return lax.ppermute(block, "tok", route)


def swapped(blocks, share):
    size = lax.axis_size("tok")
    chips = [[first + core for core in range(share)] for first in range(0, size, share)]
    return lax.all_to_all(blocks, "tok", 0, 0, axis_index_groups=chips, tiled=True)


def flipped(block, share, bit):
    route = [(t, t ^ (bit * share)) for t in range(lax.axis_size("tok"))]
    return lax.ppermute(block, "tok", route)


def crossed(block, one, two, both):
    size = lax.axis_size("tok")
    route = [(one * size + t, two * size + t) for t in range(size)]
    if both:
        route += [(two * size + t, one * size + t) for t in range(size)]
    covered = {device for pair in route for device in pair}
    every = range(size * lax.axis_size("block"))
    route += [(device, device) for device in every if device not in covered]
    return lax.ppermute(block, ("block", "tok"), route)


def body(tokens, input_weight, rate_weight, fast_init, output_weight):
    block_count, tok_rows, model_width = tokens.shape
    heads, _, head_dim, _ = fast_init.shape
    share = heads
    members = lax.axis_size("head")
    groups = lax.axis_size("block")
    position = lax.axis_index("block")
    member = lax.axis_index("head")
    core = lax.axis_index("tok") % share
    chip = lax.axis_index("tok") // share
    length = lax.axis_size("tok") // share
    bits = [1 << b for b in range(1, length.bit_length() - 1)]
    flattened = tokens.reshape(tok_rows, model_width)
    weight = jnp.transpose(input_weight, (1, 0, 2))
    rate = jnp.transpose(rate_weight)
    columns = output_weight.shape[1] // members
    every_head = range(heads)

    def exchanged(block):
        return [block] + [within_chip(block, share, distance) for distance in range(1, share)]

    def around(block, ahead):
        return lax.ppermute(block, "head", [(i, (i + ahead) % members) for i in range(members)])

    def place(helper, keep):
        return jnp.stack([core, position == helper, keep, member, chip]).astype(jnp.int32)

    token = jnp.zeros(token_shape.shape, jnp.float32)
    never = position < 0
    here = place(1, never)
    sides = []
    for head in every_head:
        chosen_parts = [(1, head), (2, head)]
        if head + 1 == heads:
            chosen_parts += [(0, other) for other in every_head]
        *made, token = project(here, token, flattened, weight, rate, chosen_parts, heads, 2)
        sides.append(exchanged(made[0]))
    queries = exchanged(made[1])

    kept = [None] * heads
    steps = [None] * heads
    far_weights = []
    parts = [None] * heads

    def start_section(section, head, here, helper, token):
        if section == 0:
            late = queries if head + 1 == heads else ()
            *pieces, token = fast_grad(
                here, token, fast_init, head, sides[head], share, 0, None, late
            )
            weights = None
        else:
            pieces, weights = steps[head]
            sums, token = square_sums(here, token, pieces)
            *pieces, weights, token = fast_grad(
                here, token, fast_init, head, sides[head], share, section,
                (pieces, exchanged(sums), weights),
            )
            kept[head] = (
                weights
                if section == 1
                else jnp.where(position == section - 1, weights, kept[head])
            )
        own, line, other = pieces
        steps[head] = None, weights
        parts[head] = own, line, crossed(other, section, helper, section == 0)
        return token

    def advance(stage, head, here, section, helper, last, token, late):
        count = len(bits)
        if stage == 0:
            *outs, token = combine(here, token, gather_kernel, parts[head], None, late)
            parts[head] = outs[1], flipped(outs[0], share, 1)
        elif stage <= count + 1:
            bit = bits[stage - 1] if stage <= count else None
            *outs, token = combine(here, token, add_kernel, parts[head], bit, late)
            total = outs[-1]
            if bit is not None:
                parts[head] = total, flipped(outs[0], share, bit)
        else:
            bit = bits[2 * count + 1 - stage] if stage <= 2 * count + 1 else None
            name = "combine_last" if last and bit is None else "combine"
            total, token = combine(here, token, pair_kernel, parts[head], bit, late, name)
        if count < stage <= 2 * count:
            parts[head] = total, flipped(total, share, bits[2 * count - stage])
        elif stage == 2 * count + 1:
            parts[head] = total, flipped(total, share, 1)
        elif stage == 2 * count + 2:
            steps[head] = (total, crossed(total, helper, section, not last)), steps[head][1]
        return token

    near, distant = [], [[] for _ in range(1, members)]
    for section in range(groups):
        last = section + 1 == groups
        helper = section - 1 if last else section + 1
        previous, here = here, place(helper, never)
        for head in every_head:
            token = start_section(section, head, previous, helper, token)
        stages = 2 * len(bits) + 3
        for turn in range(stages + 2 * (heads - 1)):
            for head in reversed(every_head):
                stage = turn - 2 * head
                if 0 <= stage < stages:
                    late = []
                    if section == 1 and head == heads - 1 and stage == 0:
                        late = [blocks[0] for blocks in far_weights]
                    if section == 1 and head == heads - 1 and stage == 2:
                        late = [block for blocks in far_weights for block in blocks]
                    token = advance(stage, head, here, section, helper, last, token, late)
                    if section == 0 and head == 0 and stage == 0:
                        for ahead in range(1, members):
                            wide, token = widen(here, token, output_weight, ahead, members, share)
                            far_weights.append(exchanged(around(wide, ahead)))

    here = place(helper, position != groups - 1)
    for head in every_head:
        pieces, weights = steps[head]
        sums, token = square_sums(here, token, pieces)
        *made, token = fast_apply(
            here, token, fast_init, head, queries, share,
            pieces, exchanged(sums), weights, kept[head],
            (),
        )
        whole_block, token = finish(here, token, swapped(made[0], share))
        near.append(whole_block)
        for ahead in range(1, members):
            distant[ahead - 1].append(around(whole_block, ahead))
    pairs = [(head, near[head], output_weight) for head in every_head]
    others = [
        (head, distant[ahead][head], far_weights[ahead])
        for head in every_head
        for ahead in range(members - 1)
    ]
    if not others:
        mixed, token = output(here, token, pairs, [], None, columns, share)
        mixed = mixed.astype(jnp.bfloat16)
    else:
        head, block, candidates = others[-1]
        mixed, ready, token = output(
            here, token, pairs, others[:-1], (head, candidates), columns, share
        )
        mixed, token = add_last(here, token, mixed, block, ready)
    return mixed.reshape(block_count, tok_rows, -1)


def solution(mesh):
    placed = (
        P("block", "tok", None),
        P(None, None, "head"),
        P(None, "head"),
        P("head", None, None, None),
        P("head", None),
    )
    return jax.shard_map(
        body, mesh=mesh, in_specs=placed, out_specs=P("block", "tok", "head"), check_vma=False
    )
```

```python
import functools

import jax
import jax.numpy as jnp
from jax import lax
from jax.experimental import pallas as pl
from jax.experimental.pallas import tpu as pltpu
from jax.sharding import PartitionSpec as P

epsilon = 1e-06
step_size = 0.03
vmem_bytes = 14 * 2**20
rows_by_rows = (((1,), (1,)), ((), ()))
over_rows = (((0,), (0,)), ((), ()))
plain = (((1,), (0,)), ((), ()))


def params(limit=vmem_bytes):
    return pltpu.CompilerParams(vmem_limit_bytes=limit)


def dot(left, right, dims=plain):
    return lax.dot_general(left, right, dims, preferred_element_type=jnp.float32)


def split(values):
    high = values.astype(jnp.bfloat16)
    return high, (values - high.astype(jnp.float32)).astype(jnp.bfloat16)


def dot3(left, right, dims=plain):
    return dot(left[0], right[0], dims) + (dot(left[0], right[1], dims) + dot(left[1], right[0], dims))


def normalize(values):
    return values / jnp.sqrt(jnp.mean(values * values, axis=-1, keepdims=True) + epsilon)


token_shape = jax.ShapeDtypeStruct((8, 128), jnp.float32)
unread = pl.BlockSpec(memory_space=pl.ANY)


def whole():
    return pl.BlockSpec(memory_space=pltpu.VMEM)


hiding = {"project": 40 * 10**9, "combine": 2 * 10**9, "widen": 8 * 10**9}


def ordered(kernel, grid, in_specs, out_specs, out_shape, scratch, name, limit=vmem_bytes, late=0):
    def traced(place, token, *refs):
        outs = len(out_shape)
        inputs = len(in_specs)
        refs = refs[:inputs] + refs[inputs + late :]
        refs[inputs + outs][...] = jnp.zeros(token_shape.shape, jnp.float32)
        kernel(place, *refs[: inputs + outs], *refs[inputs + outs + 1 :])

    return pl.pallas_call(
        traced,
        grid_spec=pltpu.PrefetchScalarGridSpec(
            num_scalar_prefetch=1,
            grid=grid,
            in_specs=[unread] + in_specs + [unread] * late,
            out_specs=list(out_specs)
            + [pl.BlockSpec(token_shape.shape, lambda i, place: (0, 0))],
            scratch_shapes=scratch,
        ),
        out_shape=list(out_shape) + [token_shape],
        compiler_params=params(limit),
        cost_estimate=pl.CostEstimate(
            flops=hiding.get(name, 0), bytes_accessed=0, transcendentals=0
        ),
        name=name,
    )


def project_kernel(chosen, pairs, place, tokens, weight, rate, *outs):
    values = dot(tokens[...], weight[...])
    for i, (part, head) in enumerate(chosen):

        @pl.when(pl.program_id(0) == i)
        def _():
            if part == 2:
                logits = dot(tokens[...], rate[...], rows_by_rows)
                logit = logits[:, head : head + 1]
                rates = jnp.maximum(logit, 0.0) + jnp.log1p(jnp.exp(-jnp.abs(logit)))
                outs[0][...] = values * rates
            else:
                outs[0 if i < pairs else 1][...] = normalize(values)


def project(place, token, tokens, weight, rate, chosen, heads, pairs):
    rows, depth = tokens.shape
    count = len(chosen)
    width = weight.shape[2] // heads
    by_part = [part for part, _ in chosen]
    by_head = [head for _, head in chosen]

    def table(values, i):
        picked = values[0]
        for at, value in enumerate(values[1:], 1):
            picked = jnp.where(i >= at, value, picked)
        return picked

    sizes = [pairs] + ([count - pairs] if count > pairs else [])
    places = [lambda i: jnp.minimum(i, pairs - 1), lambda i: jnp.maximum(i - pairs, 0)]
    return ordered(
        functools.partial(project_kernel, chosen, pairs),
        (count,),
        [
            pl.BlockSpec((rows, depth), lambda i, place: (0, 0)),
            pl.BlockSpec(
                (None, depth, width),
                lambda i, place: (table(by_part, i), 0, table(by_head, i)),
            ),
            pl.BlockSpec(rate.shape, lambda i, place: (0, 0)),
        ],
        [
            pl.BlockSpec((None, rows, width), lambda i, place, at=at: (at(i), 0, 0))
            for at in places[: len(sizes)]
        ],
        [jax.ShapeDtypeStruct((size, rows, width), jnp.float32) for size in sizes],
        [],
        "project",
        50 * 2**20,
    )(place, token, tokens, weight, rate)


def widen_kernel(place, weight, out):
    out[...] = weight[...].astype(jnp.float32)


def widen(place, token, weight, ahead, members, share):
    rows, columns = weight.shape[0] // share, weight.shape[1] // members
    step = rows // 2

    def chosen(i, place):
        return place[0] * 2 + i, lax.rem(place[3] + ahead, members)

    return ordered(
        widen_kernel,
        (2,),
        [pl.BlockSpec((step, columns), chosen)],
        [pl.BlockSpec((step, columns), lambda i, place: (i, 0))],
        [jax.ShapeDtypeStruct((rows, columns), jnp.float32)],
        [],
        "widen",
    )(place, token, weight)


def piece_rows(place, role, size):
    odd = lax.rem(place[4], 2)
    for piece in (2 * role + odd, 2 * role + 1 - odd, 2 * (1 - role) + odd, 2 * (1 - role) + 1 - odd):
        yield pl.ds(pl.multiple_of(piece * size, size), size)


def cut(grads, outs, m, place):
    own, line, other = outs
    size = own.shape[1]
    first, second, third, fourth = piece_rows(place, 0, size)
    own[m] = grads[first, :]
    line[m] = grads[second, :]
    other[m, :size, :] = grads[third, :]
    other[m, size:, :] = grads[fourth, :]


def joined(pairs, m, place, full):
    size = pairs[0].shape[1] // 2
    rows = piece_rows(place, place[1], size)
    for pair in pairs:
        full[next(rows), :] = pair[m, :size, :]
        full[next(rows), :] = pair[m, size:, :]
    return full[...]


def stepped(place, pieces, sums, weights, start, share, full):
    results = []
    for m in range(3):
        grads = joined(pieces, m, place, full)
        square = sums[0][m, 0]
        for other in sums[1:]:
            square = square + other[m, 0]
        scale = jnp.full((1, 1), square / (grads.size * share) + epsilon, jnp.float32)
        moved = weights[m].astype(jnp.float32) + grads * (step_size / jnp.sqrt(scale))
        first = start[m].astype(jnp.float32)
        base = jnp.sqrt(jnp.mean(first * first, axis=0, keepdims=True))
        column = jnp.mean(moved * moved, axis=0, keepdims=True)
        results.append(moved * (base / jnp.sqrt(column + epsilon)))
    return results


def sums_kernel(place, *refs):
    pieces, out = refs[:-1], refs[-1]
    row = lax.broadcasted_iota(jnp.int32, out.shape, 0)
    total = jnp.zeros(out.shape, jnp.float32)
    for m in range(3):
        square = sum(jnp.sum(piece[m] * piece[m]) for piece in pieces)
        total = jnp.where(row == m, square, total)
    out[...] = total


def square_sums(place, token, pieces):
    return ordered(
        sums_kernel, (1,), [whole()] * len(pieces), [whole()], [token_shape], [], "square_sums"
    )(place, token, *pieces)


def grad_kernel(share, count, first, place, start, *refs):
    refs = list(refs)
    stepping = count > 0
    if stepping:
        pieces, refs = refs[:2], refs[2:]
        sums, refs = refs[:share], refs[share:]
        if not first:
            old, refs = refs[0], refs[1:]
    sides, refs = refs[:share], refs[share:]
    outs, refs = refs[:3], refs[3:]
    if stepping:
        new, refs = refs[0], refs[1:]
    full, key, target, hidden, upward, gateward = refs
    if stepping:
        weights = stepped(place, pieces, sums, start if first else old, start, share, full)
        for m in range(3):
            new[m] = weights[m]
    else:
        weights = [start[m].astype(jnp.float32) for m in range(3)]
    gate_weight, up_weight, down_weight = (split(block) for block in weights)
    rows = sides[0].shape[1]
    chunk = min(rows, 256)
    for at, side in enumerate(sides):
        for begin in range(0, rows, chunk):
            here = pl.ds(at * rows + begin, chunk)
            keys = split(side[0, begin : begin + chunk, :])
            targets = split(side[1, begin : begin + chunk, :])
            key[here, :], target[here, :] = keys[0], targets[0]
            gate = dot3(keys, gate_weight)
            upper = dot3(keys, up_weight)
            back = dot3(targets, down_weight)
            sigma = jax.nn.sigmoid(gate)
            active = gate * sigma
            hidden[0, here, :], hidden[1, here, :] = split(active * upper)
            upward[0, here, :], upward[1, here, :] = split(back * active)
            slope = upper * sigma * (1.0 + gate * (1.0 - sigma))
            gateward[0, here, :], gateward[1, here, :] = split(back * slope)
    for m, left, right in ((2, target, hidden), (1, key, upward), (0, key, gateward)):
        rows_first = left[...]
        full[...] = dot(rows_first, right[0], over_rows) + dot(rows_first, right[1], over_rows)
        cut(full, outs, m, place)


def start_spec(start, head, share):
    _, parts, width, hidden = start.shape
    return pl.BlockSpec(
        (None, parts, width, hidden // share), lambda i, place: (head, 0, 0, place[0])
    )


def fast_grad(place, token, start, head, sides, share, count, step=None, late=()):
    rows = sum(side.shape[1] for side in sides)
    _, parts, width, hidden = start.shape
    hidden = hidden // share
    piece = jax.ShapeDtypeStruct((parts, width // 4, hidden), jnp.float32)
    pair = jax.ShapeDtypeStruct((parts, width // 2, hidden), jnp.float32)
    out_shape = [piece, piece, pair]
    operands = list(sides)
    if step is not None:
        pieces, sums, weights = step
        old = [] if weights is None else [weights]
        operands = list(pieces) + list(sums) + old + operands
        out_shape.append(jax.ShapeDtypeStruct((parts, width, hidden), jnp.float32))
    by_width = pltpu.VMEM((rows, width), jnp.bfloat16)
    by_hidden = pltpu.VMEM((2, rows, hidden), jnp.bfloat16)
    return ordered(
        functools.partial(grad_kernel, share, count, step is not None and step[2] is None),
        (1,),
        [start_spec(start, head, share)] + [whole() for _ in operands],
        [whole() for _ in out_shape],
        out_shape,
        [
            pltpu.VMEM((width, hidden), jnp.float32),
            by_width,
            by_width,
            by_hidden,
            by_hidden,
            by_hidden,
        ],
        "fast_grad",
        late=len(late),
    )(place, token, start, *operands, *late)


def apply_kernel(share, head, place, start, *refs):
    pieces, refs = refs[:2], refs[2:]
    sums, refs = refs[:share], refs[share:]
    old, kept, refs = refs[0], refs[1], refs[2:]
    queries, out, full = refs[:share], refs[share], refs[-1]
    keep = place[2] == 1
    weights = stepped(place, pieces, sums, old, start, share, full)
    weights = [jnp.where(keep, kept[m], weights[m]) for m in range(3)]
    gate_weight, up_weight, down_weight = (split(block) for block in weights)
    rows = queries[0].shape[1]
    chunk = min(rows, 256)
    for distance, query in enumerate(queries):
        slot = lax.rem(place[0] + share - distance, share)
        for begin in range(0, rows, chunk):
            here = pl.ds(begin, chunk)
            values = split(query[head, here, :])
            gate = dot3(values, gate_weight)
            hidden = split(gate * jax.nn.sigmoid(gate) * dot3(values, up_weight))
            out[slot, here, :] = dot3(hidden, down_weight, rows_by_rows)


def fast_apply(place, token, start, head, queries, share, pieces, sums, weights, kept, late):
    operands = list(pieces) + list(sums) + [weights, kept] + list(queries)
    _, rows, width = queries[0].shape
    return ordered(
        functools.partial(apply_kernel, share, head),
        (1,),
        [start_spec(start, head, share)] + [whole() for _ in operands],
        [whole()],
        [jax.ShapeDtypeStruct((share, rows, width), jnp.float32)],
        [pltpu.VMEM(weights.shape[1:], jnp.float32)],
        "fast_apply",
        late=len(late),
    )(place, token, start, *operands, *late)


def finish_kernel(place, *refs):
    parts, out = refs
    total = parts[0]
    for i in range(1, parts.shape[0]):
        total = total + parts[i]
    out[...] = normalize(total)


def finish(place, token, parts):
    return ordered(
        finish_kernel,
        (1,),
        [whole()],
        [whole()],
        [jax.ShapeDtypeStruct(parts.shape[1:], jnp.float32)],
        [],
        "finish",
    )(place, token, parts)


def halve(total, bit, place, outs):
    if bit is None:
        outs[0][...] = total
        return
    size = outs[0].shape[1]
    mine = lax.rem(lax.div(place[4], bit), 2) == 1
    low, high = total[:, :size], total[:, size:]
    outs[0][...] = jnp.where(mine, low, high)
    outs[1][...] = jnp.where(mine, high, low)


def gather_kernel(bit, place, own, line, other, send, keep):
    helping = place[1] == 1
    size = own.shape[1]
    send[...] = jnp.where(helping, other[:, size:], line[...])
    keep[...] = jnp.where(helping, other[:, :size], own[...])


def add_kernel(bit, place, own, other, *outs):
    halve(own[...] + other[...], bit, place, outs)


def pair_kernel(bit, place, own, other, out):
    size = own.shape[1]
    if bit is None:
        out[:, :size] = own[...]
        out[:, size:] = other[...]
        return
    mine = lax.rem(lax.div(place[4], bit), 2) == 1
    out[:, :size] = jnp.where(mine, other[...], own[...])
    out[:, size:] = jnp.where(mine, own[...], other[...])


def combine(place, token, kernel, operands, bit, late=(), name="combine"):
    parts, size, width = operands[0].shape
    count = 1
    if kernel is pair_kernel:
        size = 2 * size
    elif kernel is gather_kernel:
        count = 2
    elif bit is not None:
        count, size = 2, size // 2
    return ordered(
        functools.partial(kernel, bit),
        (1,),
        [whole() for _ in operands],
        [whole()] * count,
        [jax.ShapeDtypeStruct((parts, size, width), jnp.float32)] * count,
        [],
        name,
        late=len(late),
    )(place, token, *operands, *late)


def output_kernel(heads, prepared, share, place, *refs):
    refs = list(refs)
    out = refs.pop(-2 if prepared is not None else -1)
    total = None

    def chosen(head):
        weight = refs.pop(0)[...]
        for distance in range(1, share):
            other = refs.pop(0)[...]
            weight = jnp.where(lax.rem(place[0] + share - distance, share) == head, other, weight)
        return weight.astype(jnp.bfloat16)

    for head, far in heads:
        block = refs.pop(0)[...].astype(jnp.bfloat16)
        part = dot(block, chosen(head) if far else refs.pop(0)[...])
        total = part if total is None else total + part
    out[...] = total
    if prepared is not None:
        refs[-1][...] = chosen(prepared)


def output(place, token, near, distant, prepared, columns, share):
    rows, width = near[0][1].shape
    half = columns // 2
    by_half = pl.BlockSpec((rows, half), lambda i, place: (0, i))
    by_rows = pl.BlockSpec((rows, width), lambda i, place: (0, 0))
    weight_half = pl.BlockSpec((width, half), lambda i, place: (0, i))
    operands, in_specs = [], []
    for head, block, weight in near:
        operands += [block, weight]
        spec = pl.BlockSpec((width, half), lambda i, place, head=head: (head, 2 * place[3] + i))
        in_specs += [by_rows, spec]
    for head, block, weights in distant:
        operands += [block] + list(weights)
        in_specs += [by_rows] + [weight_half for _ in weights]
    out_specs, out_shape = [by_half], [jax.ShapeDtypeStruct((rows, columns), jnp.float32)]
    ready = None
    if prepared is not None:
        ready, weights = prepared
        operands += list(weights)
        in_specs += [weight_half for _ in weights]
        out_specs.append(weight_half)
        out_shape.append(jax.ShapeDtypeStruct((width, columns), jnp.bfloat16))
    heads = [(head, False) for head, _, _ in near] + [(head, True) for head, _, _ in distant]
    return ordered(
        functools.partial(output_kernel, heads, ready, share),
        (2,),
        in_specs,
        out_specs,
        out_shape,
        [],
        "output",
    )(place, token, *operands)


def last_kernel(place, sofar, block, weight, out):
    total = sofar[...] + dot(block[...].astype(jnp.bfloat16), weight[...])
    out[...] = total.astype(out.dtype)


def add_last(place, token, sofar, block, weight):
    return ordered(
        last_kernel,
        (1,),
        [whole()] * 3,
        [whole()],
        [jax.ShapeDtypeStruct(sofar.shape, jnp.bfloat16)],
        [],
        "add_last",
    )(place, token, sofar, block, weight)


def within_chip(block, share, distance):
    devices = range(lax.axis_size("tok"))
    route = [(t, t // share * share + (t + distance) % share) for t in devices]
    return lax.ppermute(block, "tok", route)


def swapped(blocks, share):
    size = lax.axis_size("tok")
    chips = [[first + core for core in range(share)] for first in range(0, size, share)]
    return lax.all_to_all(blocks, "tok", 0, 0, axis_index_groups=chips, tiled=True)


def flipped(block, share, bit):
    route = [(t, t ^ (bit * share)) for t in range(lax.axis_size("tok"))]
    return lax.ppermute(block, "tok", route)


def crossed(block, one, two, both):
    size = lax.axis_size("tok")
    route = [(one * size + t, two * size + t) for t in range(size)]
    if both:
        route += [(two * size + t, one * size + t) for t in range(size)]
    covered = {device for pair in route for device in pair}
    every = range(size * lax.axis_size("block"))
    route += [(device, device) for device in every if device not in covered]
    return lax.ppermute(block, ("block", "tok"), route)


def body(tokens, input_weight, rate_weight, fast_init, output_weight):
    block_count, tok_rows, model_width = tokens.shape
    heads, _, head_dim, _ = fast_init.shape
    share = heads
    members = lax.axis_size("head")
    groups = lax.axis_size("block")
    position = lax.axis_index("block")
    member = lax.axis_index("head")
    core = lax.axis_index("tok") % share
    chip = lax.axis_index("tok") // share
    length = lax.axis_size("tok") // share
    bits = [1 << b for b in range(1, length.bit_length() - 1)]
    flattened = tokens.reshape(tok_rows, model_width)
    weight = jnp.transpose(input_weight, (1, 0, 2))
    rate = jnp.transpose(rate_weight)
    columns = output_weight.shape[1] // members
    every_head = range(heads)

    def exchanged(block):
        return [block] + [within_chip(block, share, distance) for distance in range(1, share)]

    def around(block, ahead):
        return lax.ppermute(block, "head", [(i, (i + ahead) % members) for i in range(members)])

    def place(helper, keep):
        return jnp.stack([core, position == helper, keep, member, chip]).astype(jnp.int32)

    token = jnp.zeros(token_shape.shape, jnp.float32)
    never = position < 0
    sides = [None] * heads
    queries = []

    kept = [None] * heads
    steps = [None] * heads
    far_weights = []
    parts = [None] * heads

    def start_section(section, head, here, helper, token):
        if section == 0:
            late = queries if head + 1 == heads else ()
            *pieces, token = fast_grad(
                here, token, fast_init, head, sides[head], share, 0, None, late
            )
            weights = None
        else:
            pieces, weights = steps[head]
            sums, token = square_sums(here, token, pieces)
            *pieces, weights, token = fast_grad(
                here, token, fast_init, head, sides[head], share, section,
                (pieces, exchanged(sums), weights),
            )
            kept[head] = (
                weights
                if section == 1
                else jnp.where(position == section - 1, weights, kept[head])
            )
        own, line, other = pieces
        steps[head] = None, weights
        parts[head] = own, line, crossed(other, section, helper, section == 0)
        return token

    def advance(stage, head, here, section, helper, last, token, late):
        count = len(bits)
        if stage == 0:
            *outs, token = combine(here, token, gather_kernel, parts[head], None, late)
            parts[head] = outs[1], flipped(outs[0], share, 1)
        elif stage <= count + 1:
            bit = bits[stage - 1] if stage <= count else None
            *outs, token = combine(here, token, add_kernel, parts[head], bit, late)
            total = outs[-1]
            if bit is not None:
                parts[head] = total, flipped(outs[0], share, bit)
        else:
            bit = bits[2 * count + 1 - stage] if stage <= 2 * count + 1 else None
            name = "combine_last" if bit is None else "combine"
            total, token = combine(here, token, pair_kernel, parts[head], bit, late, name)
        if count < stage <= 2 * count:
            parts[head] = total, flipped(total, share, bits[2 * count - stage])
        elif stage == 2 * count + 1:
            parts[head] = total, flipped(total, share, 1)
        elif stage == 2 * count + 2:
            steps[head] = (total, crossed(total, helper, section, not last)), steps[head][1]
        return token

    helpers = [section + 1 if section + 1 < groups else section - 1 for section in range(groups)]
    places = [place(helper, never) for helper in helpers]
    final = place(helpers[-1], position != groups - 1)
    near, distant = [], [[] for _ in range(1, members)]
    applied = [None] * heads
    stages = 2 * len(bits) + 3

    compute, cross, hop = 7.0, 18.0, 10.0
    period = compute + 2 * cross + (stages - 1) * hop
    tasks = []
    for head in every_head:
        begin = head * (period / heads + 3.0)
        tasks.append((begin - compute if head == 0 else head * compute, "project", 0, head, 0))
        for section in range(groups):
            tasks.append((begin, "start", section, head, 0))
            for stage in range(stages):
                when = begin + compute + cross + stage * hop
                tasks.append((when, "stage", section, head, stage))
                if section == 0 and head == 0 and stage == 0:
                    tasks.append((when + 0.1, "widen", 0, 0, 0))
            begin += period
        tasks.append((begin, "apply", 0, head, 0))
        tasks.append((begin + 5.5, "finish", 0, head, 0))

    for _, task, section, head, stage in sorted(tasks):
        last = section + 1 == groups
        helper = helpers[section]
        here = places[section]
        if task == "project":
            chosen_parts = [(1, head), (2, head)]
            if head + 1 == heads:
                chosen_parts += [(0, other) for other in every_head]
            *made, token = project(here, token, flattened, weight, rate, chosen_parts, heads, 2)
            sides[head] = exchanged(made[0])
            if head + 1 == heads:
                queries += exchanged(made[1])
        elif task == "start":
            token = start_section(section, head, places[max(section - 1, 0)], helper, token)
        elif task == "stage":
            late = []
            if section == 1 and head == 0 and stage == 0:
                late = [blocks[0] for blocks in far_weights]
            if section == 1 and head == heads - 1 and stage == 0:
                late = [block for blocks in far_weights for block in blocks]
            token = advance(stage, head, here, section, helper, last, token, late)
        elif task == "widen":
            for ahead in range(1, members):
                wide, token = widen(here, token, output_weight, ahead, members, share)
                far_weights.append(exchanged(around(wide, ahead)))
        elif task == "apply":
            pieces, weights = steps[head]
            sums, token = square_sums(final, token, pieces)
            *made, token = fast_apply(
                final, token, fast_init, head, queries, share,
                pieces, exchanged(sums), weights, kept[head],
                [block for blocks in distant for block in blocks],
            )
            applied[head] = swapped(made[0], share)
        else:
            whole_block, token = finish(final, token, applied[head])
            near.append(whole_block)
            for ahead in range(1, members):
                distant[ahead - 1].append(around(whole_block, ahead))

    here = final
    pairs = [(head, near[head], output_weight) for head in every_head]
    others = [
        (head, distant[ahead][head], far_weights[ahead])
        for head in every_head
        for ahead in range(members - 1)
    ]
    if not others:
        mixed, token = output(here, token, pairs, [], None, columns, share)
        mixed = mixed.astype(jnp.bfloat16)
    else:
        head, block, candidates = others[-1]
        mixed, ready, token = output(
            here, token, pairs, others[:-1], (head, candidates), columns, share
        )
        mixed, token = add_last(here, token, mixed, block, ready)
    return mixed.reshape(block_count, tok_rows, -1)


def solution(mesh):
    placed = (
        P("block", "tok", None),
        P(None, None, "head"),
        P(None, "head"),
        P("head", None, None, None),
        P("head", None),
    )
    return jax.shard_map(
        body, mesh=mesh, in_specs=placed, out_specs=P("block", "tok", "head"), check_vma=False
    )
```

```python
import functools

import jax
import jax.numpy as jnp
from jax import lax
from jax.experimental import pallas as pl
from jax.experimental.pallas import tpu as pltpu
from jax.sharding import PartitionSpec as P

epsilon = 1e-06
step_size = 0.03
vmem_bytes = 14 * 2**20
rows_by_rows = (((1,), (1,)), ((), ()))
over_rows = (((0,), (0,)), ((), ()))
plain = (((1,), (0,)), ((), ()))


def params(limit=vmem_bytes):
    return pltpu.CompilerParams(vmem_limit_bytes=limit)


def dot(left, right, dims=plain):
    return lax.dot_general(left, right, dims, preferred_element_type=jnp.float32)


def split(values):
    high = values.astype(jnp.bfloat16)
    return high, (values - high.astype(jnp.float32)).astype(jnp.bfloat16)


def dot3(left, right, dims=plain):
    return dot(left[0], right[0], dims) + (dot(left[0], right[1], dims) + dot(left[1], right[0], dims))


def normalize(values):
    return values / jnp.sqrt(jnp.mean(values * values, axis=-1, keepdims=True) + epsilon)


token_shape = jax.ShapeDtypeStruct((8, 128), jnp.float32)
unread = pl.BlockSpec(memory_space=pl.ANY)


def whole():
    return pl.BlockSpec(memory_space=pltpu.VMEM)


hiding = {"project": 40 * 10**9, "combine": 2 * 10**9, "widen": 12 * 10**9, "output": 3 * 10**9}


def ordered(kernel, grid, in_specs, out_specs, out_shape, scratch, name, limit=vmem_bytes, late=0):
    def traced(place, token, *refs):
        outs = len(out_shape)
        inputs = len(in_specs)
        refs = refs[:inputs] + refs[inputs + late :]
        refs[inputs + outs][...] = jnp.zeros(token_shape.shape, jnp.float32)
        kernel(place, *refs[: inputs + outs], *refs[inputs + outs + 1 :])

    return pl.pallas_call(
        traced,
        grid_spec=pltpu.PrefetchScalarGridSpec(
            num_scalar_prefetch=1,
            grid=grid,
            in_specs=[unread] + in_specs + [unread] * late,
            out_specs=list(out_specs)
            + [pl.BlockSpec(token_shape.shape, lambda i, place: (0, 0))],
            scratch_shapes=scratch,
        ),
        out_shape=list(out_shape) + [token_shape],
        compiler_params=params(limit),
        cost_estimate=pl.CostEstimate(
            flops=hiding.get(name, 0), bytes_accessed=0, transcendentals=0
        ),
        name=name,
    )


def project_kernel(chosen, pairs, place, tokens, weight, rate, *outs):
    values = dot(tokens[...], weight[...])
    for i, (part, head) in enumerate(chosen):

        @pl.when(pl.program_id(0) == i)
        def _():
            if part == 2:
                logits = dot(tokens[...], rate[...], rows_by_rows)
                logit = logits[:, head : head + 1]
                rates = jnp.maximum(logit, 0.0) + jnp.log1p(jnp.exp(-jnp.abs(logit)))
                outs[0][...] = values * rates
            else:
                outs[0 if i < pairs else 1][...] = normalize(values)


def project(place, token, tokens, weight, rate, chosen, heads, pairs):
    rows, depth = tokens.shape
    count = len(chosen)
    width = weight.shape[2] // heads
    by_part = [part for part, _ in chosen]
    by_head = [head for _, head in chosen]

    def table(values, i):
        picked = values[0]
        for at, value in enumerate(values[1:], 1):
            picked = jnp.where(i >= at, value, picked)
        return picked

    sizes = [pairs] + ([count - pairs] if count > pairs else [])
    places = [lambda i: jnp.minimum(i, pairs - 1), lambda i: jnp.maximum(i - pairs, 0)]
    return ordered(
        functools.partial(project_kernel, chosen, pairs),
        (count,),
        [
            pl.BlockSpec((rows, depth), lambda i, place: (0, 0)),
            pl.BlockSpec(
                (None, depth, width),
                lambda i, place: (table(by_part, i), 0, table(by_head, i)),
            ),
            pl.BlockSpec(rate.shape, lambda i, place: (0, 0)),
        ],
        [
            pl.BlockSpec((None, rows, width), lambda i, place, at=at: (at(i), 0, 0))
            for at in places[: len(sizes)]
        ],
        [jax.ShapeDtypeStruct((size, rows, width), jnp.float32) for size in sizes],
        [],
        "project",
        50 * 2**20,
    )(place, token, tokens, weight, rate)


def widen_kernel(place, weight, out):
    out[...] = weight[...].astype(jnp.float32)


def widen(place, token, weight, ahead, members, share):
    rows, columns = weight.shape[0] // share, weight.shape[1] // members
    step = rows // 2

    def chosen(i, place):
        return place[0] * 2 + i, lax.rem(place[3] + ahead, members)

    return ordered(
        widen_kernel,
        (2,),
        [pl.BlockSpec((step, columns), chosen)],
        [pl.BlockSpec((step, columns), lambda i, place: (i, 0))],
        [jax.ShapeDtypeStruct((rows, columns), jnp.float32)],
        [],
        "widen",
    )(place, token, weight)


def piece_rows(place, role, size):
    odd = lax.rem(place[4], 2)
    for piece in (2 * role + odd, 2 * role + 1 - odd, 2 * (1 - role) + odd, 2 * (1 - role) + 1 - odd):
        yield pl.ds(pl.multiple_of(piece * size, size), size)


def cut(grads, outs, m, place):
    own, line, other = outs
    size = own.shape[1]
    first, second, third, fourth = piece_rows(place, 0, size)
    own[m] = grads[first, :]
    line[m] = grads[second, :]
    other[m, :size, :] = grads[third, :]
    other[m, size:, :] = grads[fourth, :]


def joined(pairs, m, place, full):
    size = pairs[0].shape[1] // 2
    rows = piece_rows(place, place[1], size)
    for pair in pairs:
        full[next(rows), :] = pair[m, :size, :]
        full[next(rows), :] = pair[m, size:, :]
    return full[...]


def stepped(place, pieces, sums, weights, start, share, full):
    results = []
    for m in range(3):
        grads = joined(pieces, m, place, full)
        square = sums[0][m, 0]
        for other in sums[1:]:
            square = square + other[m, 0]
        scale = jnp.full((1, 1), square / (grads.size * share) + epsilon, jnp.float32)
        moved = weights[m].astype(jnp.float32) + grads * (step_size / jnp.sqrt(scale))
        first = start[m].astype(jnp.float32)
        base = jnp.sqrt(jnp.mean(first * first, axis=0, keepdims=True))
        column = jnp.mean(moved * moved, axis=0, keepdims=True)
        results.append(moved * (base / jnp.sqrt(column + epsilon)))
    return results


def sums_kernel(place, *refs):
    pieces, out = refs[:-1], refs[-1]
    row = lax.broadcasted_iota(jnp.int32, out.shape, 0)
    total = jnp.zeros(out.shape, jnp.float32)
    for m in range(3):
        square = sum(jnp.sum(piece[m] * piece[m]) for piece in pieces)
        total = jnp.where(row == m, square, total)
    out[...] = total


def square_sums(place, token, pieces):
    return ordered(
        sums_kernel, (1,), [whole()] * len(pieces), [whole()], [token_shape], [], "square_sums"
    )(place, token, *pieces)


def grad_kernel(share, count, first, place, start, *refs):
    refs = list(refs)
    stepping = count > 0
    if stepping:
        pieces, refs = refs[:2], refs[2:]
        sums, refs = refs[:share], refs[share:]
        if not first:
            old, refs = refs[0], refs[1:]
    sides, refs = refs[:share], refs[share:]
    outs, refs = refs[:3], refs[3:]
    if stepping:
        new, refs = refs[0], refs[1:]
    full, key, target, hidden, upward, gateward = refs
    if stepping:
        weights = stepped(place, pieces, sums, start if first else old, start, share, full)
        for m in range(3):
            new[m] = weights[m]
    else:
        weights = [start[m].astype(jnp.float32) for m in range(3)]
    gate_weight, up_weight, down_weight = (split(block) for block in weights)
    rows = sides[0].shape[1]
    chunk = min(rows, 256)
    for at, side in enumerate(sides):
        for begin in range(0, rows, chunk):
            here = pl.ds(at * rows + begin, chunk)
            keys = split(side[0, begin : begin + chunk, :])
            targets = split(side[1, begin : begin + chunk, :])
            key[here, :], target[here, :] = keys[0], targets[0]
            gate = dot3(keys, gate_weight)
            upper = dot3(keys, up_weight)
            back = dot3(targets, down_weight)
            sigma = jax.nn.sigmoid(gate)
            active = gate * sigma
            hidden[0, here, :], hidden[1, here, :] = split(active * upper)
            upward[0, here, :], upward[1, here, :] = split(back * active)
            slope = upper * sigma * (1.0 + gate * (1.0 - sigma))
            gateward[0, here, :], gateward[1, here, :] = split(back * slope)
    for m, left, right in ((2, target, hidden), (1, key, upward), (0, key, gateward)):
        rows_first = left[...]
        full[...] = dot(rows_first, right[0], over_rows) + dot(rows_first, right[1], over_rows)
        cut(full, outs, m, place)


def start_spec(start, head, share):
    _, parts, width, hidden = start.shape
    return pl.BlockSpec(
        (None, parts, width, hidden // share), lambda i, place: (head, 0, 0, place[0])
    )


def fast_grad(place, token, start, head, sides, share, count, step=None, late=()):
    rows = sum(side.shape[1] for side in sides)
    _, parts, width, hidden = start.shape
    hidden = hidden // share
    piece = jax.ShapeDtypeStruct((parts, width // 4, hidden), jnp.float32)
    pair = jax.ShapeDtypeStruct((parts, width // 2, hidden), jnp.float32)
    out_shape = [piece, piece, pair]
    operands = list(sides)
    if step is not None:
        pieces, sums, weights = step
        old = [] if weights is None else [weights]
        operands = list(pieces) + list(sums) + old + operands
        out_shape.append(jax.ShapeDtypeStruct((parts, width, hidden), jnp.float32))
    by_width = pltpu.VMEM((rows, width), jnp.bfloat16)
    by_hidden = pltpu.VMEM((2, rows, hidden), jnp.bfloat16)
    return ordered(
        functools.partial(grad_kernel, share, count, step is not None and step[2] is None),
        (1,),
        [start_spec(start, head, share)] + [whole() for _ in operands],
        [whole() for _ in out_shape],
        out_shape,
        [
            pltpu.VMEM((width, hidden), jnp.float32),
            by_width,
            by_width,
            by_hidden,
            by_hidden,
            by_hidden,
        ],
        "fast_grad",
        late=len(late),
    )(place, token, start, *operands, *late)


def apply_kernel(share, head, place, start, *refs):
    pieces, refs = refs[:2], refs[2:]
    sums, refs = refs[:share], refs[share:]
    old, kept, refs = refs[0], refs[1], refs[2:]
    queries, out, full = refs[:share], refs[share], refs[-1]
    keep = place[2] == 1
    weights = stepped(place, pieces, sums, old, start, share, full)
    weights = [jnp.where(keep, kept[m], weights[m]) for m in range(3)]
    gate_weight, up_weight, down_weight = (split(block) for block in weights)
    rows = queries[0].shape[1]
    chunk = min(rows, 256)
    for distance, query in enumerate(queries):
        slot = lax.rem(place[0] + share - distance, share)
        for begin in range(0, rows, chunk):
            here = pl.ds(begin, chunk)
            values = split(query[head, here, :])
            gate = dot3(values, gate_weight)
            hidden = split(gate * jax.nn.sigmoid(gate) * dot3(values, up_weight))
            out[slot, here, :] = dot3(hidden, down_weight, rows_by_rows)


def fast_apply(place, token, start, head, queries, share, pieces, sums, weights, kept, late):
    operands = list(pieces) + list(sums) + [weights, kept] + list(queries)
    _, rows, width = queries[0].shape
    return ordered(
        functools.partial(apply_kernel, share, head),
        (1,),
        [start_spec(start, head, share)] + [whole() for _ in operands],
        [whole()],
        [jax.ShapeDtypeStruct((share, rows, width), jnp.float32)],
        [pltpu.VMEM(weights.shape[1:], jnp.float32)],
        "fast_apply",
        late=len(late),
    )(place, token, start, *operands, *late)


def finish_kernel(place, *refs):
    parts, out = refs
    total = parts[0]
    for i in range(1, parts.shape[0]):
        total = total + parts[i]
    out[...] = normalize(total)


def finish(place, token, parts, late):
    return ordered(
        finish_kernel,
        (1,),
        [whole()],
        [whole()],
        [jax.ShapeDtypeStruct(parts.shape[1:], jnp.float32)],
        [],
        "finish",
        late=len(late),
    )(place, token, parts, *late)


def halve(total, bit, place, outs):
    if bit is None:
        outs[0][...] = total
        return
    size = outs[0].shape[1]
    mine = lax.rem(lax.div(place[4], bit), 2) == 1
    low, high = total[:, :size], total[:, size:]
    outs[0][...] = jnp.where(mine, low, high)
    outs[1][...] = jnp.where(mine, high, low)


def gather_kernel(bit, place, own, line, other, send, keep):
    helping = place[1] == 1
    size = own.shape[1]
    send[...] = jnp.where(helping, other[:, size:], line[...])
    keep[...] = jnp.where(helping, other[:, :size], own[...])


def add_kernel(bit, place, own, other, *outs):
    halve(own[...] + other[...], bit, place, outs)


def pair_kernel(bit, place, own, other, out):
    size = own.shape[1]
    if bit is None:
        out[:, :size] = own[...]
        out[:, size:] = other[...]
        return
    mine = lax.rem(lax.div(place[4], bit), 2) == 1
    out[:, :size] = jnp.where(mine, other[...], own[...])
    out[:, size:] = jnp.where(mine, own[...], other[...])


def combine(place, token, kernel, operands, bit, late=(), name="combine"):
    parts, size, width = operands[0].shape
    count = 1
    if kernel is pair_kernel:
        size = 2 * size
    elif kernel is gather_kernel:
        count = 2
    elif bit is not None:
        count, size = 2, size // 2
    return ordered(
        functools.partial(kernel, bit),
        (1,),
        [whole() for _ in operands],
        [whole()] * count,
        [jax.ShapeDtypeStruct((parts, size, width), jnp.float32)] * count,
        [],
        name,
        late=len(late),
    )(place, token, *operands, *late)


def output_kernel(heads, prepared, share, place, *refs):
    refs = list(refs)
    out = refs.pop(-2 if prepared is not None else -1)
    total = None

    def chosen(head):
        weight = refs.pop(0)[...]
        for distance in range(1, share):
            other = refs.pop(0)[...]
            weight = jnp.where(lax.rem(place[0] + share - distance, share) == head, other, weight)
        return weight.astype(jnp.bfloat16)

    for head, far in heads:
        block = refs.pop(0)[...].astype(jnp.bfloat16)
        part = dot(block, chosen(head) if far else refs.pop(0)[...])
        total = part if total is None else total + part
    out[...] = total
    if prepared is not None:
        refs[-1][...] = chosen(prepared)


def output(place, token, near, distant, prepared, columns, share):
    rows, width = near[0][1].shape
    half = columns // 2
    by_half = pl.BlockSpec((rows, half), lambda i, place: (0, i))
    by_rows = pl.BlockSpec((rows, width), lambda i, place: (0, 0))
    weight_half = pl.BlockSpec((width, half), lambda i, place: (0, i))
    operands, in_specs = [], []
    for head, block, weight in near:
        operands += [block, weight]
        spec = pl.BlockSpec((width, half), lambda i, place, head=head: (head, 2 * place[3] + i))
        in_specs += [by_rows, spec]
    for head, block, weights in distant:
        operands += [block] + list(weights)
        in_specs += [by_rows] + [weight_half for _ in weights]
    out_specs, out_shape = [by_half], [jax.ShapeDtypeStruct((rows, columns), jnp.float32)]
    ready = None
    if prepared is not None:
        ready, weights = prepared
        operands += list(weights)
        in_specs += [weight_half for _ in weights]
        out_specs.append(weight_half)
        out_shape.append(jax.ShapeDtypeStruct((width, columns), jnp.bfloat16))
    heads = [(head, False) for head, _, _ in near] + [(head, True) for head, _, _ in distant]
    return ordered(
        functools.partial(output_kernel, heads, ready, share),
        (2,),
        in_specs,
        out_specs,
        out_shape,
        [],
        "output",
    )(place, token, *operands)


def last_kernel(place, sofar, block, weight, out):
    total = sofar[...] + dot(block[...].astype(jnp.bfloat16), weight[...])
    out[...] = total.astype(out.dtype)


def add_last(place, token, sofar, block, weight):
    return ordered(
        last_kernel,
        (1,),
        [whole()] * 3,
        [whole()],
        [jax.ShapeDtypeStruct(sofar.shape, jnp.bfloat16)],
        [],
        "add_last",
    )(place, token, sofar, block, weight)


def within_chip(block, share, distance):
    devices = range(lax.axis_size("tok"))
    route = [(t, t // share * share + (t + distance) % share) for t in devices]
    return lax.ppermute(block, "tok", route)


def swapped(blocks, share):
    size = lax.axis_size("tok")
    chips = [[first + core for core in range(share)] for first in range(0, size, share)]
    return lax.all_to_all(blocks, "tok", 0, 0, axis_index_groups=chips, tiled=True)


def flipped(block, share, bit):
    route = [(t, t ^ (bit * share)) for t in range(lax.axis_size("tok"))]
    return lax.ppermute(block, "tok", route)


def crossed(block, one, two, both):
    size = lax.axis_size("tok")
    route = [(one * size + t, two * size + t) for t in range(size)]
    if both:
        route += [(two * size + t, one * size + t) for t in range(size)]
    covered = {device for pair in route for device in pair}
    every = range(size * lax.axis_size("block"))
    route += [(device, device) for device in every if device not in covered]
    return lax.ppermute(block, ("block", "tok"), route)


def body(tokens, input_weight, rate_weight, fast_init, output_weight):
    block_count, tok_rows, model_width = tokens.shape
    heads, _, head_dim, _ = fast_init.shape
    share = heads
    members = lax.axis_size("head")
    groups = lax.axis_size("block")
    position = lax.axis_index("block")
    member = lax.axis_index("head")
    core = lax.axis_index("tok") % share
    chip = lax.axis_index("tok") // share
    length = lax.axis_size("tok") // share
    bits = [1 << b for b in range(1, length.bit_length() - 1)]
    flattened = tokens.reshape(tok_rows, model_width)
    weight = jnp.transpose(input_weight, (1, 0, 2))
    rate = jnp.transpose(rate_weight)
    columns = output_weight.shape[1] // members
    every_head = range(heads)

    def exchanged(block):
        return [block] + [within_chip(block, share, distance) for distance in range(1, share)]

    def around(block, ahead):
        return lax.ppermute(block, "head", [(i, (i + ahead) % members) for i in range(members)])

    def place(helper, keep):
        return jnp.stack([core, position == helper, keep, member, chip]).astype(jnp.int32)

    token = jnp.zeros(token_shape.shape, jnp.float32)
    never = position < 0
    sides = [None] * heads
    queries = []

    kept = [None] * heads
    steps = [None] * heads
    far_weights = []
    parts = [None] * heads

    def start_section(section, head, here, helper, token):
        if section == 0:
            late = queries if head + 1 == heads else ()
            *pieces, token = fast_grad(
                here, token, fast_init, head, sides[head], share, 0, None, late
            )
            weights = None
        else:
            pieces, weights = steps[head]
            *pieces, weights, token = fast_grad(
                here, token, fast_init, head, sides[head], share, section,
                (pieces, squares[head], weights),
            )
            kept[head] = (
                weights
                if section == 1
                else jnp.where(position == section - 1, weights, kept[head])
            )
        own, line, other = pieces
        steps[head] = None, weights
        parts[head] = own, line, crossed(other, section, helper, section == 0)
        return token

    def advance(stage, head, here, section, helper, last, token, late):
        count = len(bits)
        if stage == 0:
            *outs, token = combine(here, token, gather_kernel, parts[head], None, late)
            parts[head] = outs[1], flipped(outs[0], share, 1)
        elif stage <= count + 1:
            bit = bits[stage - 1] if stage <= count else None
            *outs, token = combine(here, token, add_kernel, parts[head], bit, late)
            total = outs[-1]
            if bit is not None:
                parts[head] = total, flipped(outs[0], share, bit)
        else:
            bit = bits[2 * count + 1 - stage] if stage <= 2 * count + 1 else None
            name = "combine_last" if bit is None else "combine"
            total, token = combine(here, token, pair_kernel, parts[head], bit, late, name)
        if count < stage <= 2 * count:
            parts[head] = total, flipped(total, share, bits[2 * count - stage])
        elif stage == 2 * count + 1:
            parts[head] = total, flipped(total, share, 1)
        elif stage == 2 * count + 2:
            steps[head] = (total, crossed(total, helper, section, not last)), steps[head][1]
        return token

    helpers = [section + 1 if section + 1 < groups else section - 1 for section in range(groups)]
    places = [place(helper, never) for helper in helpers]
    final = place(helpers[-1], position != groups - 1)
    near, distant = [], [[] for _ in range(1, members)]
    applied = [None] * heads
    squares = [None] * heads
    stages = 2 * len(bits) + 3

    compute, cross, hop, reduce = 6.0, 19.0, 10.5, 3.0
    tasks = []
    for head in every_head:
        begin = head * 25.3
        tasks.append((begin - compute if head == 0 else head * compute, "project", 0, head, 0))
        for section in range(groups):
            tasks.append((begin, "start", section, head, 0))
            for stage in range(stages):
                when = begin + compute + cross + stage * hop
                tasks.append((when, "stage", section, head, stage))
                if section == 0 and head == 0 and stage == 0:
                    tasks.append((when + 0.1, "widen", 0, 0, 0))
            begin += compute + 2 * cross + (stages - 1) * hop
            tasks.append((begin, "sums", section, head, 0))
            begin += reduce
        tasks.append((begin + 5.0, "apply", 0, head, 0))
        tasks.append((begin + 11.0, "finish", 0, head, 0))

    for _, task, section, head, stage in sorted(tasks):
        last = section + 1 == groups
        helper = helpers[section]
        here = places[section]
        if task == "project":
            chosen_parts = [(1, head), (2, head)]
            if head + 1 == heads:
                chosen_parts += [(0, other) for other in every_head]
            *made, token = project(here, token, flattened, weight, rate, chosen_parts, heads, 2)
            sides[head] = exchanged(made[0])
            if head + 1 == heads:
                queries += exchanged(made[1])
        elif task == "start":
            token = start_section(section, head, places[max(section - 1, 0)], helper, token)
        elif task == "stage":
            late = []
            if section == 1 and head == 0 and stage == 0:
                late = [blocks[0] for blocks in far_weights]
            if section == 1 and head == heads - 1 and stage == 0:
                late = [block for blocks in far_weights for block in blocks]
            token = advance(stage, head, here, section, helper, last, token, late)
        elif task == "widen":
            for ahead in range(1, members):
                wide, token = widen(here, token, output_weight, ahead, members, share)
                far_weights.append(exchanged(around(wide, ahead)))
        elif task == "sums":
            sums, token = square_sums(here, token, steps[head][0])
            squares[head] = exchanged(sums)
        elif task == "apply":
            pieces, weights = steps[head]
            *made, token = fast_apply(
                final, token, fast_init, head, queries, share,
                pieces, squares[head], weights, kept[head],
                (),
            )
            applied[head] = swapped(made[0], share)
        else:
            late = [block for blocks in distant for block in blocks]
            whole_block, token = finish(final, token, applied[head], ())
            near.append(whole_block)
            for ahead in range(1, members):
                distant[ahead - 1].append(around(whole_block, ahead))

    here = final
    pairs = [(head, near[head], output_weight) for head in every_head]
    others = [
        (head, distant[ahead][head], far_weights[ahead])
        for head in every_head
        for ahead in range(members - 1)
    ]
    if not others:
        mixed, token = output(here, token, pairs, [], None, columns, share)
        mixed = mixed.astype(jnp.bfloat16)
    else:
        head, block, candidates = others[-1]
        mixed, ready, token = output(
            here, token, pairs, others[:-1], (head, candidates), columns, share
        )
        mixed, token = add_last(here, token, mixed, block, ready)
    return mixed.reshape(block_count, tok_rows, -1)


def solution(mesh):
    placed = (
        P("block", "tok", None),
        P(None, None, "head"),
        P(None, "head"),
        P("head", None, None, None),
        P("head", None),
    )
    return jax.shard_map(
        body, mesh=mesh, in_specs=placed, out_specs=P("block", "tok", "head"), check_vma=False
    )
```

```python
import functools

import jax
import jax.numpy as jnp
from jax import lax
from jax.experimental import pallas as pl
from jax.experimental.pallas import tpu as pltpu
from jax.sharding import PartitionSpec as P

epsilon = 1e-06
step_size = 0.03
vmem_bytes = 14 * 2**20
rows_by_rows = (((1,), (1,)), ((), ()))
over_rows = (((0,), (0,)), ((), ()))
plain = (((1,), (0,)), ((), ()))


def params(limit=vmem_bytes):
    return pltpu.CompilerParams(vmem_limit_bytes=limit)


def dot(left, right, dims=plain):
    return lax.dot_general(left, right, dims, preferred_element_type=jnp.float32)


def split(values):
    high = values.astype(jnp.bfloat16)
    return high, (values - high.astype(jnp.float32)).astype(jnp.bfloat16)


def dot3(left, right, dims=plain):
    return dot(left[0], right[0], dims) + (dot(left[0], right[1], dims) + dot(left[1], right[0], dims))


def normalize(values):
    return values / jnp.sqrt(jnp.mean(values * values, axis=-1, keepdims=True) + epsilon)


token_shape = jax.ShapeDtypeStruct((8, 128), jnp.float32)
unread = pl.BlockSpec(memory_space=pl.ANY)


def whole():
    return pl.BlockSpec(memory_space=pltpu.VMEM)


hiding = {"project": 40 * 10**9, "output": 2 * 10**9, "fast_step": 4 * 10**9}


def ordered(kernel, grid, in_specs, out_specs, out_shape, scratch, name, limit=vmem_bytes, late=0):
    def traced(place, token, *refs):
        outs = len(out_shape)
        inputs = len(in_specs)
        refs = refs[:inputs] + refs[inputs + late :]
        refs[inputs + outs][...] = jnp.zeros(token_shape.shape, jnp.float32)
        kernel(place, *refs[: inputs + outs], *refs[inputs + outs + 1 :])

    return pl.pallas_call(
        traced,
        grid_spec=pltpu.PrefetchScalarGridSpec(
            num_scalar_prefetch=1,
            grid=grid,
            in_specs=[unread] + in_specs + [unread] * late,
            out_specs=list(out_specs)
            + [pl.BlockSpec(token_shape.shape, lambda i, place: (0, 0))],
            scratch_shapes=scratch,
        ),
        out_shape=list(out_shape) + [token_shape],
        compiler_params=params(limit),
        cost_estimate=pl.CostEstimate(
            flops=hiding.get(name, 0), bytes_accessed=0, transcendentals=0
        ),
        name=name,
    )


def project_kernel(chosen, pairs, place, tokens, weight, rate, *outs):
    values = dot(tokens[...], weight[...])
    for i, (part, head) in enumerate(chosen):

        @pl.when(pl.program_id(0) == i)
        def _():
            if part == 2:
                logits = dot(tokens[...], rate[...], rows_by_rows)
                logit = logits[:, head : head + 1]
                rates = jnp.maximum(logit, 0.0) + jnp.log1p(jnp.exp(-jnp.abs(logit)))
                outs[0][...] = values * rates
            else:
                outs[0 if i < pairs else 1][...] = normalize(values)


def project(place, token, tokens, weight, rate, chosen, heads, pairs):
    rows, depth = tokens.shape
    count = len(chosen)
    width = weight.shape[2] // heads
    by_part = [part for part, _ in chosen]
    by_head = [head for _, head in chosen]

    def table(values, i):
        picked = values[0]
        for at, value in enumerate(values[1:], 1):
            picked = jnp.where(i >= at, value, picked)
        return picked

    sizes = [pairs] + ([count - pairs] if count > pairs else [])
    places = [lambda i: jnp.minimum(i, pairs - 1), lambda i: jnp.maximum(i - pairs, 0)]
    return ordered(
        functools.partial(project_kernel, chosen, pairs),
        (count,),
        [
            pl.BlockSpec((rows, depth), lambda i, place: (0, 0)),
            pl.BlockSpec(
                (None, depth, width),
                lambda i, place: (table(by_part, i), 0, table(by_head, i)),
            ),
            pl.BlockSpec(rate.shape, lambda i, place: (0, 0)),
        ],
        [
            pl.BlockSpec((None, rows, width), lambda i, place, at=at: (at(i), 0, 0))
            for at in places[: len(sizes)]
        ],
        [jax.ShapeDtypeStruct((size, rows, width), jnp.float32) for size in sizes],
        [],
        "project",
        50 * 2**20,
    )(place, token, tokens, weight, rate)


def widen_kernel(place, weight, out):
    out[...] = weight[...].astype(jnp.float32)


def widen(place, token, weight, ahead, members, share):
    rows, columns = weight.shape[0] // share, weight.shape[1] // members
    step = rows // 2

    def chosen(i, place):
        return place[0] * 2 + i, lax.rem(place[3] + ahead, members)

    return ordered(
        widen_kernel,
        (2,),
        [pl.BlockSpec((step, columns), chosen)],
        [pl.BlockSpec((step, columns), lambda i, place: (i, 0))],
        [jax.ShapeDtypeStruct((rows, columns), jnp.float32)],
        [],
        "widen",
    )(place, token, weight)


def cut(grads, outs, m, place, role):
    size = outs[0].shape[1]
    odd = lax.rem(place[4], 2)
    for out, piece in zip(
        outs,
        (2 * role + odd, 2 * role + 1 - odd, 2 * (1 - role) + odd, 2 * (1 - role) + 1 - odd),
    ):
        out[m] = grads[pl.ds(pl.multiple_of(piece * size, size), size), :]


def joined(pieces, m, place, role, full):
    size = pieces[0].shape[1]
    odd = lax.rem(place[4], 2)
    for block, piece in zip(
        pieces,
        (2 * role + odd, 2 * role + 1 - odd, 2 * (1 - role) + odd, 2 * (1 - role) + 1 - odd),
    ):
        full[pl.ds(pl.multiple_of(piece * size, size), size), :] = block[m]
    return full[...]


def stepped(place, pieces, sums, weights, start, share, full):
    results = []
    for m in range(3):
        grads = joined(pieces, m, place, place[1], full)
        square = sums[0][m, 0]
        for other in sums[1:]:
            square = square + other[m, 0]
        scale = jnp.full((1, 1), square / (grads.size * share) + epsilon, jnp.float32)
        moved = weights[m].astype(jnp.float32) + grads * (step_size / jnp.sqrt(scale))
        first = start[m].astype(jnp.float32)
        base = jnp.sqrt(jnp.mean(first * first, axis=0, keepdims=True))
        column = jnp.mean(moved * moved, axis=0, keepdims=True)
        results.append(moved * (base / jnp.sqrt(column + epsilon)))
    return results


def sums_kernel(place, *refs):
    pieces, out = refs[:-1], refs[-1]
    row = lax.broadcasted_iota(jnp.int32, out.shape, 0)
    total = jnp.zeros(out.shape, jnp.float32)
    for m in range(3):
        square = sum(jnp.sum(piece[m] * piece[m]) for piece in pieces)
        total = jnp.where(row == m, square, total)
    out[...] = total


def square_sums(place, token, pieces):
    return ordered(
        sums_kernel, (1,), [whole()] * len(pieces), [whole()], [token_shape], [], "square_sums"
    )(place, token, *pieces)


def grad_kernel(share, count, first, place, start, *refs):
    refs = list(refs)
    stepping = count > 0
    if stepping:
        pieces, refs = refs[:4], refs[4:]
        sums, refs = refs[:share], refs[share:]
        if not first:
            old, refs = refs[0], refs[1:]
    sides, refs = refs[:share], refs[share:]
    if stepping:
        *refs, held, arrived = refs
        copies = [
            pltpu.make_async_copy(side, held.at[i], arrived.at[i]) for i, side in enumerate(sides)
        ]
        for copy in copies:
            copy.start()
        sides = [held.at[i] for i in range(share)]
    outs, refs = refs[:4], refs[4:]
    if stepping:
        new, refs = refs[0], refs[1:]
    full, key, target, hidden, upward, gateward = refs
    if stepping:
        weights = stepped(place, pieces, sums, start if first else old, start, share, full)
        for m in range(3):
            new[m] = weights[m]
        for copy in copies:
            copy.wait()
    else:
        weights = [start[m].astype(jnp.float32) for m in range(3)]
    gate_weight, up_weight, down_weight = (split(block) for block in weights)
    rows = sides[0].shape[1]
    chunk = min(rows, 256)
    for at, side in enumerate(sides):
        for begin in range(0, rows, chunk):
            here = pl.ds(at * rows + begin, chunk)
            keys = split(side[0, begin : begin + chunk, :])
            targets = split(side[1, begin : begin + chunk, :])
            key[here, :], target[here, :] = keys[0], targets[0]
            gate = dot3(keys, gate_weight)
            upper = dot3(keys, up_weight)
            back = dot3(targets, down_weight)
            sigma = jax.nn.sigmoid(gate)
            active = gate * sigma
            hidden[0, here, :], hidden[1, here, :] = split(active * upper)
            upward[0, here, :], upward[1, here, :] = split(back * active)
            slope = upper * sigma * (1.0 + gate * (1.0 - sigma))
            gateward[0, here, :], gateward[1, here, :] = split(back * slope)
    for m, left, right in ((2, target, hidden), (1, key, upward), (0, key, gateward)):
        rows_first = left[...]
        full[...] = dot(rows_first, right[0], over_rows) + dot(rows_first, right[1], over_rows)
        cut(full, outs, m, place, 0)


def start_spec(start, head, share):
    _, parts, width, hidden = start.shape
    return pl.BlockSpec(
        (None, parts, width, hidden // share), lambda i, place: (head, 0, 0, place[0])
    )


def fast_grad(place, token, start, head, sides, share, count, step=None, late=()):
    rows = sum(side.shape[1] for side in sides)
    _, parts, width, hidden = start.shape
    hidden = hidden // share
    piece = jax.ShapeDtypeStruct((parts, width // 4, hidden), jnp.float32)
    out_shape = [piece] * 4
    operands = list(sides)
    extra = []
    if step is not None:
        extra = [
            pltpu.VMEM((share,) + sides[0].shape, jnp.float32),
            pltpu.SemaphoreType.DMA((share,)),
        ]
        pieces, sums, weights = step
        old = [] if weights is None else [weights]
        operands = list(pieces) + list(sums) + old + operands
        out_shape.append(jax.ShapeDtypeStruct((parts, width, hidden), jnp.float32))
    by_width = pltpu.VMEM((rows, width), jnp.bfloat16)
    by_hidden = pltpu.VMEM((2, rows, hidden), jnp.bfloat16)
    return ordered(
        functools.partial(grad_kernel, share, count, step is not None and step[2] is None),
        (1,),
        [start_spec(start, head, share)]
        + [whole() for _ in operands[: len(operands) - share]]
        + [whole() if step is None else unread] * share,
        [whole() for _ in out_shape],
        out_shape,
        [
            pltpu.VMEM((width, hidden), jnp.float32),
            by_width,
            by_width,
            by_hidden,
            by_hidden,
            by_hidden,
        ]
        + extra,
        "fast_grad" if step is None else "fast_step",
        20 * 2**20,
        late=len(late),
    )(place, token, start, *operands, *late)


def apply_kernel(share, head, place, start, *refs):
    pieces, refs = refs[:4], refs[4:]
    sums, refs = refs[:share], refs[share:]
    old, kept, refs = refs[0], refs[1], refs[2:]
    queries, (out, full, held, arrived) = refs[:share], refs[share:]
    copies = [
        pltpu.make_async_copy(query.at[head], held.at[i], arrived.at[i])
        for i, query in enumerate(queries)
    ]
    for copy in copies:
        copy.start()
    keep = place[2] == 1
    weights = stepped(place, pieces, sums, old, start, share, full)
    weights = [jnp.where(keep, kept[m], weights[m]) for m in range(3)]
    gate_weight, up_weight, down_weight = (split(block) for block in weights)
    rows = held.shape[1]
    chunk = min(rows, 256)
    for copy in copies:
        copy.wait()
    for distance in range(share):
        slot = lax.rem(place[0] + share - distance, share)
        for begin in range(0, rows, chunk):
            here = pl.ds(begin, chunk)
            values = split(held[distance, here, :])
            gate = dot3(values, gate_weight)
            hidden = split(gate * jax.nn.sigmoid(gate) * dot3(values, up_weight))
            out[slot, here, :] = dot3(hidden, down_weight, rows_by_rows)


def fast_apply(place, token, start, head, queries, share, pieces, sums, weights, kept, late):
    operands = list(pieces) + list(sums) + [weights, kept] + list(queries)
    _, rows, width = queries[0].shape
    return ordered(
        functools.partial(apply_kernel, share, head),
        (1,),
        [start_spec(start, head, share)]
        + [whole() for _ in operands[: len(operands) - share]]
        + [unread] * share,
        [whole()],
        [jax.ShapeDtypeStruct((share, rows, width), jnp.float32)],
        [
            pltpu.VMEM(weights.shape[1:], jnp.float32),
            pltpu.VMEM((share, rows, width), jnp.float32),
            pltpu.SemaphoreType.DMA((share,)),
        ],
        "fast_apply",
        20 * 2**20,
        late=len(late),
    )(place, token, start, *operands, *late)


def finish_kernel(place, *refs):
    parts, out = refs
    total = parts[0]
    for i in range(1, parts.shape[0]):
        total = total + parts[i]
    out[...] = normalize(total)


def finish(place, token, parts):
    return ordered(
        finish_kernel,
        (1,),
        [whole()],
        [whole()],
        [jax.ShapeDtypeStruct(parts.shape[1:], jnp.float32)],
        [],
        "finish",
    )(place, token, parts)


def halve(total, bit, place, outs):
    if bit is None:
        outs[0][...] = total
        return
    size = outs[0].shape[1]
    mine = lax.rem(lax.div(place[4], bit), 2) == 1
    low, high = total[:, :size], total[:, size:]
    outs[0][...] = jnp.where(mine, low, high)
    outs[1][...] = jnp.where(mine, high, low)


def gather_kernel(bit, place, own, line, across, corner, *outs):
    helping = place[1] == 1
    total = jnp.where(helping, across[...], own[...]) + jnp.where(helping, corner[...], line[...])
    halve(total, bit, place, outs)


def add_kernel(bit, place, own, other, *outs):
    halve(own[...] + other[...], bit, place, outs)


def pair_kernel(bit, place, own, other, out):
    size = own.shape[1]
    mine = lax.rem(lax.div(place[4], bit), 2) == 1
    out[:, :size] = jnp.where(mine, other[...], own[...])
    out[:, size:] = jnp.where(mine, own[...], other[...])


def combine(place, token, kernel, operands, bit, late=()):
    parts, size, width = operands[0].shape
    count = 1
    if kernel is pair_kernel:
        size = 2 * size
    elif bit is not None:
        count, size = 2, size // 2
    return ordered(
        functools.partial(kernel, bit),
        (1,),
        [whole() for _ in operands],
        [whole()] * count,
        [jax.ShapeDtypeStruct((parts, size, width), jnp.float32)] * count,
        [],
        "combine",
        late=len(late),
    )(place, token, *operands, *late)


def output_kernel(heads, prepared, share, place, *refs):
    refs = list(refs)
    out = refs.pop(-2 if prepared is not None else -1)
    total = None

    def chosen(head):
        weight = refs.pop(0)[...]
        for distance in range(1, share):
            other = refs.pop(0)[...]
            weight = jnp.where(lax.rem(place[0] + share - distance, share) == head, other, weight)
        return weight.astype(jnp.bfloat16)

    for head, far in heads:
        block = refs.pop(0)[...].astype(jnp.bfloat16)
        part = dot(block, chosen(head) if far else refs.pop(0)[...])
        total = part if total is None else total + part
    out[...] = total
    if prepared is not None:
        refs[-1][...] = chosen(prepared)


def output(place, token, near, distant, prepared, columns, share):
    rows, width = near[0][1].shape
    half = columns // 2
    by_half = pl.BlockSpec((rows, half), lambda i, place: (0, i))
    by_rows = pl.BlockSpec((rows, width), lambda i, place: (0, 0))
    weight_half = pl.BlockSpec((width, half), lambda i, place: (0, i))
    operands, in_specs = [], []
    for head, block, weight in near:
        operands += [block, weight]
        spec = pl.BlockSpec((width, half), lambda i, place, head=head: (head, 2 * place[3] + i))
        in_specs += [by_rows, spec]
    for head, block, weights in distant:
        operands += [block] + list(weights)
        in_specs += [by_rows] + [weight_half for _ in weights]
    out_specs, out_shape = [by_half], [jax.ShapeDtypeStruct((rows, columns), jnp.float32)]
    ready = None
    if prepared is not None:
        ready, weights = prepared
        operands += list(weights)
        in_specs += [weight_half for _ in weights]
        out_specs.append(weight_half)
        out_shape.append(jax.ShapeDtypeStruct((width, columns), jnp.bfloat16))
    heads = [(head, False) for head, _, _ in near] + [(head, True) for head, _, _ in distant]
    return ordered(
        functools.partial(output_kernel, heads, ready, share),
        (2,),
        in_specs,
        out_specs,
        out_shape,
        [],
        "output",
    )(place, token, *operands)


def last_kernel(place, sofar, block, weight, out):
    total = sofar[...] + dot(block[...].astype(jnp.bfloat16), weight[...])
    out[...] = total.astype(out.dtype)


def add_last(place, token, sofar, block, weight):
    return ordered(
        last_kernel,
        (1,),
        [whole()] * 3,
        [whole()],
        [jax.ShapeDtypeStruct(sofar.shape, jnp.bfloat16)],
        [],
        "add_last",
    )(place, token, sofar, block, weight)


def within_chip(block, share, distance):
    devices = range(lax.axis_size("tok"))
    route = [(t, t // share * share + (t + distance) % share) for t in devices]
    return lax.ppermute(block, "tok", route)


def swapped(blocks, share):
    size = lax.axis_size("tok")
    chips = [[first + core for core in range(share)] for first in range(0, size, share)]
    return lax.all_to_all(blocks, "tok", 0, 0, axis_index_groups=chips, tiled=True)


def flipped(block, share, bit):
    route = [(t, t ^ (bit * share)) for t in range(lax.axis_size("tok"))]
    return lax.ppermute(block, "tok", route)


def crossed(block, share, bit, one, two, both):
    size = lax.axis_size("tok")
    route = [(one * size + t, two * size + (t ^ (bit * share))) for t in range(size)]
    if one != two:
        back = bit * share if both else 0
        route += [(two * size + t, one * size + (t ^ back)) for t in range(size)]
    covered = {source for source, _ in route}
    every = range(size * lax.axis_size("block"))
    route += [(device, device) for device in every if device not in covered]
    return lax.ppermute(block, ("block", "tok"), route)


def body(tokens, input_weight, rate_weight, fast_init, output_weight):
    block_count, tok_rows, model_width = tokens.shape
    heads, _, head_dim, _ = fast_init.shape
    share = heads
    members = lax.axis_size("head")
    groups = lax.axis_size("block")
    position = lax.axis_index("block")
    member = lax.axis_index("head")
    core = lax.axis_index("tok") % share
    chip = lax.axis_index("tok") // share
    length = lax.axis_size("tok") // share
    bits = [1 << b for b in range(1, length.bit_length() - 1)]
    flattened = tokens.reshape(tok_rows, model_width)
    weight = jnp.transpose(input_weight, (1, 0, 2))
    rate = jnp.transpose(rate_weight)
    columns = output_weight.shape[1] // members
    every_head = range(heads)

    def exchanged(block):
        return [block] + [within_chip(block, share, distance) for distance in range(1, share)]

    def around(block, ahead):
        return lax.ppermute(block, "head", [(i, (i + ahead) % members) for i in range(members)])

    def place(helper, keep):
        return jnp.stack([core, position == helper, keep, member, chip]).astype(jnp.int32)

    token = jnp.zeros(token_shape.shape, jnp.float32)
    never = position < 0
    here = place(1, never)
    sides = []
    for head in every_head:
        chosen_parts = [(1, head), (2, head)]
        if head + 1 == heads:
            chosen_parts += [(0, other) for other in every_head]
        *made, token = project(here, token, flattened, weight, rate, chosen_parts, heads, 2)
        sides.append(exchanged(made[0]))
    queries = exchanged(made[1])

    kept = [None] * heads
    steps = [None] * heads
    far_weights = []
    parts = [None] * heads

    def start_section(section, head, here, helper, token):
        if section == 0:
            late = queries if head + 1 == heads else ()
            *pieces, token = fast_grad(
                here, token, fast_init, head, sides[head], share, 0, None, late
            )
            weights = None
        else:
            pieces, weights = steps[head]
            sums, token = square_sums(here, token, pieces)
            *pieces, weights, token = fast_grad(
                here, token, fast_init, head, sides[head], share, section,
                (pieces, exchanged(sums), weights),
            )
            kept[head] = (
                weights
                if section == 1
                else jnp.where(position == section - 1, weights, kept[head])
            )
        own, line, across, corner = pieces
        steps[head] = None, weights
        parts[head] = (
            own,
            crossed(line, share, 1, section, section, False),
            crossed(across, share, 0, section, helper, False),
            crossed(corner, share, 1, section, helper, False),
        )
        return token

    def advance(stage, head, here, section, helper, last, token, late):
        count = len(bits)
        if stage <= count:
            bit = bits[stage] if stage < count else None
            kernel = add_kernel if stage else gather_kernel
            *outs, token = combine(here, token, kernel, parts[head], bit, late)
            total = outs[-1]
            if bit is not None:
                parts[head] = total, flipped(outs[0], share, bit)
                return token
        else:
            bit = bits[2 * count - stage]
            total, token = combine(here, token, pair_kernel, parts[head], bit, late)
        if stage < 2 * count:
            parts[head] = total, flipped(total, share, bits[2 * count - stage - 1])
        else:
            pieces = (
                total,
                crossed(total, share, 1, section, section, False)
                if last
                else flipped(total, share, 1),
                crossed(total, share, 0, helper, section, not last),
                crossed(total, share, 1, helper, section, not last),
            )
            steps[head] = pieces, steps[head][1]
        return token

    near, distant = [], [[] for _ in range(1, members)]
    for section in range(groups):
        last = section + 1 == groups
        helper = section - 1 if last else section + 1
        previous, here = here, place(helper, never)
        for head in every_head:
            token = start_section(section, head, previous, helper, token)
            if section == 0 and head == 0:
                for ahead in range(1, members):
                    wide, token = widen(here, token, output_weight, ahead, members, share)
                    far_weights.append(exchanged(around(wide, ahead)))
        stages = 2 * len(bits) + 1
        for turn in range(stages + heads - 1):
            for head in every_head:
                stage = turn - head
                if 0 <= stage < stages:
                    late = []
                    if section == 0 and head == 0 and stage == 1:
                        late = [blocks[0] for blocks in far_weights]
                    token = advance(stage, head, here, section, helper, last, token, late)

    here = place(helper, position != groups - 1)
    for head in every_head:
        pieces, weights = steps[head]
        sums, token = square_sums(here, token, pieces)
        *made, token = fast_apply(
            here, token, fast_init, head, queries, share,
            pieces, exchanged(sums), weights, kept[head],
            (),
        )
        whole_block, token = finish(here, token, swapped(made[0], share))
        near.append(whole_block)
        for ahead in range(1, members):
            distant[ahead - 1].append(around(whole_block, ahead))
    pairs = [(head, near[head], output_weight) for head in every_head]
    others = [
        (head, distant[ahead][head], far_weights[ahead])
        for head in every_head
        for ahead in range(members - 1)
    ]
    if not others:
        mixed, token = output(here, token, pairs, [], None, columns, share)
        mixed = mixed.astype(jnp.bfloat16)
    else:
        head, block, candidates = others[-1]
        mixed, ready, token = output(
            here, token, pairs, others[:-1], (head, candidates), columns, share
        )
        mixed, token = add_last(here, token, mixed, block, ready)
    return mixed.reshape(block_count, tok_rows, -1)


def solution(mesh):
    placed = (
        P("block", "tok", None),
        P(None, None, "head"),
        P(None, "head"),
        P("head", None, None, None),
        P("head", None),
    )
    return jax.shard_map(
        body, mesh=mesh, in_specs=placed, out_specs=P("block", "tok", "head"), check_vma=False
    )
```

```python
import functools

import jax
import jax.numpy as jnp
from jax import lax
from jax.experimental import pallas as pl
from jax.experimental.pallas import tpu as pltpu
from jax.sharding import PartitionSpec as P

epsilon = 1e-06
step_size = 0.03
vmem_bytes = 14 * 2**20
rows_by_rows = (((1,), (1,)), ((), ()))
over_rows = (((0,), (0,)), ((), ()))
plain = (((1,), (0,)), ((), ()))


def params(limit=vmem_bytes):
    return pltpu.CompilerParams(vmem_limit_bytes=limit)


def dot(left, right, dims=plain):
    return lax.dot_general(left, right, dims, preferred_element_type=jnp.float32)


def split(values):
    high = values.astype(jnp.bfloat16)
    return high, (values - high.astype(jnp.float32)).astype(jnp.bfloat16)


def dot3(left, right, dims=plain):
    return dot(left[0], right[0], dims) + (dot(left[0], right[1], dims) + dot(left[1], right[0], dims))


def normalize(values):
    return values / jnp.sqrt(jnp.mean(values * values, axis=-1, keepdims=True) + epsilon)


token_shape = jax.ShapeDtypeStruct((8, 128), jnp.float32)
unread = pl.BlockSpec(memory_space=pl.ANY)


def whole():
    return pl.BlockSpec(memory_space=pltpu.VMEM)


hiding = {"project": 40 * 10**9, "output": 2 * 10**9, "fast_step": 4 * 10**9}


def ordered(kernel, grid, in_specs, out_specs, out_shape, scratch, name, limit=vmem_bytes, late=0):
    def traced(place, token, *refs):
        outs = len(out_shape)
        inputs = len(in_specs)
        refs = refs[:inputs] + refs[inputs + late :]
        refs[inputs + outs][...] = jnp.zeros(token_shape.shape, jnp.float32)
        kernel(place, *refs[: inputs + outs], *refs[inputs + outs + 1 :])

    return pl.pallas_call(
        traced,
        grid_spec=pltpu.PrefetchScalarGridSpec(
            num_scalar_prefetch=1,
            grid=grid,
            in_specs=[unread] + in_specs + [unread] * late,
            out_specs=list(out_specs)
            + [pl.BlockSpec(token_shape.shape, lambda i, place: (0, 0))],
            scratch_shapes=scratch,
        ),
        out_shape=list(out_shape) + [token_shape],
        compiler_params=params(limit),
        cost_estimate=pl.CostEstimate(
            flops=hiding.get(name, 0), bytes_accessed=0, transcendentals=0
        ),
        name=name,
    )


def project_kernel(chosen, pairs, place, tokens, weight, rate, *outs):
    values = dot(tokens[...], weight[...])
    for i, (part, head) in enumerate(chosen):

        @pl.when(pl.program_id(0) == i)
        def _():
            if part == 2:
                logits = dot(tokens[...], rate[...], rows_by_rows)
                logit = logits[:, head : head + 1]
                rates = jnp.maximum(logit, 0.0) + jnp.log1p(jnp.exp(-jnp.abs(logit)))
                outs[0][...] = values * rates
            else:
                outs[0 if i < pairs else 1][...] = normalize(values)


def project(place, token, tokens, weight, rate, chosen, heads, pairs):
    rows, depth = tokens.shape
    count = len(chosen)
    width = weight.shape[2] // heads
    by_part = [part for part, _ in chosen]
    by_head = [head for _, head in chosen]

    def table(values, i):
        picked = values[0]
        for at, value in enumerate(values[1:], 1):
            picked = jnp.where(i >= at, value, picked)
        return picked

    sizes = [pairs] + ([count - pairs] if count > pairs else [])
    places = [lambda i: jnp.minimum(i, pairs - 1), lambda i: jnp.maximum(i - pairs, 0)]
    return ordered(
        functools.partial(project_kernel, chosen, pairs),
        (count,),
        [
            pl.BlockSpec((rows, depth), lambda i, place: (0, 0)),
            pl.BlockSpec(
                (None, depth, width),
                lambda i, place: (table(by_part, i), 0, table(by_head, i)),
            ),
            pl.BlockSpec(rate.shape, lambda i, place: (0, 0)),
        ],
        [
            pl.BlockSpec((None, rows, width), lambda i, place, at=at: (at(i), 0, 0))
            for at in places[: len(sizes)]
        ],
        [jax.ShapeDtypeStruct((size, rows, width), jnp.float32) for size in sizes],
        [],
        "project",
        50 * 2**20,
    )(place, token, tokens, weight, rate)


def widen_kernel(place, weight, out):
    out[...] = weight[...].astype(jnp.float32)


def widen(place, token, weight, ahead, members, share):
    rows, columns = weight.shape[0] // share, weight.shape[1] // members
    step = rows // 2

    def chosen(i, place):
        return place[0] * 2 + i, lax.rem(place[3] + ahead, members)

    return ordered(
        widen_kernel,
        (2,),
        [pl.BlockSpec((step, columns), chosen)],
        [pl.BlockSpec((step, columns), lambda i, place: (i, 0))],
        [jax.ShapeDtypeStruct((rows, columns), jnp.float32)],
        [],
        "widen",
    )(place, token, weight)


def cut(grads, outs, m, place, role):
    size = outs[0].shape[1]
    odd = lax.rem(place[4], 2)
    for out, piece in zip(
        outs,
        (2 * role + odd, 2 * role + 1 - odd, 2 * (1 - role) + odd, 2 * (1 - role) + 1 - odd),
    ):
        out[m] = grads[pl.ds(pl.multiple_of(piece * size, size), size), :]


def joined(pieces, m, place, role, full):
    size = pieces[0].shape[1]
    odd = lax.rem(place[4], 2)
    for block, piece in zip(
        pieces,
        (2 * role + odd, 2 * role + 1 - odd, 2 * (1 - role) + odd, 2 * (1 - role) + 1 - odd),
    ):
        full[pl.ds(pl.multiple_of(piece * size, size), size), :] = block[m]
    return full[...]


def stepped(place, pieces, sums, weights, start, share, full):
    results = []
    for m in range(3):
        grads = joined(pieces, m, place, place[1], full)
        square = sums[0][m, 0]
        for other in sums[1:]:
            square = square + other[m, 0]
        scale = jnp.full((1, 1), square / (grads.size * share) + epsilon, jnp.float32)
        moved = weights[m].astype(jnp.float32) + grads * (step_size / jnp.sqrt(scale))
        first = start[m].astype(jnp.float32)
        base = jnp.sqrt(jnp.mean(first * first, axis=0, keepdims=True))
        column = jnp.mean(moved * moved, axis=0, keepdims=True)
        results.append(moved * (base / jnp.sqrt(column + epsilon)))
    return results


def sums_kernel(place, *refs):
    pieces, out = refs[:-1], refs[-1]
    row = lax.broadcasted_iota(jnp.int32, out.shape, 0)
    total = jnp.zeros(out.shape, jnp.float32)
    for m in range(3):
        square = sum(jnp.sum(piece[m] * piece[m]) for piece in pieces)
        total = jnp.where(row == m, square, total)
    out[...] = total


def square_sums(place, token, pieces):
    return ordered(
        sums_kernel, (1,), [whole()] * len(pieces), [whole()], [token_shape], [], "square_sums"
    )(place, token, *pieces)


def grad_kernel(share, count, first, place, start, *refs):
    refs = list(refs)
    stepping = count > 0
    if stepping:
        pieces, refs = refs[:4], refs[4:]
        sums, refs = refs[:share], refs[share:]
        if not first:
            old, refs = refs[0], refs[1:]
    sides, refs = refs[:share], refs[share:]
    outs, refs = refs[:4], refs[4:]
    if stepping:
        new, refs = refs[0], refs[1:]
    full, key, target, hidden, upward, gateward = refs
    if stepping:
        weights = stepped(place, pieces, sums, start if first else old, start, share, full)
        for m in range(3):
            new[m] = weights[m]
    else:
        weights = [start[m].astype(jnp.float32) for m in range(3)]
    gate_weight, up_weight, down_weight = (split(block) for block in weights)
    rows = sides[0].shape[1]
    chunk = min(rows, 256)
    for at, side in enumerate(sides):
        for begin in range(0, rows, chunk):
            here = pl.ds(at * rows + begin, chunk)
            keys = split(side[0, begin : begin + chunk, :])
            targets = split(side[1, begin : begin + chunk, :])
            key[here, :], target[here, :] = keys[0], targets[0]
            gate = dot3(keys, gate_weight)
            upper = dot3(keys, up_weight)
            back = dot3(targets, down_weight)
            sigma = jax.nn.sigmoid(gate)
            active = gate * sigma
            hidden[0, here, :], hidden[1, here, :] = split(active * upper)
            upward[0, here, :], upward[1, here, :] = split(back * active)
            slope = upper * sigma * (1.0 + gate * (1.0 - sigma))
            gateward[0, here, :], gateward[1, here, :] = split(back * slope)
    for m, left, right in ((2, target, hidden), (1, key, upward), (0, key, gateward)):
        rows_first = left[...]
        full[...] = dot(rows_first, right[0], over_rows) + dot(rows_first, right[1], over_rows)
        cut(full, outs, m, place, 0)


def start_spec(start, head, share):
    _, parts, width, hidden = start.shape
    return pl.BlockSpec(
        (None, parts, width, hidden // share), lambda i, place: (head, 0, 0, place[0])
    )


def fast_grad(place, token, start, head, sides, share, count, step=None, late=()):
    rows = sum(side.shape[1] for side in sides)
    _, parts, width, hidden = start.shape
    hidden = hidden // share
    piece = jax.ShapeDtypeStruct((parts, width // 4, hidden), jnp.float32)
    out_shape = [piece] * 4
    operands = list(sides)
    if step is not None:
        pieces, sums, weights = step
        old = [] if weights is None else [weights]
        operands = list(pieces) + list(sums) + old + operands
        out_shape.append(jax.ShapeDtypeStruct((parts, width, hidden), jnp.float32))
    by_width = pltpu.VMEM((rows, width), jnp.bfloat16)
    by_hidden = pltpu.VMEM((2, rows, hidden), jnp.bfloat16)
    return ordered(
        functools.partial(grad_kernel, share, count, step is not None and step[2] is None),
        (1,),
        [start_spec(start, head, share)] + [whole() for _ in operands],
        [whole() for _ in out_shape],
        out_shape,
        [
            pltpu.VMEM((width, hidden), jnp.float32),
            by_width,
            by_width,
            by_hidden,
            by_hidden,
            by_hidden,
        ],
        "fast_grad" if step is None else "fast_step",
        late=len(late),
    )(place, token, start, *operands, *late)


def apply_kernel(share, head, place, start, *refs):
    pieces, refs = refs[:4], refs[4:]
    sums, refs = refs[:share], refs[share:]
    old, kept, refs = refs[0], refs[1], refs[2:]
    queries, out, full = refs[:share], refs[share], refs[-1]
    keep = place[2] == 1
    weights = stepped(place, pieces, sums, old, start, share, full)
    weights = [jnp.where(keep, kept[m], weights[m]) for m in range(3)]
    gate_weight, up_weight, down_weight = (split(block) for block in weights)
    rows = queries[0].shape[1]
    chunk = min(rows, 256)
    for distance, query in enumerate(queries):
        slot = lax.rem(place[0] + share - distance, share)
        for begin in range(0, rows, chunk):
            here = pl.ds(begin, chunk)
            values = split(query[head, here, :])
            gate = dot3(values, gate_weight)
            hidden = split(gate * jax.nn.sigmoid(gate) * dot3(values, up_weight))
            out[slot, here, :] = dot3(hidden, down_weight, rows_by_rows)


def fast_apply(place, token, start, head, queries, share, pieces, sums, weights, kept, late):
    operands = list(pieces) + list(sums) + [weights, kept] + list(queries)
    _, rows, width = queries[0].shape
    return ordered(
        functools.partial(apply_kernel, share, head),
        (1,),
        [start_spec(start, head, share)] + [whole() for _ in operands],
        [whole()],
        [jax.ShapeDtypeStruct((share, rows, width), jnp.float32)],
        [pltpu.VMEM(weights.shape[1:], jnp.float32)],
        "fast_apply",
        late=len(late),
    )(place, token, start, *operands, *late)


def finish_kernel(place, *refs):
    parts, out = refs
    total = parts[0]
    for i in range(1, parts.shape[0]):
        total = total + parts[i]
    out[...] = normalize(total)


def finish(place, token, parts):
    return ordered(
        finish_kernel,
        (1,),
        [whole()],
        [whole()],
        [jax.ShapeDtypeStruct(parts.shape[1:], jnp.float32)],
        [],
        "finish",
    )(place, token, parts)


def halve(total, bit, place, outs):
    if bit is None:
        outs[0][...] = total
        return
    size = outs[0].shape[1]
    mine = lax.rem(lax.div(place[4], bit), 2) == 1
    low, high = total[:, :size], total[:, size:]
    outs[0][...] = jnp.where(mine, low, high)
    outs[1][...] = jnp.where(mine, high, low)


def gather_kernel(bit, place, own, line, across, corner, *outs):
    helping = place[1] == 1
    total = jnp.where(helping, across[...], own[...]) + jnp.where(helping, corner[...], line[...])
    halve(total, bit, place, outs)


def add_kernel(bit, place, own, other, *outs):
    halve(own[...] + other[...], bit, place, outs)


def pair_kernel(bit, place, own, other, out):
    size = own.shape[1]
    mine = lax.rem(lax.div(place[4], bit), 2) == 1
    out[:, :size] = jnp.where(mine, other[...], own[...])
    out[:, size:] = jnp.where(mine, own[...], other[...])


def combine(place, token, kernel, operands, bit, late=()):
    parts, size, width = operands[0].shape
    count = 1
    if kernel is pair_kernel:
        size = 2 * size
    elif bit is not None:
        count, size = 2, size // 2
    return ordered(
        functools.partial(kernel, bit),
        (1,),
        [whole() for _ in operands],
        [whole()] * count,
        [jax.ShapeDtypeStruct((parts, size, width), jnp.float32)] * count,
        [],
        "combine",
        late=len(late),
    )(place, token, *operands, *late)


def output_kernel(heads, prepared, share, place, *refs):
    refs = list(refs)
    out = refs.pop(-2 if prepared is not None else -1)
    total = None

    def chosen(head):
        weight = refs.pop(0)[...]
        for distance in range(1, share):
            other = refs.pop(0)[...]
            weight = jnp.where(lax.rem(place[0] + share - distance, share) == head, other, weight)
        return weight.astype(jnp.bfloat16)

    for head, far in heads:
        block = refs.pop(0)[...].astype(jnp.bfloat16)
        part = dot(block, chosen(head) if far else refs.pop(0)[...])
        total = part if total is None else total + part
    out[...] = total
    if prepared is not None:
        refs[-1][...] = chosen(prepared)


def output(place, token, near, distant, prepared, columns, share):
    rows, width = near[0][1].shape
    half = columns // 2
    by_half = pl.BlockSpec((rows, half), lambda i, place: (0, i))
    by_rows = pl.BlockSpec((rows, width), lambda i, place: (0, 0))
    weight_half = pl.BlockSpec((width, half), lambda i, place: (0, i))
    operands, in_specs = [], []
    for head, block, weight in near:
        operands += [block, weight]
        spec = pl.BlockSpec((width, half), lambda i, place, head=head: (head, 2 * place[3] + i))
        in_specs += [by_rows, spec]
    for head, block, weights in distant:
        operands += [block] + list(weights)
        in_specs += [by_rows] + [weight_half for _ in weights]
    out_specs, out_shape = [by_half], [jax.ShapeDtypeStruct((rows, columns), jnp.float32)]
    ready = None
    if prepared is not None:
        ready, weights = prepared
        operands += list(weights)
        in_specs += [weight_half for _ in weights]
        out_specs.append(weight_half)
        out_shape.append(jax.ShapeDtypeStruct((width, columns), jnp.bfloat16))
    heads = [(head, False) for head, _, _ in near] + [(head, True) for head, _, _ in distant]
    return ordered(
        functools.partial(output_kernel, heads, ready, share),
        (2,),
        in_specs,
        out_specs,
        out_shape,
        [],
        "output",
    )(place, token, *operands)


def last_kernel(place, sofar, block, weight, out):
    total = sofar[...] + dot(block[...].astype(jnp.bfloat16), weight[...])
    out[...] = total.astype(out.dtype)


def add_last(place, token, sofar, block, weight):
    return ordered(
        last_kernel,
        (1,),
        [whole()] * 3,
        [whole()],
        [jax.ShapeDtypeStruct(sofar.shape, jnp.bfloat16)],
        [],
        "add_last",
    )(place, token, sofar, block, weight)


def within_chip(block, share, distance):
    devices = range(lax.axis_size("tok"))
    route = [(t, t // share * share + (t + distance) % share) for t in devices]
    return lax.ppermute(block, "tok", route)


def swapped(blocks, share):
    size = lax.axis_size("tok")
    chips = [[first + core for core in range(share)] for first in range(0, size, share)]
    return lax.all_to_all(blocks, "tok", 0, 0, axis_index_groups=chips, tiled=True)


def flipped(block, share, bit):
    route = [(t, t ^ (bit * share)) for t in range(lax.axis_size("tok"))]
    return lax.ppermute(block, "tok", route)


def crossed(block, share, bit, one, two, both):
    size = lax.axis_size("tok")
    route = [(one * size + t, two * size + (t ^ (bit * share))) for t in range(size)]
    if one != two:
        back = bit * share if both else 0
        route += [(two * size + t, one * size + (t ^ back)) for t in range(size)]
    covered = {source for source, _ in route}
    every = range(size * lax.axis_size("block"))
    route += [(device, device) for device in every if device not in covered]
    return lax.ppermute(block, ("block", "tok"), route)


def body(tokens, input_weight, rate_weight, fast_init, output_weight):
    block_count, tok_rows, model_width = tokens.shape
    heads, _, head_dim, _ = fast_init.shape
    share = heads
    members = lax.axis_size("head")
    groups = lax.axis_size("block")
    position = lax.axis_index("block")
    member = lax.axis_index("head")
    core = lax.axis_index("tok") % share
    chip = lax.axis_index("tok") // share
    length = lax.axis_size("tok") // share
    bits = [1 << b for b in range(1, length.bit_length() - 1)]
    flattened = tokens.reshape(tok_rows, model_width)
    weight = jnp.transpose(input_weight, (1, 0, 2))
    rate = jnp.transpose(rate_weight)
    columns = output_weight.shape[1] // members
    every_head = range(heads)

    def exchanged(block):
        return [block] + [within_chip(block, share, distance) for distance in range(1, share)]

    def around(block, ahead):
        return lax.ppermute(block, "head", [(i, (i + ahead) % members) for i in range(members)])

    def place(helper, keep):
        return jnp.stack([core, position == helper, keep, member, chip]).astype(jnp.int32)

    token = jnp.zeros(token_shape.shape, jnp.float32)
    never = position < 0
    here = place(1, never)
    sides = []
    for head in every_head:
        chosen_parts = [(1, head), (2, head)]
        if head + 1 == heads:
            chosen_parts += [(0, other) for other in every_head]
        *made, token = project(here, token, flattened, weight, rate, chosen_parts, heads, 2)
        sides.append(exchanged(made[0]))
    queries = exchanged(made[1])

    kept = [None] * heads
    steps = [None] * heads
    far_weights = []
    parts = [None] * heads

    def start_section(section, head, here, helper, token):
        if section == 0:
            late = queries if head + 1 == heads else ()
            *pieces, token = fast_grad(
                here, token, fast_init, head, sides[head], share, 0, None, late
            )
            weights = None
        else:
            pieces, weights = steps[head]
            sums, token = square_sums(here, token, pieces)
            *pieces, weights, token = fast_grad(
                here, token, fast_init, head, sides[head], share, section,
                (pieces, exchanged(sums), weights),
            )
            kept[head] = (
                weights
                if section == 1
                else jnp.where(position == section - 1, weights, kept[head])
            )
        own, line, across, corner = pieces
        steps[head] = None, weights
        parts[head] = (
            own,
            crossed(line, share, 1, section, section, False),
            crossed(across, share, 0, section, helper, False),
            crossed(corner, share, 1, section, helper, False),
        )
        return token

    def advance(stage, head, here, section, helper, last, token, late):
        count = len(bits)
        if stage <= count:
            bit = bits[stage] if stage < count else None
            kernel = add_kernel if stage else gather_kernel
            *outs, token = combine(here, token, kernel, parts[head], bit, late)
            total = outs[-1]
            if bit is not None:
                parts[head] = total, flipped(outs[0], share, bit)
                return token
        else:
            bit = bits[2 * count - stage]
            total, token = combine(here, token, pair_kernel, parts[head], bit, late)
        if stage < 2 * count:
            parts[head] = total, flipped(total, share, bits[2 * count - stage - 1])
        else:
            pieces = (
                total,
                crossed(total, share, 1, section, section, False)
                if last
                else flipped(total, share, 1),
                crossed(total, share, 0, helper, section, not last),
                crossed(total, share, 1, helper, section, not last),
            )
            steps[head] = pieces, steps[head][1]
        return token

    near, distant = [], [[] for _ in range(1, members)]
    for section in range(groups):
        last = section + 1 == groups
        helper = section - 1 if last else section + 1
        previous, here = here, place(helper, never)
        for head in every_head:
            token = start_section(section, head, previous, helper, token)
            if section == 0 and head == 0:
                for ahead in range(1, members):
                    wide, token = widen(here, token, output_weight, ahead, members, share)
                    far_weights.append(exchanged(around(wide, ahead)))
        stages = 2 * len(bits) + 1
        for turn in range(stages + heads - 1):
            for head in every_head:
                stage = turn - head
                if 0 <= stage < stages:
                    late = []
                    if section == 0 and head == heads - 1 and stage == 1:
                        late = [blocks[0] for blocks in far_weights]
                    token = advance(stage, head, here, section, helper, last, token, late)

    here = place(helper, position != groups - 1)
    for head in every_head:
        pieces, weights = steps[head]
        sums, token = square_sums(here, token, pieces)
        *made, token = fast_apply(
            here, token, fast_init, head, queries, share,
            pieces, exchanged(sums), weights, kept[head],
            (),
        )
        whole_block, token = finish(here, token, swapped(made[0], share))
        near.append(whole_block)
        for ahead in range(1, members):
            distant[ahead - 1].append(around(whole_block, ahead))
    pairs = [(head, near[head], output_weight) for head in every_head]
    others = [
        (head, distant[ahead][head], far_weights[ahead])
        for head in every_head
        for ahead in range(members - 1)
    ]
    if not others:
        mixed, token = output(here, token, pairs, [], None, columns, share)
        mixed = mixed.astype(jnp.bfloat16)
    else:
        head, block, candidates = others[-1]
        mixed, ready, token = output(
            here, token, pairs, others[:-1], (head, candidates), columns, share
        )
        mixed, token = add_last(here, token, mixed, block, ready)
    return mixed.reshape(block_count, tok_rows, -1)


def solution(mesh):
    placed = (
        P("block", "tok", None),
        P(None, None, "head"),
        P(None, "head"),
        P("head", None, None, None),
        P("head", None),
    )
    return jax.shard_map(
        body, mesh=mesh, in_specs=placed, out_specs=P("block", "tok", "head"), check_vma=False
    )
```

```python
import functools

import jax
import jax.numpy as jnp
from jax import lax
from jax.experimental import pallas as pl
from jax.experimental.pallas import tpu as pltpu
from jax.sharding import PartitionSpec as P

epsilon = 1e-06
step_size = 0.03
vmem_bytes = 14 * 2**20
rows_by_rows = (((1,), (1,)), ((), ()))
over_rows = (((0,), (0,)), ((), ()))
plain = (((1,), (0,)), ((), ()))


def params(limit=vmem_bytes):
    return pltpu.CompilerParams(vmem_limit_bytes=limit)


def dot(left, right, dims=plain):
    return lax.dot_general(left, right, dims, preferred_element_type=jnp.float32)


def split(values):
    high = values.astype(jnp.bfloat16)
    return high, (values - high.astype(jnp.float32)).astype(jnp.bfloat16)


def dot3(left, right, dims=plain):
    return dot(left[0], right[0], dims) + (dot(left[0], right[1], dims) + dot(left[1], right[0], dims))


def normalize(values):
    return values / jnp.sqrt(jnp.mean(values * values, axis=-1, keepdims=True) + epsilon)


token_shape = jax.ShapeDtypeStruct((8, 128), jnp.float32)
unread = pl.BlockSpec(memory_space=pl.ANY)


def whole():
    return pl.BlockSpec(memory_space=pltpu.VMEM)


hiding = {"project": 40 * 10**9, "output": 2 * 10**9, "fast_step": 4 * 10**9, "widen": 12 * 10**9, "combine_first": 6 * 10**9}


def ordered(kernel, grid, in_specs, out_specs, out_shape, scratch, name, limit=vmem_bytes, late=0):
    def traced(place, token, *refs):
        outs = len(out_shape)
        inputs = len(in_specs)
        refs = refs[:inputs] + refs[inputs + late :]
        refs[inputs + outs][...] = jnp.zeros(token_shape.shape, jnp.float32)
        kernel(place, *refs[: inputs + outs], *refs[inputs + outs + 1 :])

    return pl.pallas_call(
        traced,
        grid_spec=pltpu.PrefetchScalarGridSpec(
            num_scalar_prefetch=1,
            grid=grid,
            in_specs=[unread] + in_specs + [unread] * late,
            out_specs=list(out_specs)
            + [pl.BlockSpec(token_shape.shape, lambda i, place: (0, 0))],
            scratch_shapes=scratch,
        ),
        out_shape=list(out_shape) + [token_shape],
        compiler_params=params(limit),
        cost_estimate=pl.CostEstimate(
            flops=hiding.get(name, 0), bytes_accessed=0, transcendentals=0
        ),
        name=name,
    )


def project_kernel(chosen, pairs, place, tokens, weight, rate, *outs):
    values = dot(tokens[...], weight[...])
    for i, (part, head) in enumerate(chosen):

        @pl.when(pl.program_id(0) == i)
        def _():
            if part == 2:
                logits = dot(tokens[...], rate[...], rows_by_rows)
                logit = logits[:, head : head + 1]
                rates = jnp.maximum(logit, 0.0) + jnp.log1p(jnp.exp(-jnp.abs(logit)))
                outs[0][...] = values * rates
            else:
                outs[0 if i < pairs else 1][...] = normalize(values)


def project(place, token, tokens, weight, rate, chosen, heads, pairs):
    rows, depth = tokens.shape
    count = len(chosen)
    width = weight.shape[2] // heads
    by_part = [part for part, _ in chosen]
    by_head = [head for _, head in chosen]

    def table(values, i):
        picked = values[0]
        for at, value in enumerate(values[1:], 1):
            picked = jnp.where(i >= at, value, picked)
        return picked

    sizes = [pairs] + ([count - pairs] if count > pairs else [])
    places = [lambda i: jnp.minimum(i, pairs - 1), lambda i: jnp.maximum(i - pairs, 0)]
    return ordered(
        functools.partial(project_kernel, chosen, pairs),
        (count,),
        [
            pl.BlockSpec((rows, depth), lambda i, place: (0, 0)),
            pl.BlockSpec(
                (None, depth, width),
                lambda i, place: (table(by_part, i), 0, table(by_head, i)),
            ),
            pl.BlockSpec(rate.shape, lambda i, place: (0, 0)),
        ],
        [
            pl.BlockSpec((None, rows, width), lambda i, place, at=at: (at(i), 0, 0))
            for at in places[: len(sizes)]
        ],
        [jax.ShapeDtypeStruct((size, rows, width), jnp.float32) for size in sizes],
        [],
        "project",
        50 * 2**20,
    )(place, token, tokens, weight, rate)


def widen_kernel(place, weight, out):
    out[...] = weight[...].astype(jnp.float32)


def widen(place, token, weight, ahead, members, share):
    rows, columns = weight.shape[0] // share, weight.shape[1] // members
    step = rows // 2

    def chosen(i, place):
        return place[0] * 2 + i, lax.rem(place[3] + ahead, members)

    return ordered(
        widen_kernel,
        (2,),
        [pl.BlockSpec((step, columns), chosen)],
        [pl.BlockSpec((step, columns), lambda i, place: (i, 0))],
        [jax.ShapeDtypeStruct((rows, columns), jnp.float32)],
        [],
        "widen",
    )(place, token, weight)


def cut(grads, outs, m, place, role):
    size = outs[0].shape[1]
    odd = lax.rem(place[4], 2)
    for out, piece in zip(
        outs,
        (2 * role + odd, 2 * role + 1 - odd, 2 * (1 - role) + odd, 2 * (1 - role) + 1 - odd),
    ):
        out[m] = grads[pl.ds(pl.multiple_of(piece * size, size), size), :]


def joined(pieces, m, place, role, full):
    size = pieces[0].shape[1]
    odd = lax.rem(place[4], 2)
    for block, piece in zip(
        pieces,
        (2 * role + odd, 2 * role + 1 - odd, 2 * (1 - role) + odd, 2 * (1 - role) + 1 - odd),
    ):
        full[pl.ds(pl.multiple_of(piece * size, size), size), :] = block[m]
    return full[...]


def stepped(place, pieces, sums, weights, start, share, full):
    results = []
    for m in range(3):
        grads = joined(pieces, m, place, place[1], full)
        square = sums[0][m, 0]
        for other in sums[1:]:
            square = square + other[m, 0]
        scale = jnp.full((1, 1), square / (grads.size * share) + epsilon, jnp.float32)
        moved = weights[m].astype(jnp.float32) + grads * (step_size / jnp.sqrt(scale))
        first = start[m].astype(jnp.float32)
        base = jnp.sqrt(jnp.mean(first * first, axis=0, keepdims=True))
        column = jnp.mean(moved * moved, axis=0, keepdims=True)
        results.append(moved * (base / jnp.sqrt(column + epsilon)))
    return results


def sums_kernel(place, *refs):
    pieces, out = refs[:-1], refs[-1]
    row = lax.broadcasted_iota(jnp.int32, out.shape, 0)
    total = jnp.zeros(out.shape, jnp.float32)
    for m in range(3):
        square = sum(jnp.sum(piece[m] * piece[m]) for piece in pieces)
        total = jnp.where(row == m, square, total)
    out[...] = total


def square_sums(place, token, pieces):
    return ordered(
        sums_kernel, (1,), [whole()] * len(pieces), [whole()], [token_shape], [], "square_sums"
    )(place, token, *pieces)


def grad_kernel(share, count, first, place, start, *refs):
    refs = list(refs)
    stepping = count > 0
    if stepping:
        pieces, refs = refs[:4], refs[4:]
        sums, refs = refs[:share], refs[share:]
        if not first:
            old, refs = refs[0], refs[1:]
    sides, refs = refs[:share], refs[share:]
    outs, refs = refs[:4], refs[4:]
    if stepping:
        new, refs = refs[0], refs[1:]
    full, key, target, hidden, upward, gateward = refs
    if stepping:
        weights = stepped(place, pieces, sums, start if first else old, start, share, full)
        for m in range(3):
            new[m] = weights[m]
    else:
        weights = [start[m].astype(jnp.float32) for m in range(3)]
    gate_weight, up_weight, down_weight = (split(block) for block in weights)
    rows = sides[0].shape[1]
    chunk = min(rows, 256)
    for at, side in enumerate(sides):
        for begin in range(0, rows, chunk):
            here = pl.ds(at * rows + begin, chunk)
            keys = split(side[0, begin : begin + chunk, :])
            targets = split(side[1, begin : begin + chunk, :])
            key[here, :], target[here, :] = keys[0], targets[0]
            gate = dot3(keys, gate_weight)
            upper = dot3(keys, up_weight)
            back = dot3(targets, down_weight)
            sigma = jax.nn.sigmoid(gate)
            active = gate * sigma
            hidden[0, here, :], hidden[1, here, :] = split(active * upper)
            upward[0, here, :], upward[1, here, :] = split(back * active)
            slope = upper * sigma * (1.0 + gate * (1.0 - sigma))
            gateward[0, here, :], gateward[1, here, :] = split(back * slope)
    for m, left, right in ((2, target, hidden), (1, key, upward), (0, key, gateward)):
        rows_first = left[...]
        full[...] = dot(rows_first, right[0], over_rows) + dot(rows_first, right[1], over_rows)
        cut(full, outs, m, place, 0)


def start_spec(start, head, share):
    _, parts, width, hidden = start.shape
    return pl.BlockSpec(
        (None, parts, width, hidden // share), lambda i, place: (head, 0, 0, place[0])
    )


def fast_grad(place, token, start, head, sides, share, count, step=None, late=()):
    rows = sum(side.shape[1] for side in sides)
    _, parts, width, hidden = start.shape
    hidden = hidden // share
    piece = jax.ShapeDtypeStruct((parts, width // 4, hidden), jnp.float32)
    out_shape = [piece] * 4
    operands = list(sides)
    if step is not None:
        pieces, sums, weights = step
        old = [] if weights is None else [weights]
        operands = list(pieces) + list(sums) + old + operands
        out_shape.append(jax.ShapeDtypeStruct((parts, width, hidden), jnp.float32))
    by_width = pltpu.VMEM((rows, width), jnp.bfloat16)
    by_hidden = pltpu.VMEM((2, rows, hidden), jnp.bfloat16)
    return ordered(
        functools.partial(grad_kernel, share, count, step is not None and step[2] is None),
        (1,),
        [start_spec(start, head, share)] + [whole() for _ in operands],
        [whole() for _ in out_shape],
        out_shape,
        [
            pltpu.VMEM((width, hidden), jnp.float32),
            by_width,
            by_width,
            by_hidden,
            by_hidden,
            by_hidden,
        ],
        "fast_grad" if step is None else "fast_step",
        late=len(late),
    )(place, token, start, *operands, *late)


def apply_kernel(share, head, place, start, *refs):
    pieces, refs = refs[:4], refs[4:]
    sums, refs = refs[:share], refs[share:]
    old, kept, refs = refs[0], refs[1], refs[2:]
    queries, out, full = refs[:share], refs[share], refs[-1]
    keep = place[2] == 1
    weights = stepped(place, pieces, sums, old, start, share, full)
    weights = [jnp.where(keep, kept[m], weights[m]) for m in range(3)]
    gate_weight, up_weight, down_weight = (split(block) for block in weights)
    rows = queries[0].shape[1]
    chunk = min(rows, 256)
    for distance, query in enumerate(queries):
        slot = lax.rem(place[0] + share - distance, share)
        for begin in range(0, rows, chunk):
            here = pl.ds(begin, chunk)
            values = split(query[head, here, :])
            gate = dot3(values, gate_weight)
            hidden = split(gate * jax.nn.sigmoid(gate) * dot3(values, up_weight))
            out[slot, here, :] = dot3(hidden, down_weight, rows_by_rows)


def fast_apply(place, token, start, head, queries, share, pieces, sums, weights, kept, late):
    operands = list(pieces) + list(sums) + [weights, kept] + list(queries)
    _, rows, width = queries[0].shape
    return ordered(
        functools.partial(apply_kernel, share, head),
        (1,),
        [start_spec(start, head, share)] + [whole() for _ in operands],
        [whole()],
        [jax.ShapeDtypeStruct((share, rows, width), jnp.float32)],
        [pltpu.VMEM(weights.shape[1:], jnp.float32)],
        "fast_apply",
        late=len(late),
    )(place, token, start, *operands, *late)


def finish_kernel(place, *refs):
    parts, out = refs
    total = parts[0]
    for i in range(1, parts.shape[0]):
        total = total + parts[i]
    out[...] = normalize(total)


def finish(place, token, parts):
    return ordered(
        finish_kernel,
        (1,),
        [whole()],
        [whole()],
        [jax.ShapeDtypeStruct(parts.shape[1:], jnp.float32)],
        [],
        "finish",
    )(place, token, parts)


def halve(total, bit, place, outs):
    if bit is None:
        outs[0][...] = total
        return
    size = outs[0].shape[1]
    mine = lax.rem(lax.div(place[4], bit), 2) == 1
    low, high = total[:, :size], total[:, size:]
    outs[0][...] = jnp.where(mine, low, high)
    outs[1][...] = jnp.where(mine, high, low)


def gather_kernel(bit, place, own, line, across, corner, *outs):
    helping = place[1] == 1
    total = jnp.where(helping, across[...], own[...]) + jnp.where(helping, corner[...], line[...])
    halve(total, bit, place, outs)


def add_kernel(bit, place, own, other, *outs):
    halve(own[...] + other[...], bit, place, outs)


def pair_kernel(bit, place, own, other, out):
    size = own.shape[1]
    mine = lax.rem(lax.div(place[4], bit), 2) == 1
    out[:, :size] = jnp.where(mine, other[...], own[...])
    out[:, size:] = jnp.where(mine, own[...], other[...])


def combine(place, token, kernel, operands, bit, late=(), name="combine"):
    parts, size, width = operands[0].shape
    count = 1
    if kernel is pair_kernel:
        size = 2 * size
    elif bit is not None:
        count, size = 2, size // 2
    return ordered(
        functools.partial(kernel, bit),
        (1,),
        [whole() for _ in operands],
        [whole()] * count,
        [jax.ShapeDtypeStruct((parts, size, width), jnp.float32)] * count,
        [],
        name,
        late=len(late),
    )(place, token, *operands, *late)


def output_kernel(heads, prepared, share, place, *refs):
    refs = list(refs)
    out = refs.pop(-2 if prepared is not None else -1)
    total = None

    def chosen(head):
        weight = refs.pop(0)[...]
        for distance in range(1, share):
            other = refs.pop(0)[...]
            weight = jnp.where(lax.rem(place[0] + share - distance, share) == head, other, weight)
        return weight.astype(jnp.bfloat16)

    for head, far in heads:
        block = refs.pop(0)[...].astype(jnp.bfloat16)
        part = dot(block, chosen(head) if far else refs.pop(0)[...])
        total = part if total is None else total + part
    out[...] = total
    if prepared is not None:
        refs[-1][...] = chosen(prepared)


def output(place, token, near, distant, prepared, columns, share):
    rows, width = near[0][1].shape
    half = columns // 2
    by_half = pl.BlockSpec((rows, half), lambda i, place: (0, i))
    by_rows = pl.BlockSpec((rows, width), lambda i, place: (0, 0))
    weight_half = pl.BlockSpec((width, half), lambda i, place: (0, i))
    operands, in_specs = [], []
    for head, block, weight in near:
        operands += [block, weight]
        spec = pl.BlockSpec((width, half), lambda i, place, head=head: (head, 2 * place[3] + i))
        in_specs += [by_rows, spec]
    for head, block, weights in distant:
        operands += [block] + list(weights)
        in_specs += [by_rows] + [weight_half for _ in weights]
    out_specs, out_shape = [by_half], [jax.ShapeDtypeStruct((rows, columns), jnp.float32)]
    ready = None
    if prepared is not None:
        ready, weights = prepared
        operands += list(weights)
        in_specs += [weight_half for _ in weights]
        out_specs.append(weight_half)
        out_shape.append(jax.ShapeDtypeStruct((width, columns), jnp.bfloat16))
    heads = [(head, False) for head, _, _ in near] + [(head, True) for head, _, _ in distant]
    return ordered(
        functools.partial(output_kernel, heads, ready, share),
        (2,),
        in_specs,
        out_specs,
        out_shape,
        [],
        "output",
    )(place, token, *operands)


def last_kernel(place, sofar, block, weight, out):
    total = sofar[...] + dot(block[...].astype(jnp.bfloat16), weight[...])
    out[...] = total.astype(out.dtype)


def add_last(place, token, sofar, block, weight):
    return ordered(
        last_kernel,
        (1,),
        [whole()] * 3,
        [whole()],
        [jax.ShapeDtypeStruct(sofar.shape, jnp.bfloat16)],
        [],
        "add_last",
    )(place, token, sofar, block, weight)


def within_chip(block, share, distance):
    devices = range(lax.axis_size("tok"))
    route = [(t, t // share * share + (t + distance) % share) for t in devices]
    return lax.ppermute(block, "tok", route)


def swapped(blocks, share):
    size = lax.axis_size("tok")
    chips = [[first + core for core in range(share)] for first in range(0, size, share)]
    return lax.all_to_all(blocks, "tok", 0, 0, axis_index_groups=chips, tiled=True)


def flipped(block, share, bit):
    route = [(t, t ^ (bit * share)) for t in range(lax.axis_size("tok"))]
    return lax.ppermute(block, "tok", route)


def crossed(block, share, bit, one, two, both):
    size = lax.axis_size("tok")
    route = [(one * size + t, two * size + (t ^ (bit * share))) for t in range(size)]
    if one != two:
        back = bit * share if both else 0
        route += [(two * size + t, one * size + (t ^ back)) for t in range(size)]
    covered = {source for source, _ in route}
    every = range(size * lax.axis_size("block"))
    route += [(device, device) for device in every if device not in covered]
    return lax.ppermute(block, ("block", "tok"), route)


def body(tokens, input_weight, rate_weight, fast_init, output_weight):
    block_count, tok_rows, model_width = tokens.shape
    heads, _, head_dim, _ = fast_init.shape
    share = heads
    members = lax.axis_size("head")
    groups = lax.axis_size("block")
    position = lax.axis_index("block")
    member = lax.axis_index("head")
    core = lax.axis_index("tok") % share
    chip = lax.axis_index("tok") // share
    length = lax.axis_size("tok") // share
    bits = [1 << b for b in range(1, length.bit_length() - 1)]
    flattened = tokens.reshape(tok_rows, model_width)
    weight = jnp.transpose(input_weight, (1, 0, 2))
    rate = jnp.transpose(rate_weight)
    columns = output_weight.shape[1] // members
    every_head = range(heads)

    def exchanged(block):
        return [block] + [within_chip(block, share, distance) for distance in range(1, share)]

    def around(block, ahead):
        return lax.ppermute(block, "head", [(i, (i + ahead) % members) for i in range(members)])

    def place(helper, keep):
        return jnp.stack([core, position == helper, keep, member, chip]).astype(jnp.int32)

    token = jnp.zeros(token_shape.shape, jnp.float32)
    never = position < 0
    here = place(1, never)
    sides, queries = [None] * heads, []

    def project_head(head, token):
        chosen_parts = [(1, head), (2, head)]
        if head + 1 == heads:
            chosen_parts += [(0, other) for other in every_head]
        *made, token = project(here, token, flattened, weight, rate, chosen_parts, heads, 2)
        sides[head] = exchanged(made[0])
        if head + 1 == heads:
            queries.extend(exchanged(made[1]))
        return token

    kept = [None] * heads
    steps = [None] * heads
    far_weights = []
    parts = [None] * heads

    def start_section(section, head, here, helper, token):
        if section == 0:
            late = queries if head + 1 == heads else ()
            *pieces, token = fast_grad(
                here, token, fast_init, head, sides[head], share, 0, None, late
            )
            weights = None
        else:
            pieces, weights = steps[head]
            sums, token = square_sums(here, token, pieces)
            *pieces, weights, token = fast_grad(
                here, token, fast_init, head, sides[head], share, section,
                (pieces, exchanged(sums), weights),
            )
            kept[head] = (
                weights
                if section == 1
                else jnp.where(position == section - 1, weights, kept[head])
            )
        own, line, across, corner = pieces
        steps[head] = None, weights
        parts[head] = (
            own,
            crossed(line, share, 1, section, section, False),
            crossed(across, share, 0, section, helper, False),
            crossed(corner, share, 1, section, helper, False),
        )
        return token

    def advance(stage, head, here, section, helper, last, token, late):
        count = len(bits)
        if stage <= count:
            bit = bits[stage] if stage < count else None
            kernel = add_kernel if stage else gather_kernel
            name = "combine_first" if section == 0 and head == 0 and stage == 1 else "combine"
            *outs, token = combine(here, token, kernel, parts[head], bit, late, name)
            total = outs[-1]
            if bit is not None:
                parts[head] = total, flipped(outs[0], share, bit)
                return token
        else:
            bit = bits[2 * count - stage]
            total, token = combine(here, token, pair_kernel, parts[head], bit, late)
        if stage < 2 * count:
            parts[head] = total, flipped(total, share, bits[2 * count - stage - 1])
        else:
            pieces = (
                total,
                crossed(total, share, 1, section, section, False)
                if last
                else flipped(total, share, 1),
                crossed(total, share, 0, helper, section, not last),
                crossed(total, share, 1, helper, section, not last),
            )
            steps[head] = pieces, steps[head][1]
        return token

    near, distant = [], [[] for _ in range(1, members)]
    for section in range(groups):
        last = section + 1 == groups
        helper = section - 1 if last else section + 1
        previous, here = here, place(helper, never)
        for head in every_head:
            if section == 0 and head == 0:
                token = project_head(head, token)
            token = start_section(section, head, previous, helper, token)
            if section == 0 and head == 0:
                for other in every_head[1:]:
                    token = project_head(other, token)
                token = advance(0, head, here, section, helper, last, token, [])
                for ahead in range(1, members):
                    wide, token = widen(here, token, output_weight, ahead, members, share)
                    far_weights.append(exchanged(around(wide, ahead)))
        stages = 2 * len(bits) + 1
        for turn in range(stages + heads - 1):
            for head in every_head:
                stage = turn - head
                if 0 <= stage < stages and (section or head or stage):
                    late = []
                    if section == 0 and head == heads - 1 and stage == 2:
                        late = [blocks[0] for blocks in far_weights]
                    token = advance(stage, head, here, section, helper, last, token, late)

    here = place(helper, position != groups - 1)
    for head in every_head:
        pieces, weights = steps[head]
        sums, token = square_sums(here, token, pieces)
        *made, token = fast_apply(
            here, token, fast_init, head, queries, share,
            pieces, exchanged(sums), weights, kept[head],
            (),
        )
        whole_block, token = finish(here, token, swapped(made[0], share))
        near.append(whole_block)
        for ahead in range(1, members):
            distant[ahead - 1].append(around(whole_block, ahead))
    pairs = [(head, near[head], output_weight) for head in every_head]
    others = [
        (head, distant[ahead][head], far_weights[ahead])
        for head in every_head
        for ahead in range(members - 1)
    ]
    if not others:
        mixed, token = output(here, token, pairs, [], None, columns, share)
        mixed = mixed.astype(jnp.bfloat16)
    else:
        head, block, candidates = others[-1]
        mixed, ready, token = output(
            here, token, pairs, others[:-1], (head, candidates), columns, share
        )
        mixed, token = add_last(here, token, mixed, block, ready)
    return mixed.reshape(block_count, tok_rows, -1)


def solution(mesh):
    placed = (
        P("block", "tok", None),
        P(None, None, "head"),
        P(None, "head"),
        P("head", None, None, None),
        P("head", None),
    )
    return jax.shard_map(
        body, mesh=mesh, in_specs=placed, out_specs=P("block", "tok", "head"), check_vma=False
    )
```
